256 devices in a mesh: dp: 2 (over x_hi), expert: 8 (over y, core), tensor: 16 (over z, x_lo).
Axes of the slice: x: 4 (x_hi: 2, x_lo: 2; x = x_hi * 2 + x_lo), y: 4, z: 8, core: 2. Of those that a mesh axis runs over, the one named last changes fastest.
Arguments:
- tokens: bfloat16 [4, 2048, 3072], P(None, ('dp', 'expert'), 'tensor'), parts along dimension 1, may hold values from -6 to 6
- expert_ids: int32 [4, 2048, 2], P(None, ('dp', 'expert')), parts along dimension 1, may hold values from 0 to 3, all different within a row; in each aligned block of 128 rows (0 to 127, 128 to 255, ..., all dimensions but the last counted through in order) at most 80 rows name the same one
- route_weights: float32 [4, 2048, 2], P(None, ('dp', 'expert')), parts along dimension 1, may hold values from 0.2 to 1
- gate_train: bfloat16 [8, 3072, 4096], P('expert', 'tensor'), may hold values from -0.109375 to 0.109375
- up_train: bfloat16 [8, 3072, 4096], P('expert', 'tensor'), may hold values from -0.109375 to 0.109375
Outputs:
- hidden: bfloat16 [4, 2048, 2, 2, 4096], P(None, ('dp', 'expert'), None, None, 'tensor'), parts along dimension 1
The draws below stay inside these ranges and needn't reach their ends.
There are 2 independent parts, one for each index of `dp`. The reference program is written for one: setup_inputs(seed, part) draws one part's arguments, and reference() takes and returns one part's arrays. A program takes and returns all parts, laid end to end along the dimension named above; an argument that names none is the same for every part. Nothing has to cross between parts.
Inputs may be any that keep to these rules, and one draw needn't show every extreme that they name: `expert_ids`: each token names 2 different experts; within one step, in each aligned block of 128 tokens (the tokens of one index of expert) no expert is named by more than 80 tokens, a bound that some block reaches.
All inputs are finite; a program needn't handle non-finite values.
Results may differ from the reference program's by a relative error of at most 0.001.
Values may be sent and summed in bfloat16 or wider, within the bound.
No kernel may reach another device: no remote copies, remote signals or barrier semaphores. Data moves between devices by JAX's collectives and lax.ppermute only.
A program may use at most 128 MiB of HBM per device.

```python
import math
import jax
import jax.numpy as jnp
import numpy as np
from jax import lax

D = 3072
FF = 8192
E = 4
TOP = 2
STEPS = 4
TOK_DEV = 128
TOKENS = 1024
OWNERS = 8
MOST = 80


def block_levels(rng, dims, cuts, low, largest):
    factor_of, own = 1.0, jax.random.fold_in(rng, 6)
    for dim, blocks in cuts:
        steps = jnp.exp(jax.random.uniform(jax.random.fold_in(own, dim), (blocks,), jnp.float32, low / len(cuts), largest / len(cuts)))
        factor_of = factor_of * jnp.repeat(steps, dims[dim] // blocks).reshape([-1 if axis == dim else 1 for axis in range(len(dims))])
    return factor_of


def shared_out(rng, own, number, rows, number_of, top, reach, slope):
    sequence = jax.random.permutation(rng, number_of)
    packed, common = load_shares(number_of, rows * top, reach, slope, True), load_shares(number_of, rows * top, reach, slope, False)
    places = jnp.arange(number_of)

    def named(lengths, offset_by):
        used = int((lengths > 0).sum())
        fixed = max(1, used // 4)
        shifted = fixed + (places - fixed + offset_by * (used - fixed)) % max(1, number_of - fixed)
        return jnp.zeros((number_of,), jnp.int32).at[sequence[jnp.where(places < fixed, places, shifted)]].set(jnp.asarray(lengths, jnp.int32))

    lengths = jnp.where(number % 4 == 0, named(packed, number // 4), named(common, number - number // 4 - 1))
    mixed = jax.random.permutation(jax.random.fold_in(own, 3), number_of)
    giver, taker = mixed[0:number_of // 2 * 2:2], mixed[1:number_of // 2 * 2:2]
    margin = jnp.minimum(lengths[giver] - 1, reach - lengths[taker]) // 2
    margin = jnp.where((giver == sequence[0]) | (taker == sequence[0]) | (lengths[taker] == 0), 0, jnp.maximum(margin, 0))
    shifted = jax.random.randint(jax.random.fold_in(own, 4), (number_of // 2,), 0, 1 << 20) % (margin + 1)
    lengths = lengths.at[giver].add(-shifted).at[taker].add(shifted)
    labels = jnp.searchsorted(jnp.cumsum(lengths), jnp.arange(rows * top), side="right").astype(jnp.int32)
    grid = labels.reshape(top, rows).T
    grid = grid[jax.random.permutation(jax.random.fold_in(own, 1), rows)]
    offset_by = jax.random.randint(jax.random.fold_in(own, 2), (rows, 1), 0, top)
    return jnp.take_along_axis(grid, (jnp.arange(top)[None, :] + offset_by) % top, axis=1)


def load_shares(number_of, total, most, skew, full):
    portions = [(1 << 20) // math.isqrt(rank ** skew) + 1 for rank in range(1, number_of + 1)]
    largest = most if full else min(most, max(-(-total // number_of), total * portions[0] // sum(portions)))
    least = 1 if total - largest >= number_of - 1 else 0
    holding, spare = [largest] + [least] * (number_of - 1), total - largest - least * (number_of - 1)
    while spare > 0:
        candidates = [i for i in range(1, number_of) if holding[i] < largest] or [i for i in range(1, number_of) if holding[i] < most]
        whole, left = sum([portions[i] for i in candidates]), spare
        for i in candidates:
            extra = min(most - holding[i], max(1, left * portions[i] // whole), spare)
            holding[i] = holding[i] + extra
            spare = spare - extra
    return np.array(holding)


def normal_values(own_key, shape, deviation, bound, pieces=(), kind=jnp.bfloat16):
    level = block_levels(own_key, shape, pieces, -0.22, 0.18) if pieces else 1.0
    result = jax.random.normal(own_key, shape, jnp.float32) * deviation * level
    return jnp.minimum(jnp.maximum(result, -bound), bound).astype(kind)


def setup_inputs(seed: int = 0, part: int = 0) -> dict:
    splits = jax.random.split(jax.random.key(seed), 6)
    part_keys = jax.random.split(jax.random.fold_in(splits[5], part), 6)
    tokens = normal_values(part_keys[0], (STEPS, TOKENS, D), 1.0, 6.0, ((1, 8), (2, 16)))
    expert_ids_keys = jax.random.split(jax.random.fold_in(part_keys[1], 1), STEPS * TOKENS // TOK_DEV)
    expert_ids_turns = jax.random.permutation(jax.random.fold_in(part_keys[1], 3), STEPS * TOKENS // TOK_DEV)
    expert_ids = jax.vmap(lambda own, number: shared_out(jax.random.fold_in(part_keys[1], 2), own, number, TOK_DEV, E, TOP, MOST, 1))(expert_ids_keys, expert_ids_turns).reshape((STEPS, TOKENS, TOP))
    route_weights = jnp.clip(0.2 + 0.8 * jax.random.uniform(part_keys[2], (STEPS, TOKENS, TOP), jnp.float32) ** block_levels(part_keys[2], (STEPS, TOKENS, TOP), ((1, 8),), -0.2, 0.2), 0.2, 1.0)
    gate_train = normal_values(splits[3], (OWNERS, D, FF // 2), D ** -0.5, 0.109375, ((0, 8), (1, 16)))
    up_train = normal_values(splits[4], (OWNERS, D, FF // 2), D ** -0.5, 0.109375, ((0, 8), (1, 16)))
    return dict(tokens=tokens, expert_ids=expert_ids, route_weights=route_weights, gate_train=gate_train, up_train=up_train)


def reference(tokens, expert_ids, route_weights, gate_train, up_train):
    owner_count, model_dim, half_width = gate_train.shape
    gate_full = gate_train.astype(jnp.float32)
    up_full = up_train.astype(jnp.float32)

    def one_step(inputs):
        features, step_ids, step_weights = inputs
        rows_f = features.astype(jnp.float32)
        gate_val = jnp.einsum("nd,odj->noj", rows_f, gate_full, precision=lax.Precision.HIGHEST)
        up_val = jnp.einsum("nd,odj->noj", rows_f, up_full, precision=lax.Precision.HIGHEST)
        activation = jax.nn.silu(gate_val) * up_val
        activation = activation.reshape(rows_f.shape[0], owner_count // 2, 2, half_width)
        chosen = step_ids[..., None] == jnp.arange(owner_count // 2, dtype=jnp.int32)
        picked = jnp.sum(jnp.where(chosen[..., None, None], activation[:, None], jnp.float32(0.0)), axis=2)
        return (step_weights[..., None, None] * picked).astype(jnp.bfloat16)

    return lax.map(one_step, (tokens, expert_ids, route_weights))
```

```python
import functools

import jax
import jax.numpy as jnp
from jax import lax
from jax.experimental import pallas as pl
from jax.experimental.pallas import tpu as pltpu
from jax.sharding import Mesh, PartitionSpec as P

MOST = 80
X = ("dp", "xl")
BF, F32 = jnp.bfloat16, jnp.float32
ANY = pl.BlockSpec(memory_space=pl.ANY)
VM = pl.BlockSpec(memory_space=pltpu.VMEM)
SM = pl.BlockSpec(memory_space=pltpu.SMEM)


def ring(x, axis, size, step):
    return lax.ppermute(x, axis, [(i, (i + step) % size) for i in range(size)])


def ranks(member):
    n = member.shape[1]
    before = lax.broadcasted_iota(jnp.int32, (n, n), 0) < lax.broadcasted_iota(jnp.int32, (n, n), 1)
    return jnp.dot(member.astype(BF), before.astype(BF), preferred_element_type=F32)


def slots(rank, member):
    row = lax.broadcasted_iota(jnp.int32, (MOST, rank.shape[1]), 0).astype(F32)
    return (row == rank) & (member > 0)


def dispatch_kernel(pos, meta, feats, *outs):
    y, xl = pos[0], pos[2]
    zs, ss, width, n = feats.shape
    for s in range(ss):
        own = meta[2 * xl + s]
        rows = []
        members = []
        for d in range(4):
            e = lax.rem(y + d, 4).astype(F32)
            members.append(((own[0:1] == e) | (own[1:2] == e)).astype(F32))
        rank = ranks(jnp.concatenate(members, axis=0))
        for d in range(4):
            rows.append(slots(rank[d : d + 1], members[d]).astype(BF))
        onehot = jnp.concatenate(rows, axis=0)
        for z in range(zs):
            picked = lax.dot_general(onehot, feats[z, s], (((1,), (1,)), ((), ())), preferred_element_type=F32).astype(BF)
            for d in range(4):
                outs[d][s * MOST : (s + 1) * MOST, z * width : (z + 1) * width] = picked[d * MOST : (d + 1) * MOST]


def expert_kernel(chunks, pos, meta, *refs):
    xs, refs = refs[:8], refs[8:]
    ws, refs = refs[: 5 * chunks], refs[5 * chunks :]
    out, xbuf, wbuf, rwbuf, xsem, wsem = refs
    y, c, xl, dp = pos[0], pos[1], pos[2], pos[3]
    rows = xs[0].shape[0]
    depth = ws[0].shape[1]
    copies = []
    for g in range(8):
        copies.append(pltpu.make_async_copy(xs[g], xbuf.at[pl.ds(g * rows, rows)], xsem.at[g]))
    here = dp * 2 + xl
    for ch in range(chunks):
        own, left, right, far_a, far_b = ws[5 * ch : 5 * ch + 5]
        span = pl.ds(ch * depth, depth)
        for i, (src, off, zlo, zn) in enumerate(((own, 0, 0, 8), (left, 3, 0, 8), (right, 1, 0, 8), (far_a, 2, 0, 4), (far_b, 2, 4, 4))):
            j = lax.rem(here + off, 4)
            dst = wbuf.at[lax.div(j, 2), pl.ds(zlo, zn), lax.rem(j, 2), span]
            copies.append(pltpu.make_async_copy(src, dst, wsem.at[ch * 5 + i]))
    for cp in copies:
        cp.start()
    e = y.astype(F32)
    infos = []
    for cc in range(2):
        for d in range(4):
            for s in range(2):
                infos.append(meta[lax.rem(y + 4 - d, 4), c + cc - 2 * c * cc, 2 * xl + s])
    members = [((o[0:1] == e) | (o[1:2] == e)).astype(F32) for o in infos]
    rank = ranks(jnp.concatenate(members, axis=0))
    for i, o in enumerate(infos):
        weight = jnp.where(o[0:1] == e, o[2:3], o[3:4])
        value = jnp.sum(jnp.where(slots(rank[i : i + 1], members[i]), weight, 0.0), axis=1, keepdims=True)
        rwbuf[i * MOST : (i + 1) * MOST, :] = jnp.broadcast_to(value, (MOST, 128))
    for cp in copies:
        cp.wait()
    half = 4 * rows
    for m in range(2):
        data = xbuf[m * half : (m + 1) * half]
        rw = rwbuf[m * half : (m + 1) * half]
        rw = jnp.concatenate([rw, rw], axis=1)
        for t in range(2):
            gate = jnp.dot(data, wbuf[0, :, :, :, t * 256 : (t + 1) * 256].reshape(-1, 256), preferred_element_type=F32)
            up = jnp.dot(data, wbuf[1, :, :, :, t * 256 : (t + 1) * 256].reshape(-1, 256), preferred_element_type=F32)
            act = (rw * (gate / (1.0 + jnp.exp(-gate)) * up)).astype(BF)
            for d in range(4):
                out[lax.rem(y + 4 - d, 4), c + m - 2 * c * m, t] = act[d * rows : (d + 1) * rows]


def combine_kernel(meta, recv, out):
    steps = meta.shape[0]
    for s in range(steps):
        own = meta[s]
        members = [((own[0:1] == e) | (own[1:2] == e)).astype(F32) for e in range(4)]
        rank = ranks(jnp.concatenate(members, axis=0))
        left, right = [], []
        for e in range(4):
            place = slots(rank[e : e + 1], members[e])
            left.append(jnp.concatenate([(place & (own[k : k + 1] == e)).astype(BF) for k in range(2)], axis=1))
            part = pl.ds((s % 2) * MOST, MOST)
            right.append(jnp.concatenate([recv[e, h, s // 2, part] for h in range(2)], axis=1))
        picked = lax.dot_general(
            jnp.concatenate(left, axis=0), jnp.concatenate(right, axis=0), (((0,), (0,)), ((), ())), preferred_element_type=F32
        ).astype(BF)
        n = picked.shape[0] // 2
        out[s] = jnp.concatenate([picked[:n], picked[n:]], axis=1)


def body(tokens, expert_ids, route_weights, gate_train, up_train):
    chunks = 2
    dp, y, c, z, xl = (lax.axis_index(a) for a in ("dp", "y", "c", "z", "xl"))
    pos = jnp.stack([y, c, xl, dp]).astype(jnp.int32)
    steps, n, width = tokens.shape
    meta = jnp.concatenate([expert_ids.astype(F32), route_weights], axis=2).transpose(0, 2, 1)
    meta_all = lax.all_gather(meta, ("y", "c"), axis=0, tiled=False).reshape(4, 2, steps, 4, n)
    turned = tokens.transpose(0, 2, 1).reshape(2, steps // 2, width, n)
    mine = lax.dynamic_index_in_dim(turned, xl, 0, keepdims=False)
    theirs = lax.dynamic_index_in_dim(turned, 1 - xl, 0, keepdims=False)
    got = ring(theirs, "xl", 2, 1)
    pair = jnp.concatenate([jnp.where(xl == 0, mine, got), jnp.where(xl == 0, got, mine)], axis=1)
    feats = lax.all_gather(pair, "z", axis=0, tiled=False)
    sent = pl.pallas_call(
        dispatch_kernel,
        out_shape=[jax.ShapeDtypeStruct((2 * MOST, 16 * width), BF)] * 4,
        in_specs=[SM, VM, VM],
        out_specs=[VM] * 4,
        compiler_params=pltpu.CompilerParams(vmem_limit_bytes=32 << 20),
        name="dispatch",
    )(pos, meta, feats)
    held = [sent[0]] + [ring(sent[d], "y", 4, d) for d in (1, 2, 3)]
    other = [ring(h, "c", 2, 1) for h in held]
    source = jnp.where(dp == 0, gate_train[0], up_train[0])
    rows, units = source.shape
    blocks = source.reshape(rows, 8, units // 8).transpose(1, 0, 2)
    pieces = []
    for ch in range(chunks):
        depth = rows // chunks
        own = lax.all_to_all(blocks[:, ch * depth : (ch + 1) * depth], "z", split_axis=0, concat_axis=0, tiled=True)
        left, right = ring(own, X, 4, 1), ring(own, X, 4, -1)
        far_a, far_b = ring(left[:4], X, 4, 1), ring(right[4:], X, 4, -1)
        pieces += [own, left, right, far_a, far_b]
    act = pl.pallas_call(
        functools.partial(expert_kernel, chunks),
        out_shape=jax.ShapeDtypeStruct((4, 2, 2, 2 * MOST, 256), BF),
        in_specs=[SM, VM] + [ANY] * (8 + 5 * chunks),
        out_specs=VM,
        scratch_shapes=[
            pltpu.VMEM((16 * MOST, 16 * width), BF),
            pltpu.VMEM((2, 8, 2, rows, units // 8), BF),
            pltpu.VMEM((16 * MOST, 128), F32),
            pltpu.SemaphoreType.DMA((8,)),
            pltpu.SemaphoreType.DMA((5 * chunks,)),
        ],
        compiler_params=pltpu.CompilerParams(vmem_limit_bytes=44 << 20),
        cost_estimate=pl.CostEstimate(flops=16 * MOST * 16 * width * 1024 * 2, bytes_accessed=15 << 20, transcendentals=16 * MOST * 512),
        name="expert",
    )(pos, meta_all, *held, *other, *pieces)
    back = lax.all_to_all(act.reshape(16, 2 * MOST, 256), ("y", "c", "xl"), split_axis=0, concat_axis=0, tiled=True)
    out = pl.pallas_call(
        combine_kernel,
        out_shape=jax.ShapeDtypeStruct((steps, n, 1024), BF),
        in_specs=[VM, VM],
        out_specs=VM,
        compiler_params=pltpu.CompilerParams(vmem_limit_bytes=32 << 20),
        name="combine",
    )(meta, back.reshape(4, 2, 2, 2 * MOST, 256))
    return out.reshape(steps, n, 2, 2, 256)


def solution(mesh):
    fine = Mesh(mesh.devices.reshape(2, 4, 2, 8, 2), ("dp", "y", "c", "z", "xl"))
    group, tensor = ("dp", "y", "c"), ("z", "xl")
    in_specs = (
        P(None, group, tensor),
        P(None, group, None),
        P(None, group, None),
        P(("y", "c"), tensor, None),
        P(("y", "c"), tensor, None),
    )
    out_specs = P(None, group, None, None, tensor)
    return jax.shard_map(body, mesh=fine, in_specs=in_specs, out_specs=out_specs, check_vma=False)
```

```python
import functools

import jax
import jax.numpy as jnp
from jax import lax
from jax.experimental import pallas as pl
from jax.experimental.pallas import tpu as pltpu
from jax.sharding import Mesh, PartitionSpec as P

MOST = 80
X = ("dp", "xl")
BF, F32 = jnp.bfloat16, jnp.float32
ANY = pl.BlockSpec(memory_space=pl.ANY)
VM = pl.BlockSpec(memory_space=pltpu.VMEM)
SM = pl.BlockSpec(memory_space=pltpu.SMEM)


def ring(x, axis, size, step):
    return lax.ppermute(x, axis, [(i, (i + step) % size) for i in range(size)])


def ranks(member):
    n = member.shape[1]
    before = lax.broadcasted_iota(jnp.int32, (n, n), 0) < lax.broadcasted_iota(jnp.int32, (n, n), 1)
    return jnp.dot(member.astype(BF), before.astype(BF), preferred_element_type=F32)


def slots(rank, member):
    row = lax.broadcasted_iota(jnp.int32, (MOST, rank.shape[1]), 0).astype(F32)
    return (row == rank) & (member > 0)


def dispatch_kernel(pos, meta, *refs):
    y, xl = pos[0], pos[2]
    feats, outs = refs[:8], refs[8:]
    ss, width, n = feats[0].shape
    lane = lax.broadcasted_iota(jnp.int32, (MOST, 128), 1)
    for s in range(ss):
        own = meta[2 * xl + s]
        rows = []
        members = []
        for d in range(4):
            e = lax.rem(y + d, 4).astype(F32)
            members.append(((own[0:1] == e) | (own[1:2] == e)).astype(F32))
        rank = ranks(jnp.concatenate(members, axis=0))
        for d in range(4):
            place = slots(rank[d : d + 1], members[d])
            rows.append(place.astype(BF))
            e = lax.rem(y + d, 4).astype(F32)
            weight = jnp.where(own[0:1] == e, own[2:3], own[3:4])
            whole = jnp.broadcast_to(jnp.sum(jnp.where(place, weight, 0.0), axis=1, keepdims=True), (MOST, 128))
            high = whole.astype(BF)
            rest = whole - high.astype(F32)
            mid = rest.astype(BF)
            low = (rest - mid.astype(F32)).astype(BF)
            terms = jnp.where(lane == 0, high.astype(F32), jnp.where(lane == 1, mid.astype(F32), jnp.where(lane == 2, low.astype(F32), 0.0)))
            outs[d][s * MOST : (s + 1) * MOST, 8 * width :] = terms.astype(BF)
        onehot = jnp.concatenate(rows, axis=0)
        for k in range(8):
            picked = lax.dot_general(onehot, feats[k][s], (((1,), (1,)), ((), ())), preferred_element_type=F32).astype(BF)
            for d in range(4):
                outs[d][s * MOST : (s + 1) * MOST, k * width : (k + 1) * width] = picked[d * MOST : (d + 1) * MOST]


def expert_kernel(chunks, pos, *refs):
    xs, refs = refs[:8], refs[8:]
    ws, refs = refs[: 5 * chunks], refs[5 * chunks :]
    out, xbuf, wbuf, xsem, wsem = refs
    y, c, xl, dp = pos[0], pos[1], pos[2], pos[3]
    rows = xs[0].shape[0]
    depth = ws[0].shape[1]
    width = 2 * 8 * depth * chunks
    xcopies, wcopies = [], []
    for g in range(8):
        xcopies.append(pltpu.make_async_copy(xs[g], xbuf.at[pl.ds(g * rows, rows)], xsem.at[g]))
    here = dp * 2 + xl
    for ch in range(chunks):
        own, left, right, far_a, far_b = ws[5 * ch : 5 * ch + 5]
        span = pl.ds(ch * depth, depth)
        for i, (src, off, zlo, zn) in enumerate(((own, 0, 0, 8), (left, 3, 0, 8), (right, 1, 0, 8), (far_a, 2, 0, 4), (far_b, 2, 4, 4))):
            j = lax.rem(here + off, 4)
            for k in range(zn):
                dst = wbuf.at[lax.div(j, 2), lax.rem(zlo + k + 8 - pos[4], 8), lax.rem(j, 2), span]
                wcopies.append(pltpu.make_async_copy(src.at[k], dst, wsem.at[ch * 5 + i, k]))
    for cp in wcopies + xcopies:
        cp.start()
    for cp in wcopies:
        cp.wait()
    half = 4 * rows
    for m in range(2):
        for cp in xcopies[4 * m : 4 * m + 4]:
            cp.wait()
        part = slice(m * half, (m + 1) * half)
        data = xbuf[part, :width]
        rw = jnp.sum(xbuf[part, width:].astype(F32), axis=1, keepdims=True)
        gate = jnp.dot(data, wbuf[0].reshape(width, 256), preferred_element_type=F32)
        up = jnp.dot(data, wbuf[1].reshape(width, 256), preferred_element_type=F32)
        act = (rw * (gate / (1.0 + jnp.exp(-gate)) * up)).astype(BF)
        for d in range(4):
            for t in range(2):
                out[lax.rem(y + 4 - d, 4), c + m - 2 * c * m, t] = act[d * rows : (d + 1) * rows, t * 128 : (t + 1) * 128]


def combine_kernel(meta, recv_a, recv_b, out):
    steps = meta.shape[0]
    for s in range(steps):
        own = meta[s]
        members = [((own[0:1] == e) | (own[1:2] == e)).astype(F32) for e in range(4)]
        rank = ranks(jnp.concatenate(members, axis=0))
        left, right = [], []
        for e in range(4):
            place = slots(rank[e : e + 1], members[e])
            left.append(jnp.concatenate([(place & (own[k : k + 1] == e)).astype(BF) for k in range(2)], axis=1))
            part = pl.ds((s % 2) * MOST, MOST)
            right.append(jnp.concatenate([r[e, h, s // 2, part] for h in range(2) for r in (recv_a, recv_b)], axis=1))
        picked = lax.dot_general(
            jnp.concatenate(left, axis=0), jnp.concatenate(right, axis=0), (((0,), (0,)), ((), ())), preferred_element_type=F32
        ).astype(BF)
        n = picked.shape[0] // 2
        out[s] = jnp.concatenate([picked[:n], picked[n:]], axis=1)


def body(tokens, expert_ids, route_weights, gate_train, up_train):
    chunks, rounds = 1, 2
    dp, y, c, z, xl = (lax.axis_index(a) for a in ("dp", "y", "c", "z", "xl"))
    pos = jnp.stack([y, c, xl, dp, z]).astype(jnp.int32)
    steps, n, width = tokens.shape
    meta = jnp.concatenate([expert_ids.astype(F32), route_weights], axis=2).transpose(0, 2, 1)
    turned = tokens.transpose(0, 2, 1).reshape(2, steps // 2, width, n)
    mine = lax.dynamic_index_in_dim(turned, xl, 0, keepdims=False)
    theirs = lax.dynamic_index_in_dim(turned, 1 - xl, 0, keepdims=False)
    got = ring(theirs, "xl", 2, 1)
    pair = jnp.concatenate([jnp.where(xl == 0, mine, got), jnp.where(xl == 0, got, mine)], axis=1)
    source = jnp.where(dp == 0, gate_train[0], up_train[0])
    rows, units = source.shape
    depth = rows // chunks
    wide = units // 8 // 2 // rounds
    blocks = source.reshape(rows, 8, 2, rounds, wide).transpose(3, 1, 0, 2, 4).reshape(rounds, 8, rows, 2 * wide)
    below, above = [pair], [pair]
    for k in range(2):
        below.append(ring(below[-1], "z", 8, 1))
        above.append(ring(above[-1], "z", 8, -1))
    part = blocks[0, :, :depth]
    part, below[2], above[2] = lax.optimization_barrier((part, below[2], above[2]))
    first = lax.all_to_all(part, "z", split_axis=0, concat_axis=0, tiled=True)
    for k in range(2, 3):
        below.append(ring(below[-1], "z", 8, 1))
        above.append(ring(above[-1], "z", 8, -1))
    opposite = jnp.concatenate([ring(below[3][:1], "z", 8, 1), ring(above[3][1:], "z", 8, -1)], axis=0)
    feats = [pair] + above[1:] + [opposite] + below[:0:-1]
    pieces = []
    for r in range(rounds):
        for ch in range(chunks):
            own = first
            if r + ch > 0:
                part = blocks[r, :, ch * depth : (ch + 1) * depth]
                part, opposite, first = lax.optimization_barrier((part, opposite, first))
                pieces[-1][0] = first
                own = lax.all_to_all(part, "z", split_axis=0, concat_axis=0, tiled=True)
                first = own
                own, far_a, far_b = lax.optimization_barrier((own, pieces[-1][3], pieces[-1][4]))
                pieces[-1][3:] = far_a, far_b
            left, right = ring(own, X, 4, 1), ring(own, X, 4, -1)
            far_a, far_b = ring(left[:4], X, 4, 1), ring(right[4:], X, 4, -1)
            pieces.append([own, left, right, far_a, far_b])
    feats[4] = opposite
    sent = pl.pallas_call(
        dispatch_kernel,
        out_shape=[jax.ShapeDtypeStruct((2 * MOST, 16 * width + 128), BF)] * 4,
        in_specs=[SM] + [VM] * 9,
        out_specs=[VM] * 4,
        compiler_params=pltpu.CompilerParams(vmem_limit_bytes=32 << 20),
        name="dispatch",
    )(pos, meta, *feats)
    held = [sent[0]] + [ring(sent[d], "y", 4, d) for d in (1, 2, 3)]
    other = [ring(h, "c", 2, 1) for h in held]
    backs = []
    for r in range(rounds):
        ws = [w for ch in range(chunks) for w in pieces[r * chunks + ch]]
        act = pl.pallas_call(
            functools.partial(expert_kernel, chunks),
            out_shape=jax.ShapeDtypeStruct((4, 2, 2, 2 * MOST, wide), BF),
            in_specs=[SM] + [ANY] * (8 + 5 * chunks),
            out_specs=VM,
            scratch_shapes=[
                pltpu.VMEM((16 * MOST, 16 * width + 128), BF),
                pltpu.VMEM((2, 8, 2, rows, 2 * wide), BF),
                pltpu.SemaphoreType.DMA((8,)),
                pltpu.SemaphoreType.DMA((5 * chunks, 8)),
            ],
            compiler_params=pltpu.CompilerParams(vmem_limit_bytes=58 << 20),
            cost_estimate=pl.CostEstimate(
                flops=16 * MOST * 16 * width * 8 * wide, bytes_accessed=12 << 20, transcendentals=16 * MOST * 2 * wide
            ),
            name="expert",
        )(pos, *held, *other, *ws)
        back = lax.all_to_all(act.reshape(16, 2 * MOST, wide), ("y", "c", "xl"), split_axis=0, concat_axis=0, tiled=True)
        backs.append(back.reshape(4, 2, 2, 2 * MOST, wide))
    out = pl.pallas_call(
        combine_kernel,
        out_shape=jax.ShapeDtypeStruct((steps, n, 1024), BF),
        in_specs=[VM] * 3,
        out_specs=VM,
        compiler_params=pltpu.CompilerParams(vmem_limit_bytes=32 << 20),
        name="combine",
    )(meta, *backs)
    return out.reshape(steps, n, 2, 2, 256)


def solution(mesh):
    fine = Mesh(mesh.devices.reshape(2, 4, 2, 8, 2), ("dp", "y", "c", "z", "xl"))
    group, tensor = ("dp", "y", "c"), ("z", "xl")
    in_specs = (
        P(None, group, tensor),
        P(None, group, None),
        P(None, group, None),
        P(("y", "c"), tensor, None),
        P(("y", "c"), tensor, None),
    )
    out_specs = P(None, group, None, None, tensor)
    return jax.shard_map(body, mesh=fine, in_specs=in_specs, out_specs=out_specs, check_vma=False)
```

```python
import functools

import jax
import jax.numpy as jnp
from jax import lax
from jax.experimental import pallas as pl
from jax.experimental.pallas import tpu as pltpu
from jax.sharding import Mesh, PartitionSpec as P

MOST = 80
X = ("dp", "xl")
BF, F32 = jnp.bfloat16, jnp.float32
ANY = pl.BlockSpec(memory_space=pl.ANY)
VM = pl.BlockSpec(memory_space=pltpu.VMEM)
SM = pl.BlockSpec(memory_space=pltpu.SMEM)


def ring(x, axis, size, step):
    return lax.ppermute(x, axis, [(i, (i + step) % size) for i in range(size)])


def ranks(member):
    n = member.shape[1]
    before = lax.broadcasted_iota(jnp.int32, (n, n), 0) < lax.broadcasted_iota(jnp.int32, (n, n), 1)
    return jnp.dot(member.astype(BF), before.astype(BF), preferred_element_type=F32)


def slots(rank, member):
    row = lax.broadcasted_iota(jnp.int32, (MOST, rank.shape[1]), 0).astype(F32)
    return (row == rank) & (member > 0)


def dispatch_kernel(pos, meta, *refs):
    y, xl = pos[0], pos[2]
    feats, outs = refs[:8], refs[8:]
    ss, width, n = feats[0].shape
    lane = lax.broadcasted_iota(jnp.int32, (MOST, 128), 1)
    for s in range(ss):
        own = meta[2 * xl + s]
        rows = []
        members = []
        for d in range(4):
            e = lax.rem(y + d, 4).astype(F32)
            members.append(((own[0:1] == e) | (own[1:2] == e)).astype(F32))
        rank = ranks(jnp.concatenate(members, axis=0))
        for d in range(4):
            place = slots(rank[d : d + 1], members[d])
            rows.append(place.astype(BF))
            e = lax.rem(y + d, 4).astype(F32)
            weight = jnp.where(own[0:1] == e, own[2:3], own[3:4])
            whole = jnp.broadcast_to(jnp.sum(jnp.where(place, weight, 0.0), axis=1, keepdims=True), (MOST, 128))
            high = whole.astype(BF)
            rest = whole - high.astype(F32)
            mid = rest.astype(BF)
            low = (rest - mid.astype(F32)).astype(BF)
            terms = jnp.where(lane == 0, high.astype(F32), jnp.where(lane == 1, mid.astype(F32), jnp.where(lane == 2, low.astype(F32), 0.0)))
            outs[d][s * MOST : (s + 1) * MOST, 8 * width :] = terms.astype(BF)
        onehot = jnp.concatenate(rows, axis=0)
        for k in range(8):
            picked = lax.dot_general(onehot, feats[k][s], (((1,), (1,)), ((), ())), preferred_element_type=F32).astype(BF)
            for d in range(4):
                outs[d][s * MOST : (s + 1) * MOST, k * width : (k + 1) * width] = picked[d * MOST : (d + 1) * MOST]


def columns_kernel(pos, gate, up, out_a, out_b, sem):
    for flag, src in ((0, gate), (1, up)):

        @pl.when(pos[3] == flag)
        def _(src=src):
            copies = []
            for r, out in enumerate((out_a, out_b)):
                for z in range(8):
                    for t in range(2):
                        columns = pl.ds(z * 512 + t * 256 + r * 128, 128)
                        copies.append(
                            pltpu.make_async_copy(src.at[0, :, columns], out.at[z, :, pl.ds(t * 128, 128)], sem.at[len(copies)])
                        )
            for cp in copies:
                cp.start()
            for cp in copies:
                cp.wait()


def expert_kernel(chunks, pos, *refs):
    xs, refs = refs[:8], refs[8:]
    ws, refs = refs[: 5 * chunks], refs[5 * chunks :]
    out, xbuf, wbuf, xsem, wsem = refs
    y, c, xl, dp = pos[0], pos[1], pos[2], pos[3]
    rows = xs[0].shape[0]
    depth = ws[0].shape[1]
    width = 2 * 8 * depth * chunks
    xcopies, wcopies = [], []
    for g in range(8):
        xcopies.append(pltpu.make_async_copy(xs[g], xbuf.at[pl.ds(g * rows, rows)], xsem.at[g]))
    here = dp * 2 + xl
    for ch in range(chunks):
        own, left, right, far_a, far_b = ws[5 * ch : 5 * ch + 5]
        span = pl.ds(ch * depth, depth)
        for i, (src, off, zlo, zn) in enumerate(((own, 0, 0, 8), (left, 3, 0, 8), (right, 1, 0, 8), (far_a, 2, 0, 4), (far_b, 2, 4, 4))):
            j = lax.rem(here + off, 4)
            for k in range(zn):
                dst = wbuf.at[lax.div(j, 2), lax.rem(zlo + k + 8 - pos[4], 8), lax.rem(j, 2), span]
                wcopies.append(pltpu.make_async_copy(src.at[k], dst, wsem.at[ch * 5 + i, k]))
    for cp in wcopies + xcopies:
        cp.start()
    for cp in wcopies:
        cp.wait()
    half = 4 * rows
    for m in range(2):
        for cp in xcopies[4 * m : 4 * m + 4]:
            cp.wait()
        part = slice(m * half, (m + 1) * half)
        data = xbuf[part, :width]
        rw = jnp.sum(xbuf[part, width:].astype(F32), axis=1, keepdims=True)
        gate = jnp.dot(data, wbuf[0].reshape(width, 256), preferred_element_type=F32)
        up = jnp.dot(data, wbuf[1].reshape(width, 256), preferred_element_type=F32)
        act = (rw * (gate / (1.0 + jnp.exp(-gate)) * up)).astype(BF)
        for d in range(4):
            for t in range(2):
                out[lax.rem(y + 4 - d, 4), c + m - 2 * c * m, t] = act[d * rows : (d + 1) * rows, t * 128 : (t + 1) * 128]


def combine_kernel(meta, recv_a, recv_b, out):
    steps = meta.shape[0]
    for s in range(steps):
        own = meta[s]
        members = [((own[0:1] == e) | (own[1:2] == e)).astype(F32) for e in range(4)]
        rank = ranks(jnp.concatenate(members, axis=0))
        left, right = [], []
        for e in range(4):
            place = slots(rank[e : e + 1], members[e])
            left.append(jnp.concatenate([(place & (own[k : k + 1] == e)).astype(BF) for k in range(2)], axis=1))
            part = pl.ds((s % 2) * MOST, MOST)
            right.append(jnp.concatenate([r[e, h, s // 2, part] for h in range(2) for r in (recv_a, recv_b)], axis=1))
        picked = lax.dot_general(
            jnp.concatenate(left, axis=0), jnp.concatenate(right, axis=0), (((0,), (0,)), ((), ())), preferred_element_type=F32
        ).astype(BF)
        n = picked.shape[0] // 2
        out[s] = jnp.concatenate([picked[:n], picked[n:]], axis=1)


def body(tokens, expert_ids, route_weights, gate_train, up_train):
    barrier = lax.optimization_barrier
    dp, y, c, z, xl = (lax.axis_index(a) for a in ("dp", "y", "c", "z", "xl"))
    pos = jnp.stack([y, c, xl, dp, z]).astype(jnp.int32)
    steps, n, width = tokens.shape
    meta = jnp.concatenate([expert_ids.astype(F32), route_weights], axis=2).transpose(0, 2, 1)
    turned = tokens.transpose(0, 2, 1).reshape(2, steps // 2, width, n)
    mine = lax.dynamic_index_in_dim(turned, xl, 0, keepdims=False)
    theirs = lax.dynamic_index_in_dim(turned, 1 - xl, 0, keepdims=False)
    got = ring(theirs, "xl", 2, 1)
    pair = jnp.concatenate([jnp.where(xl == 0, mine, got), jnp.where(xl == 0, got, mine)], axis=1)
    rows, units = gate_train.shape[1:]
    wide = units // 32
    blocks = pl.pallas_call(
        columns_kernel,
        out_shape=[jax.ShapeDtypeStruct((8, rows, 2 * wide), BF)] * 2,
        in_specs=[SM, ANY, ANY],
        out_specs=[ANY] * 2,
        scratch_shapes=[pltpu.SemaphoreType.DMA((32,))],
        name="columns",
    )(pos, gate_train, up_train)

    def exchange(x):
        return lax.all_to_all(x, "z", split_axis=0, concat_axis=0, tiled=True)

    below, above = [pair], [pair]
    for k in range(3):
        below.append(ring(below[-1], "z", 8, 1))
        above.append(ring(above[-1], "z", 8, -1))
    own_a, below[3], above[3] = barrier((blocks[0], below[3], above[3]))
    own_a = exchange(own_a)
    opposite = jnp.concatenate([ring(below[3][:1], "z", 8, 1), ring(above[3][1:], "z", 8, -1)], axis=0)
    feats = [pair] + above[1:] + [opposite] + below[:0:-1]
    sent = pl.pallas_call(
        dispatch_kernel,
        out_shape=[jax.ShapeDtypeStruct((2 * MOST, 16 * width + 128), BF)] * 4,
        in_specs=[SM] + [VM] * 9,
        out_specs=[VM] * 4,
        compiler_params=pltpu.CompilerParams(vmem_limit_bytes=24 << 20),
        name="dispatch",
    )(pos, meta, *feats)
    held = [sent[0]] + [ring(sent[d], "y", 4, d) for d in (1, 2, 3)]
    other = [ring(sent[0], "c", 2, 1)]
    own_a, other[0] = barrier((own_a, other[0]))
    own_b, own_a = barrier((blocks[1], own_a))
    own_b = exchange(own_b)
    pieces = []
    for own in (own_a, own_b):
        if pieces:
            own, *pieces[0] = barrier((own, *pieces[0]))
        left, right = ring(own, X, 4, 1), ring(own, X, 4, -1)
        far_a, far_b = ring(left[:4], X, 4, 1), ring(right[4:], X, 4, -1)
        pieces.append([own, left, right, far_a, far_b])
    held[1:] = barrier(tuple(held[1:]))
    other += [ring(h, "c", 2, 1) for h in held[1:]]
    backs = []
    for ws in pieces:
        act = pl.pallas_call(
            functools.partial(expert_kernel, 1),
            out_shape=jax.ShapeDtypeStruct((4, 2, 2, 2 * MOST, wide), BF),
            in_specs=[SM] + [ANY] * 13,
            out_specs=VM,
            scratch_shapes=[
                pltpu.VMEM((16 * MOST, 16 * width + 128), BF),
                pltpu.VMEM((2, 8, 2, rows, 2 * wide), BF),
                pltpu.SemaphoreType.DMA((8,)),
                pltpu.SemaphoreType.DMA((5, 8)),
            ],
            compiler_params=pltpu.CompilerParams(vmem_limit_bytes=24 << 20),
            cost_estimate=pl.CostEstimate(
                flops=16 * MOST * 16 * width * 8 * wide, bytes_accessed=12 << 20, transcendentals=16 * MOST * 2 * wide
            ),
            name="expert",
        )(pos, *held, *other, *ws)
        back = lax.all_to_all(act.reshape(16, 2 * MOST, wide), ("y", "c", "xl"), split_axis=0, concat_axis=0, tiled=True)
        backs.append(back.reshape(4, 2, 2, 2 * MOST, wide))
    out = pl.pallas_call(
        combine_kernel,
        out_shape=jax.ShapeDtypeStruct((steps, n, 1024), BF),
        in_specs=[VM] * 3,
        out_specs=VM,
        compiler_params=pltpu.CompilerParams(vmem_limit_bytes=24 << 20),
        name="combine",
    )(meta, *backs)
    return out.reshape(steps, n, 2, 2, 256)


def solution(mesh):
    fine = Mesh(mesh.devices.reshape(2, 4, 2, 8, 2), ("dp", "y", "c", "z", "xl"))
    group, tensor = ("dp", "y", "c"), ("z", "xl")
    in_specs = (
        P(None, group, tensor),
        P(None, group, None),
        P(None, group, None),
        P(("y", "c"), tensor, None),
        P(("y", "c"), tensor, None),
    )
    out_specs = P(None, group, None, None, tensor)
    return jax.shard_map(body, mesh=fine, in_specs=in_specs, out_specs=out_specs, check_vma=False)
```

```python
import jax
import jax.numpy as jnp
from jax import lax
from jax.experimental import pallas as pl
from jax.experimental.pallas import tpu as pltpu
from jax.sharding import Mesh, PartitionSpec as P

MOST = 80
X = ("dp", "xl")
BF, F32 = jnp.bfloat16, jnp.float32
VM = pl.BlockSpec(memory_space=pltpu.VMEM)
SM = pl.BlockSpec(memory_space=pltpu.SMEM)


def ring(x, axis, size, step):
    return lax.ppermute(x, axis, [(i, (i + step) % size) for i in range(size)])


def ranks(member):
    n = member.shape[1]
    before = lax.broadcasted_iota(jnp.int32, (n, n), 0) < lax.broadcasted_iota(jnp.int32, (n, n), 1)
    return jnp.dot(member.astype(BF), before.astype(BF), preferred_element_type=F32)


def slots(rank, member):
    row = lax.broadcasted_iota(jnp.int32, (MOST, rank.shape[1]), 0).astype(F32)
    return (row == rank) & (member > 0)


def dispatch_kernel(pos, meta, *refs):
    y, xl = pos[0], pos[2]
    feats, outs = refs[:8], refs[8:]
    ss, width, n = feats[0].shape
    lane = lax.broadcasted_iota(jnp.int32, (MOST, 128), 1)
    for s in range(ss):
        own = meta[2 * xl + s]
        rows = []
        members = []
        for d in range(4):
            e = lax.rem(y + d, 4).astype(F32)
            members.append(((own[0:1] == e) | (own[1:2] == e)).astype(F32))
        rank = ranks(jnp.concatenate(members, axis=0))
        for d in range(4):
            place = slots(rank[d : d + 1], members[d])
            rows.append(place.astype(BF))
            e = lax.rem(y + d, 4).astype(F32)
            weight = jnp.where(own[0:1] == e, own[2:3], own[3:4])
            whole = jnp.broadcast_to(jnp.sum(jnp.where(place, weight, 0.0), axis=1, keepdims=True), (MOST, 128))
            high = whole.astype(BF)
            rest = whole - high.astype(F32)
            mid = rest.astype(BF)
            low = (rest - mid.astype(F32)).astype(BF)
            terms = jnp.where(lane == 0, high.astype(F32), jnp.where(lane == 1, mid.astype(F32), jnp.where(lane == 2, low.astype(F32), 0.0)))
            outs[d][s * MOST : (s + 1) * MOST, 8 * width :] = terms.astype(BF)
        onehot = jnp.concatenate(rows, axis=0)
        for k in range(8):
            picked = lax.dot_general(onehot, feats[k][s], (((1,), (1,)), ((), ())), preferred_element_type=F32).astype(BF)
            for d in range(4):
                outs[d][s * MOST : (s + 1) * MOST, k * width : (k + 1) * width] = picked[d * MOST : (d + 1) * MOST]


def columns_kernel(pos, gate, up, out_a, out_b):
    for flag, src in ((0, gate), (1, up)):

        @pl.when(pos[3] == flag)
        def _(src=src):
            for r, out in enumerate((out_a, out_b)):
                for z in range(8):
                    for t in range(2):
                        first = z * 512 + t * 256 + r * 128
                        out[z, :, t * 128 : (t + 1) * 128] = src[0, :, first : first + 128]


def expert_kernel(pos, *refs):
    xs, ws, out, wbuf = refs[:8], refs[8:13], refs[13], refs[14]
    y, c, xl, dp, z = (pos[i] for i in range(5))
    rows = xs[0].shape[0]
    width = 16 * ws[0].shape[1]
    for src, off, low in ((ws[0], 0, 0), (ws[1], 3, 0), (ws[2], 1, 0), (ws[3], 2, 0), (ws[4], 2, 4)):
        j = lax.rem(dp * 2 + xl + off, 4)
        for k in range(src.shape[0]):
            wbuf[lax.div(j, 2), lax.rem(low + k + 8 - z, 8), lax.rem(j, 2)] = src[k]
    for g in range(8):
        d, cc = g % 4, g // 4
        data = xs[g][:, :width]
        rw = jnp.sum(xs[g][:, width:].astype(F32), axis=1, keepdims=True)
        gate = jnp.dot(data, wbuf[0].reshape(width, 256), preferred_element_type=F32)
        up = jnp.dot(data, wbuf[1].reshape(width, 256), preferred_element_type=F32)
        act = (rw * (gate / (1.0 + jnp.exp(-gate)) * up)).astype(BF)
        for t in range(2):
            out[lax.rem(y + 4 - d, 4), c + cc - 2 * c * cc, t] = act[:, t * 128 : (t + 1) * 128]


def combine_kernel(meta, recv_a, recv_b, out):
    steps = meta.shape[0]
    for s in range(steps):
        own = meta[s]
        members = [((own[0:1] == e) | (own[1:2] == e)).astype(F32) for e in range(4)]
        rank = ranks(jnp.concatenate(members, axis=0))
        left, right = [], []
        for e in range(4):
            place = slots(rank[e : e + 1], members[e])
            left.append(jnp.concatenate([(place & (own[k : k + 1] == e)).astype(BF) for k in range(2)], axis=1))
            part = pl.ds((s % 2) * MOST, MOST)
            right.append(jnp.concatenate([r[e, h, s // 2, part] for h in range(2) for r in (recv_a, recv_b)], axis=1))
        picked = lax.dot_general(
            jnp.concatenate(left, axis=0), jnp.concatenate(right, axis=0), (((0,), (0,)), ((), ())), preferred_element_type=F32
        ).astype(BF)
        n = picked.shape[0] // 2
        out[s] = jnp.concatenate([picked[:n], picked[n:]], axis=1)


def body(tokens, expert_ids, route_weights, gate_train, up_train):
    barrier = lax.optimization_barrier
    dp, y, c, z, xl = (lax.axis_index(a) for a in ("dp", "y", "c", "z", "xl"))
    pos = jnp.stack([y, c, xl, dp, z]).astype(jnp.int32)
    steps, n, width = tokens.shape
    meta = jnp.concatenate([expert_ids.astype(F32), route_weights], axis=2).transpose(0, 2, 1)
    turned = tokens.transpose(0, 2, 1).reshape(2, steps // 2, width, n)
    mine = lax.dynamic_index_in_dim(turned, xl, 0, keepdims=False)
    theirs = lax.dynamic_index_in_dim(turned, 1 - xl, 0, keepdims=False)
    got = ring(theirs, "xl", 2, 1)
    pair = jnp.concatenate([jnp.where(xl == 0, mine, got), jnp.where(xl == 0, got, mine)], axis=1)
    rows, units = gate_train.shape[1:]
    wide = units // 32
    blocks = pl.pallas_call(
        columns_kernel,
        out_shape=[jax.ShapeDtypeStruct((8, rows, 2 * wide), BF)] * 2,
        in_specs=[SM, VM, VM],
        out_specs=[VM] * 2,
        compiler_params=pltpu.CompilerParams(vmem_limit_bytes=16 << 20),
        name="columns",
    )(pos, gate_train, up_train)

    def exchange(x):
        return lax.all_to_all(x, "z", split_axis=0, concat_axis=0, tiled=True)

    below, above = [pair], [pair]
    for k in range(3):
        below.append(ring(below[-1], "z", 8, 1))
        above.append(ring(above[-1], "z", 8, -1))
    last = barrier((blocks[0], ring(below[3][:1], "z", 8, 1), ring(above[3][1:], "z", 8, -1)))
    own_a = exchange(last[0])
    opposite = jnp.concatenate(last[1:], axis=0)
    feats = [pair] + above[1:] + [opposite] + below[:0:-1]
    sent = pl.pallas_call(
        dispatch_kernel,
        out_shape=[jax.ShapeDtypeStruct((2 * MOST, 16 * width + 128), BF)] * 4,
        in_specs=[SM] + [VM] * 9,
        out_specs=[VM] * 4,
        compiler_params=pltpu.CompilerParams(vmem_limit_bytes=24 << 20),
        name="dispatch",
    )(pos, meta, *feats)
    held = [sent[0]] + [ring(sent[d], "y", 4, d) for d in (1, 2, 3)]
    other = [ring(sent[0], "c", 2, 1)]
    own_a, other[0] = barrier((own_a, other[0]))
    own_b, own_a = barrier((blocks[1], own_a))
    own_b = exchange(own_b)
    pieces = []
    for own in (own_a, own_b):
        if pieces:
            own, *pieces[0] = barrier((own, *pieces[0]))
        left, right = ring(own, X, 4, 1), ring(own, X, 4, -1)
        far_a, far_b = ring(left[:4], X, 4, 1), ring(right[4:], X, 4, -1)
        pieces.append([own, left, right, far_a, far_b])
    held[1:] = barrier(tuple(held[1:]))
    other += [ring(h, "c", 2, 1) for h in held[1:]]
    backs = []
    for ws in pieces:
        act = pl.pallas_call(
            expert_kernel,
            out_shape=jax.ShapeDtypeStruct((4, 2, 2, 2 * MOST, wide), BF),
            in_specs=[SM] + [VM] * 13,
            out_specs=VM,
            scratch_shapes=[pltpu.VMEM((2, 8, 2, rows, 2 * wide), BF)],
            compiler_params=pltpu.CompilerParams(vmem_limit_bytes=24 << 20),
            cost_estimate=pl.CostEstimate(
                flops=16 * MOST * 16 * width * 8 * wide, bytes_accessed=12 << 20, transcendentals=16 * MOST * 2 * wide
            ),
            name="expert",
        )(pos, *held, *other, *ws)
        back = lax.all_to_all(act.reshape(16, 2 * MOST, wide), ("y", "c", "xl"), split_axis=0, concat_axis=0, tiled=True)
        backs.append(back.reshape(4, 2, 2, 2 * MOST, wide))
    out = pl.pallas_call(
        combine_kernel,
        out_shape=jax.ShapeDtypeStruct((steps, n, 1024), BF),
        in_specs=[VM] * 3,
        out_specs=VM,
        compiler_params=pltpu.CompilerParams(vmem_limit_bytes=24 << 20),
        name="combine",
    )(meta, *backs)
    return out.reshape(steps, n, 2, 2, 256)


def solution(mesh):
    fine = Mesh(mesh.devices.reshape(2, 4, 2, 8, 2), ("dp", "y", "c", "z", "xl"))
    group, tensor = ("dp", "y", "c"), ("z", "xl")
    in_specs = (
        P(None, group, tensor),
        P(None, group, None),
        P(None, group, None),
        P(("y", "c"), tensor, None),
        P(("y", "c"), tensor, None),
    )
    out_specs = P(None, group, None, None, tensor)
    return jax.shard_map(body, mesh=fine, in_specs=in_specs, out_specs=out_specs, check_vma=False)
```

```python
import jax
import jax.numpy as jnp
from jax import lax
from jax.experimental import pallas as pl
from jax.experimental.pallas import tpu as pltpu
from jax.sharding import Mesh, PartitionSpec as P

MOST = 80
X = ("dp", "xl")
BF, F32 = jnp.bfloat16, jnp.float32
HBM = pl.BlockSpec(memory_space=pltpu.HBM)
VM = pl.BlockSpec(memory_space=pltpu.VMEM)
SM = pl.BlockSpec(memory_space=pltpu.SMEM)


def ring(x, axis, size, step):
    return lax.ppermute(x, axis, [(i, (i + step) % size) for i in range(size)])


def ranks(member):
    n = member.shape[1]
    before = lax.broadcasted_iota(jnp.int32, (n, n), 0) < lax.broadcasted_iota(jnp.int32, (n, n), 1)
    return jnp.dot(member.astype(BF), before.astype(BF), preferred_element_type=F32)


def slots(rank, member):
    row = lax.broadcasted_iota(jnp.int32, (MOST, rank.shape[1]), 0).astype(F32)
    return (row == rank) & (member > 0)


def dispatch_kernel(pos, meta, *refs):
    y, xl = pos[0], pos[2]
    feats, outs = refs[:8], refs[8:]
    ss, width, n = feats[0].shape
    lane = lax.broadcasted_iota(jnp.int32, (MOST, 128), 1)
    for s in range(ss):
        own = meta[2 * xl + s]
        rows = []
        members = []
        for d in range(4):
            e = lax.rem(y + d, 4).astype(F32)
            members.append(((own[0:1] == e) | (own[1:2] == e)).astype(F32))
        rank = ranks(jnp.concatenate(members, axis=0))
        for d in range(4):
            place = slots(rank[d : d + 1], members[d])
            rows.append(place.astype(BF))
            e = lax.rem(y + d, 4).astype(F32)
            weight = jnp.where(own[0:1] == e, own[2:3], own[3:4])
            whole = jnp.broadcast_to(jnp.sum(jnp.where(place, weight, 0.0), axis=1, keepdims=True), (MOST, 128))
            high = whole.astype(BF)
            rest = whole - high.astype(F32)
            mid = rest.astype(BF)
            low = (rest - mid.astype(F32)).astype(BF)
            terms = jnp.where(lane == 0, high.astype(F32), jnp.where(lane == 1, mid.astype(F32), jnp.where(lane == 2, low.astype(F32), 0.0)))
            outs[d][s * MOST : (s + 1) * MOST, 8 * width :] = terms.astype(BF)
        onehot = jnp.concatenate(rows, axis=0)
        for k in range(8):
            picked = lax.dot_general(onehot, feats[k][s], (((1,), (1,)), ((), ())), preferred_element_type=F32).astype(BF)
            for d in range(4):
                outs[d][s * MOST : (s + 1) * MOST, k * width : (k + 1) * width] = picked[d * MOST : (d + 1) * MOST]


def columns_kernel(pos, gate, up, out_a, out_b, held, sem):
    for flag, src in ((0, gate), (1, up)):

        @pl.when(pos[3] == flag)
        def _(src=src):
            copy = pltpu.make_async_copy(src.at[0], held, sem)
            copy.start()
            copy.wait()

    for r, out in enumerate((out_a, out_b)):
        for z in range(8):
            for t in range(2):
                first = z * 512 + t * 256 + r * 128
                out[z, :, t * 128 : (t + 1) * 128] = held[:, first : first + 128]


def expert_kernel(pos, *refs):
    xs, ws, out, wbuf = refs[:8], refs[8:13], refs[13], refs[14]
    y, c, xl, dp, z = (pos[i] for i in range(5))
    rows = xs[0].shape[0]
    width = 16 * ws[0].shape[1]
    for src, off, low in ((ws[0], 0, 0), (ws[1], 3, 0), (ws[2], 1, 0), (ws[3], 2, 0), (ws[4], 2, 4)):
        j = lax.rem(dp * 2 + xl + off, 4)
        for k in range(src.shape[0]):
            wbuf[lax.div(j, 2), lax.rem(low + k + 8 - z, 8), lax.rem(j, 2)] = src[k]
    for g in range(8):
        d, cc = g % 4, g // 4
        data = xs[g][:, :width]
        rw = jnp.sum(xs[g][:, width:].astype(F32), axis=1, keepdims=True)
        gate = jnp.dot(data, wbuf[0].reshape(width, 256), preferred_element_type=F32)
        up = jnp.dot(data, wbuf[1].reshape(width, 256), preferred_element_type=F32)
        act = (rw * (gate / (1.0 + jnp.exp(-gate)) * up)).astype(BF)
        for t in range(2):
            out[lax.rem(y + 4 - d, 4), c + cc - 2 * c * cc, t] = act[:, t * 128 : (t + 1) * 128]


def combine_kernel(meta, recv_a, recv_b, out):
    steps = meta.shape[0]
    for s in range(steps):
        own = meta[s]
        members = [((own[0:1] == e) | (own[1:2] == e)).astype(F32) for e in range(4)]
        rank = ranks(jnp.concatenate(members, axis=0))
        left, right = [], []
        for e in range(4):
            place = slots(rank[e : e + 1], members[e])
            left.append(jnp.concatenate([(place & (own[k : k + 1] == e)).astype(BF) for k in range(2)], axis=1))
            part = pl.ds((s % 2) * MOST, MOST)
            right.append(jnp.concatenate([r[e, h, s // 2, part] for h in range(2) for r in (recv_a, recv_b)], axis=1))
        picked = lax.dot_general(
            jnp.concatenate(left, axis=0), jnp.concatenate(right, axis=0), (((0,), (0,)), ((), ())), preferred_element_type=F32
        ).astype(BF)
        n = picked.shape[0] // 2
        out[s] = jnp.concatenate([picked[:n], picked[n:]], axis=1)


def body(tokens, expert_ids, route_weights, gate_train, up_train):
    barrier = lax.optimization_barrier
    dp, y, c, z, xl = (lax.axis_index(a) for a in ("dp", "y", "c", "z", "xl"))
    pos = jnp.stack([y, c, xl, dp, z]).astype(jnp.int32)
    steps, n, width = tokens.shape
    meta = jnp.concatenate([expert_ids.astype(F32), route_weights], axis=2).transpose(0, 2, 1)
    turned = tokens.transpose(0, 2, 1).reshape(2, steps // 2, width, n)
    mine = lax.dynamic_index_in_dim(turned, xl, 0, keepdims=False)
    theirs = lax.dynamic_index_in_dim(turned, 1 - xl, 0, keepdims=False)
    got = ring(theirs, "xl", 2, 1)
    pair = jnp.concatenate([jnp.where(xl == 0, mine, got), jnp.where(xl == 0, got, mine)], axis=1)
    rows, units = gate_train.shape[1:]
    wide = units // 32
    blocks = pl.pallas_call(
        columns_kernel,
        out_shape=[jax.ShapeDtypeStruct((8, rows, 2 * wide), BF)] * 2,
        in_specs=[SM, HBM, HBM],
        out_specs=[VM] * 2,
        scratch_shapes=[pltpu.VMEM((rows, units), BF), pltpu.SemaphoreType.DMA(())],
        compiler_params=pltpu.CompilerParams(vmem_limit_bytes=16 << 20),
        name="columns",
    )(pos, gate_train, up_train)

    def exchange(x):
        return lax.all_to_all(x, "z", split_axis=0, concat_axis=0, tiled=True)

    def spread(own):
        left, right = ring(own, X, 4, 1), ring(own, X, 4, -1)
        return [own, left, right, ring(left[:4], X, 4, 1), ring(right[4:], X, 4, -1)]

    below, above = [pair], [pair]
    for k in range(3):
        if k == 2:
            below[2], above[2], *blocks = barrier((below[2], above[2], *blocks))
        below.append(ring(below[-1], "z", 8, 1))
        above.append(ring(above[-1], "z", 8, -1))
    last = barrier((blocks[0], ring(below[3][:1], "z", 8, 1), ring(above[3][1:], "z", 8, -1)))
    opposite = jnp.concatenate(last[1:], axis=0)
    feats = [pair] + above[1:] + [opposite] + below[:0:-1]
    own_a = exchange(last[0])
    sent = pl.pallas_call(
        dispatch_kernel,
        out_shape=[jax.ShapeDtypeStruct((2 * MOST, 16 * width + 128), BF)] * 4,
        in_specs=[SM] + [VM] * 9,
        out_specs=[VM] * 4,
        compiler_params=pltpu.CompilerParams(vmem_limit_bytes=24 << 20),
        name="dispatch",
    )(pos, meta, *feats)
    held = [sent[0], ring(sent[1], "y", 4, 1), None, ring(sent[3], "y", 4, 3)]
    own_a, part_b, held[0], held[1], far_rows, held[3] = barrier((own_a, blocks[1], held[0], held[1], sent[2], held[3]))
    own_b = exchange(part_b)
    held[2] = ring(far_rows, "y", 4, 2)
    ws_a = spread(own_a)
    other = [ring(held[d], "c", 2, 1) if d != 2 else None for d in range(4)]
    own_b, held[2], ws_a[3], ws_a[4], other[0], other[1], other[3] = barrier(
        (own_b, held[2], ws_a[3], ws_a[4], other[0], other[1], other[3])
    )
    ws_b = spread(own_b)
    other[2] = ring(held[2], "c", 2, 1)
    pieces = [ws_a, ws_b]
    backs = []
    for ws in pieces:
        act = pl.pallas_call(
            expert_kernel,
            out_shape=jax.ShapeDtypeStruct((4, 2, 2, 2 * MOST, wide), BF),
            in_specs=[SM] + [VM] * 13,
            out_specs=VM,
            scratch_shapes=[pltpu.VMEM((2, 8, 2, rows, 2 * wide), BF)],
            compiler_params=pltpu.CompilerParams(vmem_limit_bytes=8 << 20),
            cost_estimate=pl.CostEstimate(
                flops=16 * MOST * 16 * width * 8 * wide, bytes_accessed=12 << 20, transcendentals=16 * MOST * 2 * wide
            ),
            name="expert",
        )(pos, *held, *other, *ws)
        back = lax.all_to_all(act.reshape(16, 2 * MOST, wide), ("y", "c", "xl"), split_axis=0, concat_axis=0, tiled=True)
        backs.append(back.reshape(4, 2, 2, 2 * MOST, wide))
    out = pl.pallas_call(
        combine_kernel,
        out_shape=jax.ShapeDtypeStruct((steps, n, 1024), BF),
        in_specs=[VM] * 3,
        out_specs=VM,
        compiler_params=pltpu.CompilerParams(vmem_limit_bytes=24 << 20),
        name="combine",
    )(meta, *backs)
    return out.reshape(steps, n, 2, 2, 256)


def solution(mesh):
    fine = Mesh(mesh.devices.reshape(2, 4, 2, 8, 2), ("dp", "y", "c", "z", "xl"))
    group, tensor = ("dp", "y", "c"), ("z", "xl")
    in_specs = (
        P(None, group, tensor),
        P(None, group, None),
        P(None, group, None),
        P(("y", "c"), tensor, None),
        P(("y", "c"), tensor, None),
    )
    out_specs = P(None, group, None, None, tensor)
    return jax.shard_map(body, mesh=fine, in_specs=in_specs, out_specs=out_specs, check_vma=False)
```

```python
import jax
import jax.numpy as jnp
from jax import lax
from jax.experimental import pallas as pl
from jax.experimental.pallas import tpu as pltpu
from jax.sharding import Mesh, PartitionSpec as P

MOST = 80
X = ("dp", "xl")
BF, F32 = jnp.bfloat16, jnp.float32
ANY = pl.BlockSpec(memory_space=pl.ANY)
VM = pl.BlockSpec(memory_space=pltpu.VMEM)
SM = pl.BlockSpec(memory_space=pltpu.SMEM)


def ring(x, axis, size, step):
    return lax.ppermute(x, axis, [(i, (i + step) % size) for i in range(size)])


def ranks(member):
    n = member.shape[1]
    before = lax.broadcasted_iota(jnp.int32, (n, n), 0) < lax.broadcasted_iota(jnp.int32, (n, n), 1)
    return jnp.dot(member.astype(BF), before.astype(BF), preferred_element_type=F32)


def slots(rank, member):
    row = lax.broadcasted_iota(jnp.int32, (MOST, rank.shape[1]), 0).astype(F32)
    return (row == rank) & (member > 0)


def dispatch_kernel(pos, meta, *refs):
    y, xl = pos[0], pos[2]
    feats, outs = refs[:8], refs[8:]
    ss, width, n = feats[0].shape
    lane = lax.broadcasted_iota(jnp.int32, (MOST, 128), 1)
    for s in range(ss):
        own = meta[2 * xl + s]
        rows = []
        members = []
        for d in range(4):
            e = lax.rem(y + d, 4).astype(F32)
            members.append(((own[0:1] == e) | (own[1:2] == e)).astype(F32))
        rank = ranks(jnp.concatenate(members, axis=0))
        for d in range(4):
            place = slots(rank[d : d + 1], members[d])
            rows.append(place.astype(BF))
            e = lax.rem(y + d, 4).astype(F32)
            weight = jnp.where(own[0:1] == e, own[2:3], own[3:4])
            whole = jnp.broadcast_to(jnp.sum(jnp.where(place, weight, 0.0), axis=1, keepdims=True), (MOST, 128))
            high = whole.astype(BF)
            rest = whole - high.astype(F32)
            mid = rest.astype(BF)
            low = (rest - mid.astype(F32)).astype(BF)
            terms = jnp.where(lane == 0, high.astype(F32), jnp.where(lane == 1, mid.astype(F32), jnp.where(lane == 2, low.astype(F32), 0.0)))
            outs[d][s * MOST : (s + 1) * MOST, 8 * width :] = terms.astype(BF)
        onehot = jnp.concatenate(rows, axis=0)
        for k in range(8):
            picked = lax.dot_general(onehot, feats[k][s], (((1,), (1,)), ((), ())), preferred_element_type=F32).astype(BF)
            for d in range(4):
                outs[d][s * MOST : (s + 1) * MOST, k * width : (k + 1) * width] = picked[d * MOST : (d + 1) * MOST]


def columns_kernel(pos, gate, up, out_a, out_b, held, sem):
    for flag, src in ((0, gate), (1, up)):

        @pl.when(pos[3] == flag)
        def _(src=src):
            copy = pltpu.make_async_copy(src.at[0], held, sem)
            copy.start()
            copy.wait()

    for r, out in enumerate((out_a, out_b)):
        for z in range(8):
            for t in range(2):
                first = z * 512 + t * 256 + r * 128
                out[z, :, t * 128 : (t + 1) * 128] = held[:, first : first + 128]


def expert_kernel(pos, *refs):
    xs, ws, (out, xbuf, wbuf, xsem, wsem) = refs[:8], refs[8:13], refs[13:]
    y, c, xl, dp, z = (pos[i] for i in range(5))
    width = 16 * ws[0].shape[1]
    copies = []
    for i, (src, off, low) in enumerate(((ws[0], 0, 0), (ws[1], 3, 0), (ws[2], 1, 0), (ws[3], 2, 0), (ws[4], 2, 4))):
        j = lax.rem(dp * 2 + xl + off, 4)
        for k in range(src.shape[0]):
            place = wbuf.at[lax.div(j, 2), lax.rem(low + k + 8 - z, 8), lax.rem(j, 2)]
            copies.append(pltpu.make_async_copy(src.at[k], place, wsem.at[i, k]))
    for cp in copies:
        cp.start()
    rows = [pltpu.make_async_copy(xs[g], xbuf.at[g], xsem.at[g]) for g in range(8)]
    for cp in rows:
        cp.start()
    for cp in copies:
        cp.wait()
    for g in range(8):
        d, cc = g % 4, g // 4
        rows[g].wait()
        rw = jnp.sum(xbuf[g, :, width:].astype(F32), axis=1, keepdims=True)
        gate = jnp.dot(xbuf[g, :, :width], wbuf[0].reshape(width, 256), preferred_element_type=F32)
        up = jnp.dot(xbuf[g, :, :width], wbuf[1].reshape(width, 256), preferred_element_type=F32)
        act = (rw * (gate / (1.0 + jnp.exp(-gate)) * up)).astype(BF)
        for t in range(2):
            out[lax.rem(y + 4 - d, 4), c + cc - 2 * c * cc, t] = act[:, t * 128 : (t + 1) * 128]


def combine_kernel(meta, recv_a, recv_b, out):
    steps = meta.shape[0]
    for s in range(steps):
        own = meta[s]
        members = [((own[0:1] == e) | (own[1:2] == e)).astype(F32) for e in range(4)]
        rank = ranks(jnp.concatenate(members, axis=0))
        left, right = [], []
        for e in range(4):
            place = slots(rank[e : e + 1], members[e])
            left.append(jnp.concatenate([(place & (own[k : k + 1] == e)).astype(BF) for k in range(2)], axis=1))
            part = pl.ds((s % 2) * MOST, MOST)
            right.append(jnp.concatenate([r[e, h, s // 2, part] for h in range(2) for r in (recv_a, recv_b)], axis=1))
        picked = lax.dot_general(
            jnp.concatenate(left, axis=0), jnp.concatenate(right, axis=0), (((0,), (0,)), ((), ())), preferred_element_type=F32
        ).astype(BF)
        n = picked.shape[0] // 2
        out[s] = jnp.concatenate([picked[:n], picked[n:]], axis=1)


def body(tokens, expert_ids, route_weights, gate_train, up_train):
    barrier = lax.optimization_barrier
    dp, y, c, z, xl = (lax.axis_index(a) for a in ("dp", "y", "c", "z", "xl"))
    pos = jnp.stack([y, c, xl, dp, z]).astype(jnp.int32)
    steps, n, width = tokens.shape
    meta = jnp.concatenate([expert_ids.astype(F32), route_weights], axis=2).transpose(0, 2, 1)
    turned = tokens.transpose(0, 2, 1).reshape(2, steps // 2, width, n)
    mine = lax.dynamic_index_in_dim(turned, xl, 0, keepdims=False)
    theirs = lax.dynamic_index_in_dim(turned, 1 - xl, 0, keepdims=False)
    got = ring(theirs, "xl", 2, 1)
    pair = jnp.concatenate([jnp.where(xl == 0, mine, got), jnp.where(xl == 0, got, mine)], axis=1)
    rows, units = gate_train.shape[1:]
    wide = units // 32
    blocks = pl.pallas_call(
        columns_kernel,
        out_shape=[jax.ShapeDtypeStruct((8, rows, 2 * wide), BF)] * 2,
        in_specs=[SM, ANY, ANY],
        out_specs=[VM] * 2,
        scratch_shapes=[pltpu.VMEM((rows, units), BF), pltpu.SemaphoreType.DMA(())],
        compiler_params=pltpu.CompilerParams(vmem_limit_bytes=58 << 20),
        name="columns",
    )(pos, gate_train, up_train)

    def exchange(x):
        return lax.all_to_all(x, "z", split_axis=0, concat_axis=0, tiled=True)

    def spread(own):
        left, right = ring(own, X, 4, 1), ring(own, X, 4, -1)
        return [own, left, right, ring(left[:4], X, 4, 1), ring(right[4:], X, 4, -1)]

    below, above = [pair], [pair]
    for k in range(3):
        if k == 2:
            below[2], above[2], *blocks = barrier((below[2], above[2], *blocks))
        below.append(ring(below[-1], "z", 8, 1))
        above.append(ring(above[-1], "z", 8, -1))
    last = barrier((blocks[0], ring(below[3][:1], "z", 8, 1), ring(above[3][1:], "z", 8, -1)))
    opposite = jnp.concatenate(last[1:], axis=0)
    feats = [pair] + above[1:] + [opposite] + below[:0:-1]
    own_a = exchange(last[0])
    sent = pl.pallas_call(
        dispatch_kernel,
        out_shape=[jax.ShapeDtypeStruct((2 * MOST, 16 * width + 128), BF)] * 4,
        in_specs=[SM] + [VM] * 9,
        out_specs=[VM] * 4,
        compiler_params=pltpu.CompilerParams(vmem_limit_bytes=24 << 20),
        name="dispatch",
    )(pos, meta, *feats)
    held = [sent[0], ring(sent[1], "y", 4, 1), None, ring(sent[3], "y", 4, 3)]
    ws_a = spread(own_a)
    part_b, ws_a[0], far_rows, held[1], held[3] = barrier((blocks[1], ws_a[0], sent[2], held[1], held[3]))
    own_b = exchange(part_b)
    held[2] = ring(far_rows, "y", 4, 2)
    own_b, held[2], ws_a[3], ws_a[4], held[0], held[1], held[3] = barrier(
        (own_b, held[2], ws_a[3], ws_a[4], held[0], held[1], held[3])
    )
    ws_b = spread(own_b)
    other = [ring(h, "c", 2, 1) for h in held]
    pieces = [ws_a, ws_b]
    backs = []
    for ws in pieces:
        act = pl.pallas_call(
            expert_kernel,
            out_shape=jax.ShapeDtypeStruct((4, 2, 2, 2 * MOST, wide), BF),
            in_specs=[SM] + [ANY] * 13,
            out_specs=VM,
            scratch_shapes=[
                pltpu.VMEM((8, 2 * MOST, 16 * width + 128), BF),
                pltpu.VMEM((2, 8, 2, rows, 2 * wide), BF),
                pltpu.SemaphoreType.DMA((8,)),
                pltpu.SemaphoreType.DMA((5, 8)),
            ],
            compiler_params=pltpu.CompilerParams(vmem_limit_bytes=58 << 20),
            cost_estimate=pl.CostEstimate(
                flops=16 * MOST * 16 * width * 8 * wide, bytes_accessed=12 << 20, transcendentals=16 * MOST * 2 * wide
            ),
            name="expert",
        )(pos, *held, *other, *ws)
        back = lax.all_to_all(act.reshape(16, 2 * MOST, wide), ("y", "c", "xl"), split_axis=0, concat_axis=0, tiled=True)
        backs.append(back.reshape(4, 2, 2, 2 * MOST, wide))
    out = pl.pallas_call(
        combine_kernel,
        out_shape=jax.ShapeDtypeStruct((steps, n, 1024), BF),
        in_specs=[VM] * 3,
        out_specs=VM,
        compiler_params=pltpu.CompilerParams(vmem_limit_bytes=24 << 20),
        name="combine",
    )(meta, *backs)
    return out.reshape(steps, n, 2, 2, 256)


def solution(mesh):
    fine = Mesh(mesh.devices.reshape(2, 4, 2, 8, 2), ("dp", "y", "c", "z", "xl"))
    group, tensor = ("dp", "y", "c"), ("z", "xl")
    in_specs = (
        P(None, group, tensor),
        P(None, group, None),
        P(None, group, None),
        P(("y", "c"), tensor, None),
        P(("y", "c"), tensor, None),
    )
    out_specs = P(None, group, None, None, tensor)
    return jax.shard_map(body, mesh=fine, in_specs=in_specs, out_specs=out_specs, check_vma=False)
```

```python
import jax
import jax.numpy as jnp
from jax import lax
from jax.experimental import pallas as pl
from jax.experimental.pallas import tpu as pltpu
from jax.sharding import Mesh, PartitionSpec as P

MOST = 80
X = ("dp", "xl")
BF, F32 = jnp.bfloat16, jnp.float32
ANY = pl.BlockSpec(memory_space=pl.ANY)
VM = pl.BlockSpec(memory_space=pltpu.VMEM)
SM = pl.BlockSpec(memory_space=pltpu.SMEM)


def ring(x, axis, size, step):
    return lax.ppermute(x, axis, [(i, (i + step) % size) for i in range(size)])


def ranks(member):
    n = member.shape[1]
    before = lax.broadcasted_iota(jnp.int32, (n, n), 0) < lax.broadcasted_iota(jnp.int32, (n, n), 1)
    return jnp.dot(member.astype(BF), before.astype(BF), preferred_element_type=F32)


def slots(rank, member):
    row = lax.broadcasted_iota(jnp.int32, (MOST, rank.shape[1]), 0).astype(F32)
    return (row == rank) & (member > 0)


def dispatch_kernel(pos, meta, *refs):
    y, xl = pos[0], pos[2]
    feats, outs = refs[:8], refs[8:]
    ss, width, n = feats[0].shape
    lane = lax.broadcasted_iota(jnp.int32, (MOST, 128), 1)
    for s in range(ss):
        own = meta[2 * xl + s]
        rows = []
        members = []
        for d in range(4):
            e = lax.rem(y + d, 4).astype(F32)
            members.append(((own[0:1] == e) | (own[1:2] == e)).astype(F32))
        rank = ranks(jnp.concatenate(members, axis=0))
        for d in range(4):
            place = slots(rank[d : d + 1], members[d])
            rows.append(place.astype(BF))
            e = lax.rem(y + d, 4).astype(F32)
            weight = jnp.where(own[0:1] == e, own[2:3], own[3:4])
            whole = jnp.broadcast_to(jnp.sum(jnp.where(place, weight, 0.0), axis=1, keepdims=True), (MOST, 128))
            high = whole.astype(BF)
            rest = whole - high.astype(F32)
            mid = rest.astype(BF)
            low = (rest - mid.astype(F32)).astype(BF)
            terms = jnp.where(lane == 0, high.astype(F32), jnp.where(lane == 1, mid.astype(F32), jnp.where(lane == 2, low.astype(F32), 0.0)))
            outs[d][s * MOST : (s + 1) * MOST, 8 * width :] = terms.astype(BF)
        onehot = jnp.concatenate(rows, axis=0)
        for k in range(8):
            picked = lax.dot_general(onehot, feats[k][s], (((1,), (1,)), ((), ())), preferred_element_type=F32).astype(BF)
            for d in range(4):
                outs[d][s * MOST : (s + 1) * MOST, k * width : (k + 1) * width] = picked[d * MOST : (d + 1) * MOST]


def columns_kernel(pos, gate, up, out_a, out_b, held, sem):
    for flag, src in ((0, gate), (1, up)):

        @pl.when(pos[3] == flag)
        def _(src=src):
            copy = pltpu.make_async_copy(src.at[0], held, sem)
            copy.start()
            copy.wait()

    for r, out in enumerate((out_a, out_b)):
        for z in range(8):
            for t in range(2):
                first = z * 512 + t * 256 + r * 128
                out[z, :, t * 128 : (t + 1) * 128] = held[:, first : first + 128]


def expert_kernel(pos, *refs):
    xs, ws, (out, xbuf, wbuf, xsem, wsem) = refs[:8], refs[8:13], refs[13:]
    y, c, xl, dp, z = (pos[i] for i in range(5))
    width = 16 * ws[0].shape[1]
    copies = []
    for i, (src, off, low) in enumerate(((ws[0], 0, 0), (ws[1], 3, 0), (ws[2], 1, 0), (ws[3], 2, 0), (ws[4], 2, 4))):
        j = lax.rem(dp * 2 + xl + off, 4)
        for k in range(src.shape[0]):
            place = wbuf.at[lax.div(j, 2), lax.rem(low + k + 8 - z, 8), lax.rem(j, 2)]
            copies.append(pltpu.make_async_copy(src.at[k], place, wsem.at[i, k]))
    rows = [pltpu.make_async_copy(xs[g], xbuf.at[g], xsem.at[g]) for g in range(8)]
    for cp in copies:
        cp.start()
    rows[0].start()
    for cp in copies:
        cp.wait()
    rows[1].start()
    for g in range(8):
        d, cc = g % 4, g // 4
        if g < 6:
            rows[g + 2].start()
        rows[g].wait()
        rw = jnp.sum(xbuf[g, :, width:].astype(F32), axis=1, keepdims=True)
        gate = jnp.dot(xbuf[g, :, :width], wbuf[0].reshape(width, 256), preferred_element_type=F32)
        up = jnp.dot(xbuf[g, :, :width], wbuf[1].reshape(width, 256), preferred_element_type=F32)
        act = (rw * (gate / (1.0 + jnp.exp(-gate)) * up)).astype(BF)
        for t in range(2):
            out[lax.rem(y + 4 - d, 4), c + cc - 2 * c * cc, t] = act[:, t * 128 : (t + 1) * 128]


def combine_kernel(meta, recv_a, recv_b, out):
    steps = meta.shape[0]
    for s in range(steps):
        own = meta[s]
        members = [((own[0:1] == e) | (own[1:2] == e)).astype(F32) for e in range(4)]
        rank = ranks(jnp.concatenate(members, axis=0))
        left, right = [], []
        for e in range(4):
            place = slots(rank[e : e + 1], members[e])
            left.append(jnp.concatenate([(place & (own[k : k + 1] == e)).astype(BF) for k in range(2)], axis=1))
            part = pl.ds((s % 2) * MOST, MOST)
            right.append(jnp.concatenate([r[e, h, s // 2, part] for h in range(2) for r in (recv_a, recv_b)], axis=1))
        picked = lax.dot_general(
            jnp.concatenate(left, axis=0), jnp.concatenate(right, axis=0), (((0,), (0,)), ((), ())), preferred_element_type=F32
        ).astype(BF)
        n = picked.shape[0] // 2
        out[s] = jnp.concatenate([picked[:n], picked[n:]], axis=1)


def body(tokens, expert_ids, route_weights, gate_train, up_train):
    barrier = lax.optimization_barrier
    dp, y, c, z, xl = (lax.axis_index(a) for a in ("dp", "y", "c", "z", "xl"))
    pos = jnp.stack([y, c, xl, dp, z]).astype(jnp.int32)
    steps, n, width = tokens.shape
    meta = jnp.concatenate([expert_ids.astype(F32), route_weights], axis=2).transpose(0, 2, 1)
    turned = tokens.transpose(0, 2, 1).reshape(2, steps // 2, width, n)
    mine = lax.dynamic_index_in_dim(turned, xl, 0, keepdims=False)
    theirs = lax.dynamic_index_in_dim(turned, 1 - xl, 0, keepdims=False)
    got = ring(theirs, "xl", 2, 1)
    pair = jnp.concatenate([jnp.where(xl == 0, mine, got), jnp.where(xl == 0, got, mine)], axis=1)
    rows, units = gate_train.shape[1:]
    wide = units // 32
    blocks = pl.pallas_call(
        columns_kernel,
        out_shape=[jax.ShapeDtypeStruct((8, rows, 2 * wide), BF)] * 2,
        in_specs=[SM, ANY, ANY],
        out_specs=[VM] * 2,
        scratch_shapes=[pltpu.VMEM((rows, units), BF), pltpu.SemaphoreType.DMA(())],
        compiler_params=pltpu.CompilerParams(vmem_limit_bytes=58 << 20),
        name="columns",
    )(pos, gate_train, up_train)

    def exchange(x):
        return lax.all_to_all(x, "z", split_axis=0, concat_axis=0, tiled=True)

    def spread(own):
        left, right = ring(own, X, 4, 1), ring(own, X, 4, -1)
        return [own, left, right, ring(left[:4], X, 4, 1), ring(right[4:], X, 4, -1)]

    own_a, pair = barrier((exchange(blocks[0]), pair))
    ws_a = spread(own_a)
    below, above = [pair], [pair]
    for k in range(3):
        below.append(ring(below[-1], "z", 8, 1))
        above.append(ring(above[-1], "z", 8, -1))
    *last, ws_a[1], ws_a[2] = barrier(
        (blocks[1], ring(below[3][:1], "z", 8, 1), ring(above[3][1:], "z", 8, -1), ws_a[1], ws_a[2])
    )
    opposite = jnp.concatenate(last[1:], axis=0)
    feats = [pair] + above[1:] + [opposite] + below[:0:-1]
    own_b = exchange(last[0])
    sent = pl.pallas_call(
        dispatch_kernel,
        out_shape=[jax.ShapeDtypeStruct((2 * MOST, 16 * width + 128), BF)] * 4,
        in_specs=[SM] + [VM] * 9,
        out_specs=[VM] * 4,
        compiler_params=pltpu.CompilerParams(vmem_limit_bytes=24 << 20),
        name="dispatch",
    )(pos, meta, *feats)
    held = [sent[0], ring(sent[1], "y", 4, 1), None, ring(sent[3], "y", 4, 3)]
    other = [ring(sent[0], "c", 2, 1)]
    held[0], far_rows, held[1], held[3], other[0], ws_a[3], ws_a[4] = barrier(
        (held[0], sent[2], held[1], held[3], other[0], ws_a[3], ws_a[4])
    )
    held[2] = ring(far_rows, "y", 4, 2)
    ws_b = spread(own_b)
    other += [ring(h, "c", 2, 1) for h in held[1:]]
    pieces = [ws_a, ws_b]
    backs = []
    for ws in pieces:
        act = pl.pallas_call(
            expert_kernel,
            out_shape=jax.ShapeDtypeStruct((4, 2, 2, 2 * MOST, wide), BF),
            in_specs=[SM] + [ANY] * 13,
            out_specs=VM,
            scratch_shapes=[
                pltpu.VMEM((8, 2 * MOST, 16 * width + 128), BF),
                pltpu.VMEM((2, 8, 2, rows, 2 * wide), BF),
                pltpu.SemaphoreType.DMA((8,)),
                pltpu.SemaphoreType.DMA((5, 8)),
            ],
            compiler_params=pltpu.CompilerParams(vmem_limit_bytes=58 << 20),
            cost_estimate=pl.CostEstimate(
                flops=16 * MOST * 16 * width * 8 * wide, bytes_accessed=12 << 20, transcendentals=16 * MOST * 2 * wide
            ),
            name="expert",
        )(pos, *held, *other, *ws)
        back = lax.all_to_all(act.reshape(16, 2 * MOST, wide), ("y", "c", "xl"), split_axis=0, concat_axis=0, tiled=True)
        backs.append(back.reshape(4, 2, 2, 2 * MOST, wide))
    out = pl.pallas_call(
        combine_kernel,
        out_shape=jax.ShapeDtypeStruct((steps, n, 1024), BF),
        in_specs=[VM] * 3,
        out_specs=VM,
        compiler_params=pltpu.CompilerParams(vmem_limit_bytes=24 << 20),
        name="combine",
    )(meta, *backs)
    return out.reshape(steps, n, 2, 2, 256)


def solution(mesh):
    fine = Mesh(mesh.devices.reshape(2, 4, 2, 8, 2), ("dp", "y", "c", "z", "xl"))
    group, tensor = ("dp", "y", "c"), ("z", "xl")
    in_specs = (
        P(None, group, tensor),
        P(None, group, None),
        P(None, group, None),
        P(("y", "c"), tensor, None),
        P(("y", "c"), tensor, None),
    )
    out_specs = P(None, group, None, None, tensor)
    return jax.shard_map(body, mesh=fine, in_specs=in_specs, out_specs=out_specs, check_vma=False)
```

```python
import jax
import jax.numpy as jnp
from jax import lax
from jax.experimental import pallas as pl
from jax.experimental.pallas import tpu as pltpu
from jax.sharding import Mesh, PartitionSpec as P

MOST = 80
X = ("dp", "xl")
BF, F32 = jnp.bfloat16, jnp.float32
ANY = pl.BlockSpec(memory_space=pl.ANY)
VM = pl.BlockSpec(memory_space=pltpu.VMEM)
SM = pl.BlockSpec(memory_space=pltpu.SMEM)


def ring(x, axis, size, step):
    return lax.ppermute(x, axis, [(i, (i + step) % size) for i in range(size)])


def ranks(member):
    n = member.shape[1]
    before = lax.broadcasted_iota(jnp.int32, (n, n), 0) < lax.broadcasted_iota(jnp.int32, (n, n), 1)
    return jnp.dot(member.astype(BF), before.astype(BF), preferred_element_type=F32)


def slots(rank, member):
    row = lax.broadcasted_iota(jnp.int32, (MOST, rank.shape[1]), 0).astype(F32)
    return (row == rank) & (member > 0)


def dispatch_kernel(pos, meta, *refs):
    y, xl = pos[0], pos[2]
    feats, outs = refs[:8], refs[8:]
    ss, width, n = feats[0].shape
    lane = lax.broadcasted_iota(jnp.int32, (MOST, 128), 1)
    for s in range(ss):
        own = meta[2 * xl + s]
        rows = []
        members = []
        for d in range(4):
            e = lax.rem(y + d, 4).astype(F32)
            members.append(((own[0:1] == e) | (own[1:2] == e)).astype(F32))
        rank = ranks(jnp.concatenate(members, axis=0))
        for d in range(4):
            place = slots(rank[d : d + 1], members[d])
            rows.append(place.astype(BF))
            e = lax.rem(y + d, 4).astype(F32)
            weight = jnp.where(own[0:1] == e, own[2:3], own[3:4])
            whole = jnp.broadcast_to(jnp.sum(jnp.where(place, weight, 0.0), axis=1, keepdims=True), (MOST, 128))
            high = whole.astype(BF)
            rest = whole - high.astype(F32)
            mid = rest.astype(BF)
            low = (rest - mid.astype(F32)).astype(BF)
            terms = jnp.where(lane == 0, high.astype(F32), jnp.where(lane == 1, mid.astype(F32), jnp.where(lane == 2, low.astype(F32), 0.0)))
            outs[d][s * MOST : (s + 1) * MOST, 8 * width :] = terms.astype(BF)
        onehot = jnp.concatenate(rows, axis=0)
        for k in range(8):
            picked = lax.dot_general(onehot, feats[k][s], (((1,), (1,)), ((), ())), preferred_element_type=F32).astype(BF)
            for d in range(4):
                outs[d][s * MOST : (s + 1) * MOST, k * width : (k + 1) * width] = picked[d * MOST : (d + 1) * MOST]


def columns_kernel(pos, gate, up, out_a, out_b, held, sem):
    for flag, src in ((0, gate), (1, up)):

        @pl.when(pos[3] == flag)
        def _(src=src):
            copy = pltpu.make_async_copy(src.at[0], held, sem)
            copy.start()
            copy.wait()

    for r, out in enumerate((out_a, out_b)):
        for z in range(8):
            for t in range(2):
                first = z * 512 + t * 256 + r * 128
                out[z, :, t * 128 : (t + 1) * 128] = held[:, first : first + 128]


def expert_kernel(pos, *refs):
    xs, ws, (out, xbuf, wbuf, xsem, wsem) = refs[:8], refs[8:13], refs[13:]
    y, c, xl, dp, z = (pos[i] for i in range(5))
    width = 16 * ws[0].shape[1]
    copies = []
    for i, (src, off, low) in enumerate(((ws[0], 0, 0), (ws[1], 3, 0), (ws[2], 1, 0), (ws[3], 2, 0), (ws[4], 2, 4))):
        j = lax.rem(dp * 2 + xl + off, 4)
        for k in range(src.shape[0]):
            place = wbuf.at[lax.div(j, 2), lax.rem(low + k + 8 - z, 8), lax.rem(j, 2)]
            copies.append(pltpu.make_async_copy(src.at[k], place, wsem.at[i, k]))
    rows = [pltpu.make_async_copy(xs[g], xbuf.at[g], xsem.at[g]) for g in range(8)]
    for cp in copies:
        cp.start()
    rows[0].start()
    for cp in copies:
        cp.wait()
    rows[1].start()
    for g in range(8):
        d, cc = g % 4, g // 4
        if g < 6:
            rows[g + 2].start()
        rows[g].wait()
        rw = jnp.sum(xbuf[g, :, width:].astype(F32), axis=1, keepdims=True)
        gate = jnp.dot(xbuf[g, :, :width], wbuf[0].reshape(width, 256), preferred_element_type=F32)
        up = jnp.dot(xbuf[g, :, :width], wbuf[1].reshape(width, 256), preferred_element_type=F32)
        act = (rw * (gate / (1.0 + jnp.exp(-gate)) * up)).astype(BF)
        for t in range(2):
            out[lax.rem(y + 4 - d, 4), c + cc - 2 * c * cc, t] = act[:, t * 128 : (t + 1) * 128]


def combine_kernel(meta, recv_a, recv_b, out):
    steps = meta.shape[0]
    for s in range(steps):
        own = meta[s]
        members = [((own[0:1] == e) | (own[1:2] == e)).astype(F32) for e in range(4)]
        rank = ranks(jnp.concatenate(members, axis=0))
        left, right = [], []
        for e in range(4):
            place = slots(rank[e : e + 1], members[e])
            left.append(jnp.concatenate([(place & (own[k : k + 1] == e)).astype(BF) for k in range(2)], axis=1))
            part = pl.ds((s % 2) * MOST, MOST)
            right.append(jnp.concatenate([r[e, h, s // 2, part] for h in range(2) for r in (recv_a, recv_b)], axis=1))
        picked = lax.dot_general(
            jnp.concatenate(left, axis=0), jnp.concatenate(right, axis=0), (((0,), (0,)), ((), ())), preferred_element_type=F32
        ).astype(BF)
        n = picked.shape[0] // 2
        out[s] = jnp.concatenate([picked[:n], picked[n:]], axis=1)


def body(tokens, expert_ids, route_weights, gate_train, up_train):
    barrier = lax.optimization_barrier
    dp, y, c, z, xl = (lax.axis_index(a) for a in ("dp", "y", "c", "z", "xl"))
    pos = jnp.stack([y, c, xl, dp, z]).astype(jnp.int32)
    steps, n, width = tokens.shape
    meta = jnp.concatenate([expert_ids.astype(F32), route_weights], axis=2).transpose(0, 2, 1)
    turned = tokens.transpose(0, 2, 1).reshape(2, steps // 2, width, n)
    mine = lax.dynamic_index_in_dim(turned, xl, 0, keepdims=False)
    theirs = lax.dynamic_index_in_dim(turned, 1 - xl, 0, keepdims=False)
    got = ring(theirs, "xl", 2, 1)
    pair = jnp.concatenate([jnp.where(xl == 0, mine, got), jnp.where(xl == 0, got, mine)], axis=1)
    rows, units = gate_train.shape[1:]
    wide = units // 32
    blocks = pl.pallas_call(
        columns_kernel,
        out_shape=[jax.ShapeDtypeStruct((8, rows, 2 * wide), BF)] * 2,
        in_specs=[SM, ANY, ANY],
        out_specs=[VM] * 2,
        scratch_shapes=[pltpu.VMEM((rows, units), BF), pltpu.SemaphoreType.DMA(())],
        compiler_params=pltpu.CompilerParams(vmem_limit_bytes=58 << 20),
        name="columns",
    )(pos, gate_train, up_train)

    def exchange(x):
        return lax.all_to_all(x, "z", split_axis=0, concat_axis=0, tiled=True)

    def spread(own):
        left, right = ring(own, X, 4, 1), ring(own, X, 4, -1)
        return [own, left, right, ring(left[:4], X, 4, 1), ring(right[4:], X, 4, -1)]

    own_a, pair = barrier((exchange(blocks[0]), pair))
    ws_a = spread(own_a)
    below, above = [pair], [pair]
    for k in range(3):
        below.append(ring(below[-1], "z", 8, 1))
        above.append(ring(above[-1], "z", 8, -1))
    *last, ws_a[1], ws_a[2] = barrier(
        (blocks[1], ring(below[3][:1], "z", 8, 1), ring(above[3][1:], "z", 8, -1), ws_a[1], ws_a[2])
    )
    opposite = jnp.concatenate(last[1:], axis=0)
    feats = [pair] + above[1:] + [opposite] + below[:0:-1]
    own_b = exchange(last[0])
    sent = pl.pallas_call(
        dispatch_kernel,
        out_shape=[jax.ShapeDtypeStruct((2 * MOST, 16 * width + 128), BF)] * 4,
        in_specs=[SM] + [VM] * 9,
        out_specs=[VM] * 4,
        compiler_params=pltpu.CompilerParams(vmem_limit_bytes=24 << 20),
        name="dispatch",
    )(pos, meta, *feats)
    held = [sent[0], ring(sent[1], "y", 4, 1), None, ring(sent[3], "y", 4, 3)]
    other = [ring(sent[0], "c", 2, 1)]
    held[0], far_rows, held[1], held[3], other[0], ws_a[3], ws_a[4], own_b = barrier(
        (held[0], sent[2], held[1], held[3], other[0], ws_a[3], ws_a[4], own_b)
    )
    held[2] = ring(far_rows, "y", 4, 2)
    ws_b = spread(own_b)
    other += [ring(h, "c", 2, 1) for h in held[1:]]
    pieces = [ws_a, ws_b]
    backs = []
    for ws in pieces:
        act = pl.pallas_call(
            expert_kernel,
            out_shape=jax.ShapeDtypeStruct((4, 2, 2, 2 * MOST, wide), BF),
            in_specs=[SM] + [ANY] * 13,
            out_specs=VM,
            scratch_shapes=[
                pltpu.VMEM((8, 2 * MOST, 16 * width + 128), BF),
                pltpu.VMEM((2, 8, 2, rows, 2 * wide), BF),
                pltpu.SemaphoreType.DMA((8,)),
                pltpu.SemaphoreType.DMA((5, 8)),
            ],
            compiler_params=pltpu.CompilerParams(vmem_limit_bytes=58 << 20),
            cost_estimate=pl.CostEstimate(
                flops=16 * MOST * 16 * width * 8 * wide, bytes_accessed=12 << 20, transcendentals=16 * MOST * 2 * wide
            ),
            name="expert",
        )(pos, *held, *other, *ws)
        back = lax.all_to_all(act.reshape(16, 2 * MOST, wide), ("y", "c", "xl"), split_axis=0, concat_axis=0, tiled=True)
        backs.append(back.reshape(4, 2, 2, 2 * MOST, wide))
    out = pl.pallas_call(
        combine_kernel,
        out_shape=jax.ShapeDtypeStruct((steps, n, 1024), BF),
        in_specs=[VM] * 3,
        out_specs=VM,
        compiler_params=pltpu.CompilerParams(vmem_limit_bytes=24 << 20),
        name="combine",
    )(meta, *backs)
    return out.reshape(steps, n, 2, 2, 256)


def solution(mesh):
    fine = Mesh(mesh.devices.reshape(2, 4, 2, 8, 2), ("dp", "y", "c", "z", "xl"))
    group, tensor = ("dp", "y", "c"), ("z", "xl")
    in_specs = (
        P(None, group, tensor),
        P(None, group, None),
        P(None, group, None),
        P(("y", "c"), tensor, None),
        P(("y", "c"), tensor, None),
    )
    out_specs = P(None, group, None, None, tensor)
    return jax.shard_map(body, mesh=fine, in_specs=in_specs, out_specs=out_specs, check_vma=False)
```

```python
import jax
import jax.numpy as jnp
from jax import lax
from jax.experimental import pallas as pl
from jax.experimental.pallas import tpu as pltpu
from jax.sharding import Mesh, PartitionSpec as P

MOST = 80
X = ("dp", "xl")
BF, F32 = jnp.bfloat16, jnp.float32
ANY = pl.BlockSpec(memory_space=pl.ANY)
VM = pl.BlockSpec(memory_space=pltpu.VMEM)
SM = pl.BlockSpec(memory_space=pltpu.SMEM)


def ring(x, axis, size, step):
    return lax.ppermute(x, axis, [(i, (i + step) % size) for i in range(size)])


def ranks(member):
    n = member.shape[1]
    before = lax.broadcasted_iota(jnp.int32, (n, n), 0) < lax.broadcasted_iota(jnp.int32, (n, n), 1)
    return jnp.dot(member.astype(BF), before.astype(BF), preferred_element_type=F32)


def slots(rank, member):
    row = lax.broadcasted_iota(jnp.int32, (MOST, rank.shape[1]), 0).astype(F32)
    return (row == rank) & (member > 0)


def dispatch_kernel(pos, meta, *refs):
    y, xl = pos[0], pos[2]
    feats, outs = refs[:8], refs[8:]
    ss, width, n = feats[0].shape
    lane = lax.broadcasted_iota(jnp.int32, (MOST, 128), 1)
    for s in range(ss):
        own = meta[2 * xl + s]
        rows = []
        members = []
        for d in range(4):
            e = lax.rem(y + d, 4).astype(F32)
            members.append(((own[0:1] == e) | (own[1:2] == e)).astype(F32))
        rank = ranks(jnp.concatenate(members, axis=0))
        for d in range(4):
            place = slots(rank[d : d + 1], members[d])
            rows.append(place.astype(BF))
            e = lax.rem(y + d, 4).astype(F32)
            weight = jnp.where(own[0:1] == e, own[2:3], own[3:4])
            whole = jnp.broadcast_to(jnp.sum(jnp.where(place, weight, 0.0), axis=1, keepdims=True), (MOST, 128))
            high = whole.astype(BF)
            rest = whole - high.astype(F32)
            mid = rest.astype(BF)
            low = (rest - mid.astype(F32)).astype(BF)
            terms = jnp.where(lane == 0, high.astype(F32), jnp.where(lane == 1, mid.astype(F32), jnp.where(lane == 2, low.astype(F32), 0.0)))
            outs[d][s * MOST : (s + 1) * MOST, 8 * width :] = terms.astype(BF)
        onehot = jnp.concatenate(rows, axis=0)
        for k in range(8):
            picked = lax.dot_general(onehot, feats[k][s], (((1,), (1,)), ((), ())), preferred_element_type=F32).astype(BF)
            for d in range(4):
                outs[d][s * MOST : (s + 1) * MOST, k * width : (k + 1) * width] = picked[d * MOST : (d + 1) * MOST]


def columns_kernel(pos, gate, up, out_a, out_b, held, sem):
    for flag, src in ((0, gate), (1, up)):

        @pl.when(pos[3] == flag)
        def _(src=src):
            copy = pltpu.make_async_copy(src.at[0], held, sem)
            copy.start()
            copy.wait()

    for r, out in enumerate((out_a, out_b)):
        for z in range(8):
            for t in range(2):
                first = z * 512 + t * 256 + r * 128
                out[z, :, t * 128 : (t + 1) * 128] = held[:, first : first + 128]


def expert_kernel(pos, *refs):
    xs, ws, (out, xbuf, wbuf, xsem, wsem) = refs[:8], refs[8:13], refs[13:]
    y, c, xl, dp, z = (pos[i] for i in range(5))
    width = 16 * ws[0].shape[1]
    copies = []
    for i, (src, off, low) in enumerate(((ws[0], 0, 0), (ws[1], 3, 0), (ws[2], 1, 0), (ws[3], 2, 0), (ws[4], 2, 4))):
        j = lax.rem(dp * 2 + xl + off, 4)
        for k in range(src.shape[0]):
            place = wbuf.at[lax.div(j, 2), lax.rem(low + k + 8 - z, 8), lax.rem(j, 2)]
            copies.append(pltpu.make_async_copy(src.at[k], place, wsem.at[i, k]))
    rows = [pltpu.make_async_copy(xs[g], xbuf.at[g], xsem.at[g]) for g in range(8)]
    for cp in copies:
        cp.start()
    rows[0].start()
    for cp in copies:
        cp.wait()
    rows[1].start()
    for g in range(8):
        d, cc = g % 4, g // 4
        if g < 6:
            rows[g + 2].start()
        rows[g].wait()
        rw = jnp.sum(xbuf[g, :, width:].astype(F32), axis=1, keepdims=True)
        gate = jnp.dot(xbuf[g, :, :width], wbuf[0].reshape(width, 256), preferred_element_type=F32)
        up = jnp.dot(xbuf[g, :, :width], wbuf[1].reshape(width, 256), preferred_element_type=F32)
        act = (rw * (gate / (1.0 + jnp.exp(-gate)) * up)).astype(BF)
        for t in range(2):
            out[lax.rem(y + 4 - d, 4), c + cc - 2 * c * cc, t] = act[:, t * 128 : (t + 1) * 128]


def combine_kernel(meta, recv_a, recv_b, out):
    steps = meta.shape[0]
    for s in range(steps):
        own = meta[s]
        members = [((own[0:1] == e) | (own[1:2] == e)).astype(F32) for e in range(4)]
        rank = ranks(jnp.concatenate(members, axis=0))
        left, right = [], []
        for e in range(4):
            place = slots(rank[e : e + 1], members[e])
            left.append(jnp.concatenate([(place & (own[k : k + 1] == e)).astype(BF) for k in range(2)], axis=1))
            part = pl.ds((s % 2) * MOST, MOST)
            right.append(jnp.concatenate([r[e, h, s // 2, part] for h in range(2) for r in (recv_a, recv_b)], axis=1))
        picked = lax.dot_general(
            jnp.concatenate(left, axis=0), jnp.concatenate(right, axis=0), (((0,), (0,)), ((), ())), preferred_element_type=F32
        ).astype(BF)
        n = picked.shape[0] // 2
        out[s] = jnp.concatenate([picked[:n], picked[n:]], axis=1)


def body(tokens, expert_ids, route_weights, gate_train, up_train):
    barrier = lax.optimization_barrier
    dp, y, c, z, xl = (lax.axis_index(a) for a in ("dp", "y", "c", "z", "xl"))
    pos = jnp.stack([y, c, xl, dp, z]).astype(jnp.int32)
    steps, n, width = tokens.shape
    meta = jnp.concatenate([expert_ids.astype(F32), route_weights], axis=2).transpose(0, 2, 1)
    turned = tokens.transpose(0, 2, 1).reshape(2, steps // 2, width, n)
    mine = lax.dynamic_index_in_dim(turned, xl, 0, keepdims=False)
    theirs = lax.dynamic_index_in_dim(turned, 1 - xl, 0, keepdims=False)
    got = ring(theirs, "xl", 2, 1)
    pair = jnp.concatenate([jnp.where(xl == 0, mine, got), jnp.where(xl == 0, got, mine)], axis=1)
    rows, units = gate_train.shape[1:]
    wide = units // 32
    blocks = pl.pallas_call(
        columns_kernel,
        out_shape=[jax.ShapeDtypeStruct((8, rows, 2 * wide), BF)] * 2,
        in_specs=[SM, ANY, ANY],
        out_specs=[VM] * 2,
        scratch_shapes=[pltpu.VMEM((rows, units), BF), pltpu.SemaphoreType.DMA(())],
        compiler_params=pltpu.CompilerParams(vmem_limit_bytes=58 << 20),
        name="columns",
    )(pos, gate_train, up_train)

    def exchange(x):
        return lax.all_to_all(x, "z", split_axis=0, concat_axis=0, tiled=True)

    def sides(own):
        return ring(own, X, 4, 1), ring(own, X, 4, -1)

    def far(left, right):
        return ring(left[:4], X, 4, 1), ring(right[4:], X, 4, -1)

    below, above = [pair], [pair]
    for k in range(3):
        below.append(ring(below[-1], "z", 8, 1))
        above.append(ring(above[-1], "z", 8, -1))
    part_a, below[3], above[3] = barrier((blocks[0], below[3], above[3]))
    own_a = exchange(part_a)
    opposite = jnp.concatenate([ring(below[3][:1], "z", 8, 1), ring(above[3][1:], "z", 8, -1)], axis=0)
    feats = [pair] + above[1:] + [opposite] + below[:0:-1]
    sent = pl.pallas_call(
        dispatch_kernel,
        out_shape=[jax.ShapeDtypeStruct((2 * MOST, 16 * width + 128), BF)] * 4,
        in_specs=[SM] + [VM] * 9,
        out_specs=[VM] * 4,
        compiler_params=pltpu.CompilerParams(vmem_limit_bytes=24 << 20),
        name="dispatch",
    )(pos, meta, *feats)
    near = ring(sent[1], "y", 4, 1), ring(sent[3], "y", 4, 3)
    part_b, own_a = barrier((blocks[1], own_a))
    own_b = exchange(part_b)
    left_a, right_a = sides(own_a)
    far_rows, *near = barrier((sent[2], *near))
    held = [sent[0], near[0], ring(far_rows, "y", 4, 2), near[1]]
    own_b, left_a, right_a, *held = barrier((own_b, left_a, right_a, *held))
    far_a = far(left_a, right_a)
    other = [ring(h, "c", 2, 1) for h in held]
    own_b, *far_a = barrier((own_b, *far_a))
    left_b, right_b = sides(own_b)

    def expert(*ws):
        return pl.pallas_call(
            expert_kernel,
            out_shape=jax.ShapeDtypeStruct((4, 2, 2, 2 * MOST, wide), BF),
            in_specs=[SM] + [ANY] * 13,
            out_specs=VM,
            scratch_shapes=[
                pltpu.VMEM((8, 2 * MOST, 16 * width + 128), BF),
                pltpu.VMEM((2, 8, 2, rows, 2 * wide), BF),
                pltpu.SemaphoreType.DMA((8,)),
                pltpu.SemaphoreType.DMA((5, 8)),
            ],
            compiler_params=pltpu.CompilerParams(vmem_limit_bytes=58 << 20),
            cost_estimate=pl.CostEstimate(
                flops=16 * MOST * 16 * width * 8 * wide, bytes_accessed=12 << 20, transcendentals=16 * MOST * 2 * wide
            ),
            name="expert",
        )(pos, *held, *other, *ws)

    def give_back(act):
        back = lax.all_to_all(act.reshape(16, 2 * MOST, wide), ("y", "c", "xl"), split_axis=0, concat_axis=0, tiled=True)
        return back.reshape(4, 2, 2, 2 * MOST, wide)

    act_a = expert(own_a, left_a, right_a, *far_a)
    left_b, right_b, act_a = barrier((left_b, right_b, act_a))
    back_a = give_back(act_a)
    back_b = give_back(expert(own_b, left_b, right_b, *far(left_b, right_b)))
    out = pl.pallas_call(
        combine_kernel,
        out_shape=jax.ShapeDtypeStruct((steps, n, 1024), BF),
        in_specs=[VM] * 3,
        out_specs=VM,
        compiler_params=pltpu.CompilerParams(vmem_limit_bytes=24 << 20),
        name="combine",
    )(meta, back_a, back_b)
    return out.reshape(steps, n, 2, 2, 256)


def solution(mesh):
    fine = Mesh(mesh.devices.reshape(2, 4, 2, 8, 2), ("dp", "y", "c", "z", "xl"))
    group, tensor = ("dp", "y", "c"), ("z", "xl")
    in_specs = (
        P(None, group, tensor),
        P(None, group, None),
        P(None, group, None),
        P(("y", "c"), tensor, None),
        P(("y", "c"), tensor, None),
    )
    out_specs = P(None, group, None, None, tensor)
    return jax.shard_map(body, mesh=fine, in_specs=in_specs, out_specs=out_specs, check_vma=False)
```

```python
import jax
import jax.numpy as jnp
from jax import lax
from jax.experimental import pallas as pl
from jax.experimental.pallas import tpu as pltpu
from jax.sharding import Mesh, PartitionSpec as P

MOST = 80
X = ("dp", "xl")
BF, F32 = jnp.bfloat16, jnp.float32
ANY = pl.BlockSpec(memory_space=pl.ANY)
VM = pl.BlockSpec(memory_space=pltpu.VMEM)
SM = pl.BlockSpec(memory_space=pltpu.SMEM)


def ring(x, axis, size, step):
    return lax.ppermute(x, axis, [(i, (i + step) % size) for i in range(size)])


def ranks(member):
    n = member.shape[1]
    before = lax.broadcasted_iota(jnp.int32, (n, n), 0) < lax.broadcasted_iota(jnp.int32, (n, n), 1)
    return jnp.dot(member.astype(BF), before.astype(BF), preferred_element_type=F32)


def slots(rank, member):
    row = lax.broadcasted_iota(jnp.int32, (MOST, rank.shape[1]), 0).astype(F32)
    return (row == rank) & (member > 0)


def dispatch_kernel(pos, meta, *refs):
    y, xl = pos[0], pos[2]
    feats, outs = refs[:8], refs[8:]
    ss, width, n = feats[0].shape
    lane = lax.broadcasted_iota(jnp.int32, (MOST, 128), 1)
    for s in range(ss):
        own = meta[2 * xl + s]
        rows = []
        members = []
        for d in range(4):
            e = lax.rem(y + d, 4).astype(F32)
            members.append(((own[0:1] == e) | (own[1:2] == e)).astype(F32))
        rank = ranks(jnp.concatenate(members, axis=0))
        for d in range(4):
            place = slots(rank[d : d + 1], members[d])
            rows.append(place.astype(BF))
            e = lax.rem(y + d, 4).astype(F32)
            weight = jnp.where(own[0:1] == e, own[2:3], own[3:4])
            whole = jnp.broadcast_to(jnp.sum(jnp.where(place, weight, 0.0), axis=1, keepdims=True), (MOST, 128))
            high = whole.astype(BF)
            rest = whole - high.astype(F32)
            mid = rest.astype(BF)
            low = (rest - mid.astype(F32)).astype(BF)
            terms = jnp.where(lane == 0, high.astype(F32), jnp.where(lane == 1, mid.astype(F32), jnp.where(lane == 2, low.astype(F32), 0.0)))
            outs[d][s * MOST : (s + 1) * MOST, 8 * width :] = terms.astype(BF)
        onehot = jnp.concatenate(rows, axis=0)
        for k in range(8):
            picked = lax.dot_general(onehot, feats[k][s], (((1,), (1,)), ((), ())), preferred_element_type=F32).astype(BF)
            for d in range(4):
                outs[d][s * MOST : (s + 1) * MOST, k * width : (k + 1) * width] = picked[d * MOST : (d + 1) * MOST]


def columns_kernel(pos, gate, up, out_a, out_b, held, sem):
    for flag, src in ((0, gate), (1, up)):

        @pl.when(pos[3] == flag)
        def _(src=src):
            copy = pltpu.make_async_copy(src.at[0], held, sem)
            copy.start()
            copy.wait()

    for r, out in enumerate((out_a, out_b)):
        for z in range(8):
            for t in range(2):
                first = z * 512 + t * 256 + r * 128
                out[z, :, t * 128 : (t + 1) * 128] = held[:, first : first + 128]


def expert_kernel(pos, *refs):
    xs, ws, (out, xbuf, wbuf, xsem, wsem) = refs[:8], refs[8:13], refs[13:]
    y, c, xl, dp, z = (pos[i] for i in range(5))
    width = 16 * ws[0].shape[1]
    copies = []
    for i, (src, off, low) in enumerate(((ws[0], 0, 0), (ws[1], 3, 0), (ws[2], 1, 0), (ws[3], 2, 0), (ws[4], 2, 4))):
        j = lax.rem(dp * 2 + xl + off, 4)
        for k in range(src.shape[0]):
            place = wbuf.at[lax.div(j, 2), lax.rem(low + k + 8 - z, 8), lax.rem(j, 2)]
            copies.append(pltpu.make_async_copy(src.at[k], place, wsem.at[i, k]))
    rows = [pltpu.make_async_copy(xs[g], xbuf.at[g], xsem.at[g]) for g in range(8)]
    for cp in copies:
        cp.start()
    rows[0].start()
    for cp in copies:
        cp.wait()
    rows[1].start()
    for g in range(8):
        d, cc = g % 4, g // 4
        if g < 6:
            rows[g + 2].start()
        rows[g].wait()
        rw = jnp.sum(xbuf[g, :, width:].astype(F32), axis=1, keepdims=True)
        gate = jnp.dot(xbuf[g, :, :width], wbuf[0].reshape(width, 256), preferred_element_type=F32)
        up = jnp.dot(xbuf[g, :, :width], wbuf[1].reshape(width, 256), preferred_element_type=F32)
        act = (rw * (gate / (1.0 + jnp.exp(-gate)) * up)).astype(BF)
        for t in range(2):
            out[lax.rem(y + 4 - d, 4), c + cc - 2 * c * cc, t] = act[:, t * 128 : (t + 1) * 128]


def combine_kernel(meta, recv_a, recv_b, out):
    steps = meta.shape[0]
    for s in range(steps):
        own = meta[s]
        members = [((own[0:1] == e) | (own[1:2] == e)).astype(F32) for e in range(4)]
        rank = ranks(jnp.concatenate(members, axis=0))
        left, right = [], []
        for e in range(4):
            place = slots(rank[e : e + 1], members[e])
            left.append(jnp.concatenate([(place & (own[k : k + 1] == e)).astype(BF) for k in range(2)], axis=1))
            part = pl.ds((s % 2) * MOST, MOST)
            right.append(jnp.concatenate([r[e, h, s // 2, part] for h in range(2) for r in (recv_a, recv_b)], axis=1))
        picked = lax.dot_general(
            jnp.concatenate(left, axis=0), jnp.concatenate(right, axis=0), (((0,), (0,)), ((), ())), preferred_element_type=F32
        ).astype(BF)
        n = picked.shape[0] // 2
        out[s] = jnp.concatenate([picked[:n], picked[n:]], axis=1)


def body(tokens, expert_ids, route_weights, gate_train, up_train):
    barrier = lax.optimization_barrier
    dp, y, c, z, xl = (lax.axis_index(a) for a in ("dp", "y", "c", "z", "xl"))
    pos = jnp.stack([y, c, xl, dp, z]).astype(jnp.int32)
    steps, n, width = tokens.shape
    meta = jnp.concatenate([expert_ids.astype(F32), route_weights], axis=2).transpose(0, 2, 1)
    turned = tokens.transpose(0, 2, 1).reshape(2, steps // 2, width, n)
    mine = lax.dynamic_index_in_dim(turned, xl, 0, keepdims=False)
    theirs = lax.dynamic_index_in_dim(turned, 1 - xl, 0, keepdims=False)
    got = ring(theirs, "xl", 2, 1)
    pair = jnp.concatenate([jnp.where(xl == 0, mine, got), jnp.where(xl == 0, got, mine)], axis=1)
    rows, units = gate_train.shape[1:]
    wide = units // 32
    blocks = pl.pallas_call(
        columns_kernel,
        out_shape=[jax.ShapeDtypeStruct((8, rows, 2 * wide), BF)] * 2,
        in_specs=[SM, ANY, ANY],
        out_specs=[VM] * 2,
        scratch_shapes=[pltpu.VMEM((rows, units), BF), pltpu.SemaphoreType.DMA(())],
        compiler_params=pltpu.CompilerParams(vmem_limit_bytes=58 << 20),
        name="columns",
    )(pos, gate_train, up_train)

    def exchange(x):
        return lax.all_to_all(x, "z", split_axis=0, concat_axis=0, tiled=True)

    def sides(own):
        return ring(own, X, 4, 1), ring(own, X, 4, -1)

    def far(left, right):
        return ring(left[:4], X, 4, 1), ring(right[4:], X, 4, -1)

    below, above = [pair], [pair]
    for k in range(3):
        if k == 2:
            below[2], above[2], *blocks = barrier((below[2], above[2], *blocks))
        below.append(ring(below[-1], "z", 8, 1))
        above.append(ring(above[-1], "z", 8, -1))
    part_a, *last = barrier((blocks[0], ring(below[3][:1], "z", 8, 1), ring(above[3][1:], "z", 8, -1)))
    own_a = exchange(part_a)
    feats = [pair] + above[1:] + [jnp.concatenate(last, axis=0)] + below[:0:-1]
    sent = pl.pallas_call(
        dispatch_kernel,
        out_shape=[jax.ShapeDtypeStruct((2 * MOST, 16 * width + 128), BF)] * 4,
        in_specs=[SM] + [VM] * 9,
        out_specs=[VM] * 4,
        compiler_params=pltpu.CompilerParams(vmem_limit_bytes=24 << 20),
        name="dispatch",
    )(pos, meta, *feats)
    near = ring(sent[1], "y", 4, 1), ring(sent[3], "y", 4, 3)
    other = [ring(sent[0], "c", 2, 1)]
    part_b, own_a = barrier((blocks[1], own_a))
    own_b = exchange(part_b)
    left_a, right_a = sides(own_a)
    far_rows, other[0], *near = barrier((sent[2], other[0], *near))
    opposite = ring(far_rows, "y", 4, 2)
    left_a, right_a, *near = barrier((left_a, right_a, *near))
    far_a = far(left_a, right_a)
    other += [ring(h, "c", 2, 1) for h in near]
    own_b, opposite, *rest = barrier((own_b, opposite, *far_a, *other))
    far_a, other = rest[:2], rest[2:]
    left_b, right_b = sides(own_b)
    held = [sent[0], near[0], opposite, near[1]]
    other = [other[0], other[1], ring(opposite, "c", 2, 1), other[2]]

    def expert(*ws):
        return pl.pallas_call(
            expert_kernel,
            out_shape=jax.ShapeDtypeStruct((4, 2, 2, 2 * MOST, wide), BF),
            in_specs=[SM] + [ANY] * 13,
            out_specs=VM,
            scratch_shapes=[
                pltpu.VMEM((8, 2 * MOST, 16 * width + 128), BF),
                pltpu.VMEM((2, 8, 2, rows, 2 * wide), BF),
                pltpu.SemaphoreType.DMA((8,)),
                pltpu.SemaphoreType.DMA((5, 8)),
            ],
            compiler_params=pltpu.CompilerParams(vmem_limit_bytes=58 << 20),
            cost_estimate=pl.CostEstimate(
                flops=16 * MOST * 16 * width * 8 * wide, bytes_accessed=12 << 20, transcendentals=16 * MOST * 2 * wide
            ),
            name="expert",
        )(pos, *held, *other, *ws)

    def give_back(act):
        back = lax.all_to_all(act.reshape(16, 2 * MOST, wide), ("y", "c", "xl"), split_axis=0, concat_axis=0, tiled=True)
        return back.reshape(4, 2, 2, 2 * MOST, wide)

    act_a = expert(own_a, left_a, right_a, *far_a)
    left_b, right_b, act_a = barrier((left_b, right_b, act_a))
    back_a = give_back(act_a)
    back_b = give_back(expert(own_b, left_b, right_b, *far(left_b, right_b)))
    out = pl.pallas_call(
        combine_kernel,
        out_shape=jax.ShapeDtypeStruct((steps, n, 1024), BF),
        in_specs=[VM] * 3,
        out_specs=VM,
        compiler_params=pltpu.CompilerParams(vmem_limit_bytes=24 << 20),
        name="combine",
    )(meta, back_a, back_b)
    return out.reshape(steps, n, 2, 2, 256)


def solution(mesh):
    fine = Mesh(mesh.devices.reshape(2, 4, 2, 8, 2), ("dp", "y", "c", "z", "xl"))
    group, tensor = ("dp", "y", "c"), ("z", "xl")
    in_specs = (
        P(None, group, tensor),
        P(None, group, None),
        P(None, group, None),
        P(("y", "c"), tensor, None),
        P(("y", "c"), tensor, None),
    )
    out_specs = P(None, group, None, None, tensor)
    return jax.shard_map(body, mesh=fine, in_specs=in_specs, out_specs=out_specs, check_vma=False)
```

```python
import jax
import jax.numpy as jnp
from jax import lax
from jax.experimental import pallas as pl
from jax.experimental.pallas import tpu as pltpu
from jax.sharding import Mesh, PartitionSpec as P

MOST = 80
X = ("dp", "xl")
BF, F32 = jnp.bfloat16, jnp.float32
ANY = pl.BlockSpec(memory_space=pl.ANY)
VM = pl.BlockSpec(memory_space=pltpu.VMEM)
SM = pl.BlockSpec(memory_space=pltpu.SMEM)


def in_hbm(x):
    return pltpu.with_memory_space_constraint(x, pltpu.HBM)


def ring(x, axis, size, step):
    return lax.ppermute(x, axis, [(i, (i + step) % size) for i in range(size)])


def ranks(member):
    n = member.shape[1]
    before = lax.broadcasted_iota(jnp.int32, (n, n), 0) < lax.broadcasted_iota(jnp.int32, (n, n), 1)
    return jnp.dot(member.astype(BF), before.astype(BF), preferred_element_type=F32)


def slots(rank, member):
    row = lax.broadcasted_iota(jnp.int32, (MOST, rank.shape[1]), 0).astype(F32)
    return (row == rank) & (member > 0)


def dispatch_kernel(pos, meta, *refs):
    y, xl = pos[0], pos[2]
    feats, outs = refs[:8], refs[8:]
    ss, width, n = feats[0].shape
    lane = lax.broadcasted_iota(jnp.int32, (MOST, 128), 1)
    for s in range(ss):
        own = meta[2 * xl + s]
        rows = []
        members = []
        for d in range(4):
            e = lax.rem(y + d, 4).astype(F32)
            members.append(((own[0:1] == e) | (own[1:2] == e)).astype(F32))
        rank = ranks(jnp.concatenate(members, axis=0))
        for d in range(4):
            place = slots(rank[d : d + 1], members[d])
            rows.append(place.astype(BF))
            e = lax.rem(y + d, 4).astype(F32)
            weight = jnp.where(own[0:1] == e, own[2:3], own[3:4])
            whole = jnp.broadcast_to(jnp.sum(jnp.where(place, weight, 0.0), axis=1, keepdims=True), (MOST, 128))
            high = whole.astype(BF)
            rest = whole - high.astype(F32)
            mid = rest.astype(BF)
            low = (rest - mid.astype(F32)).astype(BF)
            terms = jnp.where(lane == 0, high.astype(F32), jnp.where(lane == 1, mid.astype(F32), jnp.where(lane == 2, low.astype(F32), 0.0)))
            outs[d][s * MOST : (s + 1) * MOST, 8 * width :] = terms.astype(BF)
        onehot = jnp.concatenate(rows, axis=0)
        for k in range(8):
            picked = lax.dot_general(onehot, feats[k][s], (((1,), (1,)), ((), ())), preferred_element_type=F32).astype(BF)
            for d in range(4):
                outs[d][s * MOST : (s + 1) * MOST, k * width : (k + 1) * width] = picked[d * MOST : (d + 1) * MOST]


def columns_kernel(pos, gate, up, out_a, out_b, held, sem):
    for flag, src in ((0, gate), (1, up)):

        @pl.when(pos[3] == flag)
        def _(src=src):
            copy = pltpu.make_async_copy(src.at[0], held, sem)
            copy.start()
            copy.wait()

    for r, out in enumerate((out_a, out_b)):
        for z in range(8):
            for t in range(2):
                first = z * 512 + t * 256 + r * 128
                out[z, :, t * 128 : (t + 1) * 128] = held[:, first : first + 128]


def expert_kernel(pos, *refs):
    xs, ws, (out, xbuf, wbuf, xsem, wsem) = refs[:8], refs[8:13], refs[13:]
    y, c, xl, dp, z = (pos[i] for i in range(5))
    width = 16 * ws[0].shape[1]
    copies = []
    for i, (src, off, low) in enumerate(((ws[0], 0, 0), (ws[1], 3, 0), (ws[2], 1, 0), (ws[3], 2, 0), (ws[4], 2, 4))):
        j = lax.rem(dp * 2 + xl + off, 4)
        for k in range(src.shape[0]):
            place = wbuf.at[lax.div(j, 2), lax.rem(low + k + 8 - z, 8), lax.rem(j, 2)]
            copies.append(pltpu.make_async_copy(src.at[k], place, wsem.at[i, k]))
    rows = [pltpu.make_async_copy(xs[g], xbuf.at[g], xsem.at[g]) for g in range(8)]
    for cp in copies:
        cp.start()
    rows[0].start()
    for cp in copies:
        cp.wait()
    rows[1].start()
    for g in range(8):
        d, cc = g % 4, g // 4
        if g < 6:
            rows[g + 2].start()
        rows[g].wait()
        rw = jnp.sum(xbuf[g, :, width:].astype(F32), axis=1, keepdims=True)
        gate = jnp.dot(xbuf[g, :, :width], wbuf[0].reshape(width, 256), preferred_element_type=F32)
        up = jnp.dot(xbuf[g, :, :width], wbuf[1].reshape(width, 256), preferred_element_type=F32)
        act = (rw * (gate / (1.0 + jnp.exp(-gate)) * up)).astype(BF)
        for t in range(2):
            out[lax.rem(y + 4 - d, 4), c + cc - 2 * c * cc, t] = act[:, t * 128 : (t + 1) * 128]


def combine_kernel(meta, recv_a, recv_b, out):
    steps = meta.shape[0]
    for s in range(steps):
        own = meta[s]
        members = [((own[0:1] == e) | (own[1:2] == e)).astype(F32) for e in range(4)]
        rank = ranks(jnp.concatenate(members, axis=0))
        left, right = [], []
        for e in range(4):
            place = slots(rank[e : e + 1], members[e])
            left.append(jnp.concatenate([(place & (own[k : k + 1] == e)).astype(BF) for k in range(2)], axis=1))
            part = pl.ds((s % 2) * MOST, MOST)
            right.append(jnp.concatenate([r[e, h, s // 2, part] for h in range(2) for r in (recv_a, recv_b)], axis=1))
        picked = lax.dot_general(
            jnp.concatenate(left, axis=0), jnp.concatenate(right, axis=0), (((0,), (0,)), ((), ())), preferred_element_type=F32
        ).astype(BF)
        n = picked.shape[0] // 2
        out[s] = jnp.concatenate([picked[:n], picked[n:]], axis=1)


def body(tokens, expert_ids, route_weights, gate_train, up_train):
    barrier = lax.optimization_barrier
    dp, y, c, z, xl = (lax.axis_index(a) for a in ("dp", "y", "c", "z", "xl"))
    pos = jnp.stack([y, c, xl, dp, z]).astype(jnp.int32)
    steps, n, width = tokens.shape
    meta = jnp.concatenate([expert_ids.astype(F32), route_weights], axis=2).transpose(0, 2, 1)
    turned = tokens.transpose(0, 2, 1).reshape(2, steps // 2, width, n)
    mine = lax.dynamic_index_in_dim(turned, xl, 0, keepdims=False)
    theirs = lax.dynamic_index_in_dim(turned, 1 - xl, 0, keepdims=False)
    got = ring(theirs, "xl", 2, 1)
    pair = jnp.concatenate([jnp.where(xl == 0, mine, got), jnp.where(xl == 0, got, mine)], axis=1)
    rows, units = gate_train.shape[1:]
    wide = units // 32
    blocks = pl.pallas_call(
        columns_kernel,
        out_shape=[pltpu.VMEM((8, rows, 2 * wide), BF)] * 2,
        in_specs=[SM, ANY, ANY],
        out_specs=[VM] * 2,
        scratch_shapes=[pltpu.VMEM((rows, units), BF), pltpu.SemaphoreType.DMA(())],
        compiler_params=pltpu.CompilerParams(vmem_limit_bytes=8 << 20),
        name="columns",
    )(pos, in_hbm(gate_train), in_hbm(up_train))

    def exchange(x):
        return lax.all_to_all(x, "z", split_axis=0, concat_axis=0, tiled=True)

    def sides(own):
        return ring(own, X, 4, 1), ring(own, X, 4, -1)

    def far(left, right):
        return ring(left[:4], X, 4, 1), ring(right[4:], X, 4, -1)

    below, above = [pair], [pair]
    for k in range(3):
        if k == 2:
            below[2], above[2], *blocks = barrier((below[2], above[2], *blocks))
        below.append(ring(below[-1], "z", 8, 1))
        above.append(ring(above[-1], "z", 8, -1))
    part_a, *last = barrier((blocks[0], ring(below[3][:1], "z", 8, 1), ring(above[3][1:], "z", 8, -1)))
    own_a = exchange(part_a)
    feats = [pair] + above[1:] + [jnp.concatenate(last, axis=0)] + below[:0:-1]
    sent = pl.pallas_call(
        dispatch_kernel,
        out_shape=[pltpu.VMEM((2 * MOST, 16 * width + 128), BF)] * 4,
        in_specs=[SM] + [VM] * 9,
        out_specs=[VM] * 4,
        compiler_params=pltpu.CompilerParams(vmem_limit_bytes=10 << 20),
        name="dispatch",
    )(pos, meta, *feats)
    near = ring(sent[1], "y", 4, 1), ring(sent[3], "y", 4, 3)
    other = [ring(sent[0], "c", 2, 1)]
    part_b, own_a = barrier((blocks[1], own_a))
    own_b = exchange(part_b)
    left_a, right_a = sides(own_a)
    far_rows, other[0], *near = barrier((sent[2], other[0], *near))
    opposite = ring(far_rows, "y", 4, 2)
    left_a, right_a, *near = barrier((left_a, right_a, *near))
    far_a = far(left_a, right_a)
    own_b, opposite, *rest = barrier((own_b, opposite, *near, *far_a))
    near, far_a = rest[:2], rest[2:]
    left_b, right_b = sides(own_b)
    held = [sent[0], near[0], opposite, near[1]]
    other += [ring(h, "c", 2, 1) for h in held[1:]]

    def expert(*ws):
        return pl.pallas_call(
            expert_kernel,
            out_shape=pltpu.VMEM((4, 2, 2, 2 * MOST, wide), BF),
            in_specs=[SM] + [ANY] * 13,
            out_specs=VM,
            scratch_shapes=[
                pltpu.VMEM((8, 2 * MOST, 16 * width + 128), BF),
                pltpu.VMEM((2, 8, 2, rows, 2 * wide), BF),
                pltpu.SemaphoreType.DMA((8,)),
                pltpu.SemaphoreType.DMA((5, 8)),
            ],
            compiler_params=pltpu.CompilerParams(vmem_limit_bytes=18 << 20),
            cost_estimate=pl.CostEstimate(
                flops=16 * MOST * 16 * width * 8 * wide, bytes_accessed=12 << 20, transcendentals=16 * MOST * 2 * wide
            ),
            name="expert",
        )(pos, *map(in_hbm, (*held, *other)), *ws)

    def give_back(act):
        back = lax.all_to_all(act.reshape(16, 2 * MOST, wide), ("y", "c", "xl"), split_axis=0, concat_axis=0, tiled=True)
        return back.reshape(4, 2, 2, 2 * MOST, wide)

    act_a = expert(own_a, left_a, right_a, *far_a)
    left_b, right_b, act_a = barrier((left_b, right_b, act_a))
    back_a = give_back(act_a)
    back_b = give_back(expert(own_b, left_b, right_b, *far(left_b, right_b)))
    out = pl.pallas_call(
        combine_kernel,
        out_shape=jax.ShapeDtypeStruct((steps, n, 1024), BF),
        in_specs=[VM] * 3,
        out_specs=VM,
        compiler_params=pltpu.CompilerParams(vmem_limit_bytes=10 << 20),
        name="combine",
    )(meta, back_a, back_b)
    return out.reshape(steps, n, 2, 2, 256)


def solution(mesh):
    fine = Mesh(mesh.devices.reshape(2, 4, 2, 8, 2), ("dp", "y", "c", "z", "xl"))
    group, tensor = ("dp", "y", "c"), ("z", "xl")
    in_specs = (
        P(None, group, tensor),
        P(None, group, None),
        P(None, group, None),
        P(("y", "c"), tensor, None),
        P(("y", "c"), tensor, None),
    )
    out_specs = P(None, group, None, None, tensor)
    return jax.shard_map(body, mesh=fine, in_specs=in_specs, out_specs=out_specs, check_vma=False)
```

```python
import jax
import jax.numpy as jnp
from jax import lax
from jax.experimental import pallas as pl
from jax.experimental.pallas import tpu as pltpu
from jax.sharding import Mesh, PartitionSpec as P

MOST = 80
X = ("dp", "xl")
BF, F32 = jnp.bfloat16, jnp.float32
ANY = pl.BlockSpec(memory_space=pl.ANY)
VM = pl.BlockSpec(memory_space=pltpu.VMEM)
SM = pl.BlockSpec(memory_space=pltpu.SMEM)


def in_hbm(x):
    return pltpu.with_memory_space_constraint(x, pltpu.HBM)


def ring(x, axis, size, step):
    return lax.ppermute(x, axis, [(i, (i + step) % size) for i in range(size)])


def ranks(member):
    n = member.shape[1]
    before = lax.broadcasted_iota(jnp.int32, (n, n), 0) < lax.broadcasted_iota(jnp.int32, (n, n), 1)
    return jnp.dot(member.astype(BF), before.astype(BF), preferred_element_type=F32)


def slots(rank, member):
    row = lax.broadcasted_iota(jnp.int32, (MOST, rank.shape[1]), 0).astype(F32)
    return (row == rank) & (member > 0)


def dispatch_kernel(pos, meta, *refs):
    y, xl = pos[0], pos[2]
    feats, outs = refs[:8], refs[8:]
    ss, width, n = feats[0].shape
    lane = lax.broadcasted_iota(jnp.int32, (MOST, 128), 1)
    for s in range(ss):
        own = meta[2 * xl + s]
        rows = []
        members = []
        for d in range(4):
            e = lax.rem(y + d, 4).astype(F32)
            members.append(((own[0:1] == e) | (own[1:2] == e)).astype(F32))
        rank = ranks(jnp.concatenate(members, axis=0))
        for d in range(4):
            place = slots(rank[d : d + 1], members[d])
            rows.append(place.astype(BF))
            e = lax.rem(y + d, 4).astype(F32)
            weight = jnp.where(own[0:1] == e, own[2:3], own[3:4])
            whole = jnp.broadcast_to(jnp.sum(jnp.where(place, weight, 0.0), axis=1, keepdims=True), (MOST, 128))
            high = whole.astype(BF)
            rest = whole - high.astype(F32)
            mid = rest.astype(BF)
            low = (rest - mid.astype(F32)).astype(BF)
            terms = jnp.where(lane == 0, high.astype(F32), jnp.where(lane == 1, mid.astype(F32), jnp.where(lane == 2, low.astype(F32), 0.0)))
            outs[d][s * MOST : (s + 1) * MOST, 8 * width :] = terms.astype(BF)
        onehot = jnp.concatenate(rows, axis=0)
        for k in range(8):
            picked = lax.dot_general(onehot, feats[k][s], (((1,), (1,)), ((), ())), preferred_element_type=F32).astype(BF)
            for d in range(4):
                outs[d][s * MOST : (s + 1) * MOST, k * width : (k + 1) * width] = picked[d * MOST : (d + 1) * MOST]


def columns_kernel(pos, gate, up, out_a, out_b, held, sem):
    for flag, src in ((0, gate), (1, up)):

        @pl.when(pos[3] == flag)
        def _(src=src):
            copy = pltpu.make_async_copy(src.at[0], held, sem)
            copy.start()
            copy.wait()

    for r, out in enumerate((out_a, out_b)):
        for z in range(8):
            for t in range(2):
                first = z * 512 + t * 256 + r * 128
                out[z, :, t * 128 : (t + 1) * 128] = held[:, first : first + 128]


def expert_kernel(pos, *refs):
    xs, ws, (out, xbuf, wbuf, xsem) = refs[:8], refs[8:13], refs[13:]
    y, c, xl, dp, z = (pos[i] for i in range(5))
    width = 16 * ws[0].shape[1]
    rows = [pltpu.make_async_copy(xs[g], xbuf.at[g], xsem.at[g]) for g in range(8)]
    for cp in rows:
        cp.start()
    for src, off, low in ((ws[0], 0, 0), (ws[1], 3, 0), (ws[2], 1, 0), (ws[3], 2, 0), (ws[4], 2, 4)):
        j = lax.rem(dp * 2 + xl + off, 4)
        for k in range(src.shape[0]):
            wbuf[lax.div(j, 2), lax.rem(low + k + 8 - z, 8), lax.rem(j, 2)] = src[k]
    for g in range(8):
        d, cc = g % 4, g // 4
        rows[g].wait()
        rw = jnp.sum(xbuf[g, :, width:].astype(F32), axis=1, keepdims=True)
        gate = jnp.dot(xbuf[g, :, :width], wbuf[0].reshape(width, 256), preferred_element_type=F32)
        up = jnp.dot(xbuf[g, :, :width], wbuf[1].reshape(width, 256), preferred_element_type=F32)
        act = (rw * (gate / (1.0 + jnp.exp(-gate)) * up)).astype(BF)
        for t in range(2):
            out[lax.rem(y + 4 - d, 4), c + cc - 2 * c * cc, t] = act[:, t * 128 : (t + 1) * 128]


def combine_kernel(meta, recv_a, recv_b, out):
    steps = meta.shape[0]
    for s in range(steps):
        own = meta[s]
        members = [((own[0:1] == e) | (own[1:2] == e)).astype(F32) for e in range(4)]
        rank = ranks(jnp.concatenate(members, axis=0))
        left, right = [], []
        for e in range(4):
            place = slots(rank[e : e + 1], members[e])
            left.append(jnp.concatenate([(place & (own[k : k + 1] == e)).astype(BF) for k in range(2)], axis=1))
            part = pl.ds((s % 2) * MOST, MOST)
            right.append(jnp.concatenate([r[e, h, s // 2, part] for h in range(2) for r in (recv_a, recv_b)], axis=1))
        picked = lax.dot_general(
            jnp.concatenate(left, axis=0), jnp.concatenate(right, axis=0), (((0,), (0,)), ((), ())), preferred_element_type=F32
        ).astype(BF)
        n = picked.shape[0] // 2
        out[s] = jnp.concatenate([picked[:n], picked[n:]], axis=1)


def body(tokens, expert_ids, route_weights, gate_train, up_train):
    barrier = lax.optimization_barrier
    dp, y, c, z, xl = (lax.axis_index(a) for a in ("dp", "y", "c", "z", "xl"))
    pos = jnp.stack([y, c, xl, dp, z]).astype(jnp.int32)
    steps, n, width = tokens.shape
    meta = jnp.concatenate([expert_ids.astype(F32), route_weights], axis=2).transpose(0, 2, 1)
    turned = tokens.transpose(0, 2, 1).reshape(2, steps // 2, width, n)
    mine = lax.dynamic_index_in_dim(turned, xl, 0, keepdims=False)
    theirs = lax.dynamic_index_in_dim(turned, 1 - xl, 0, keepdims=False)
    got = ring(theirs, "xl", 2, 1)
    pair = jnp.concatenate([jnp.where(xl == 0, mine, got), jnp.where(xl == 0, got, mine)], axis=1)
    rows, units = gate_train.shape[1:]
    wide = units // 32
    blocks = pl.pallas_call(
        columns_kernel,
        out_shape=[pltpu.VMEM((8, rows, 2 * wide), BF)] * 2,
        in_specs=[SM, ANY, ANY],
        out_specs=[VM] * 2,
        scratch_shapes=[pltpu.VMEM((rows, units), BF), pltpu.SemaphoreType.DMA(())],
        compiler_params=pltpu.CompilerParams(vmem_limit_bytes=8 << 20),
        name="columns",
    )(pos, in_hbm(gate_train), in_hbm(up_train))

    def exchange(x):
        return lax.all_to_all(x, "z", split_axis=0, concat_axis=0, tiled=True)

    def sides(own):
        return ring(own, X, 4, 1), ring(own, X, 4, -1)

    def far(left, right):
        return ring(left[:4], X, 4, 1), ring(right[4:], X, 4, -1)

    below, above = [pair], [pair]
    for k in range(3):
        if k == 2:
            below[2], above[2], *blocks = barrier((below[2], above[2], *blocks))
        below.append(ring(below[-1], "z", 8, 1))
        above.append(ring(above[-1], "z", 8, -1))
    part_a, *last = barrier((blocks[0], ring(below[3][:1], "z", 8, 1), ring(above[3][1:], "z", 8, -1)))
    own_a = exchange(part_a)
    feats = [pair] + above[1:] + [jnp.concatenate(last, axis=0)] + below[:0:-1]
    sent = pl.pallas_call(
        dispatch_kernel,
        out_shape=[pltpu.VMEM((2 * MOST, 16 * width + 128), BF)] * 4,
        in_specs=[SM] + [VM] * 9,
        out_specs=[VM] * 4,
        compiler_params=pltpu.CompilerParams(vmem_limit_bytes=10 << 20),
        name="dispatch",
    )(pos, meta, *feats)
    near = ring(sent[1], "y", 4, 1), ring(sent[3], "y", 4, 3)
    other = [ring(sent[0], "c", 2, 1)]
    part_b, own_a = barrier((blocks[1], own_a))
    own_b = exchange(part_b)
    left_a, right_a = sides(own_a)
    far_rows, other[0], *near = barrier((sent[2], other[0], *near))
    opposite = ring(far_rows, "y", 4, 2)
    left_a, right_a, *near = barrier((left_a, right_a, *near))
    far_a = far(left_a, right_a)
    own_b, opposite, *rest = barrier((own_b, opposite, *near, *far_a))
    near, far_a = rest[:2], rest[2:]
    left_b, right_b = sides(own_b)
    held = [sent[0], near[0], opposite, near[1]]
    other += [ring(h, "c", 2, 1) for h in held[1:]]

    def expert(*ws):
        return pl.pallas_call(
            expert_kernel,
            out_shape=pltpu.VMEM((4, 2, 2, 2 * MOST, wide), BF),
            in_specs=[SM] + [ANY] * 8 + [VM] * 5,
            out_specs=VM,
            scratch_shapes=[
                pltpu.VMEM((8, 2 * MOST, 16 * width + 128), BF),
                pltpu.VMEM((2, 8, 2, rows, 2 * wide), BF),
                pltpu.SemaphoreType.DMA((8,)),
            ],
            compiler_params=pltpu.CompilerParams(vmem_limit_bytes=18 << 20),
            cost_estimate=pl.CostEstimate(
                flops=16 * MOST * 16 * width * 8 * wide, bytes_accessed=12 << 20, transcendentals=16 * MOST * 2 * wide
            ),
            name="expert",
        )(pos, *map(in_hbm, (*held, *other)), *ws)

    def give_back(act):
        back = lax.all_to_all(act.reshape(16, 2 * MOST, wide), ("y", "c", "xl"), split_axis=0, concat_axis=0, tiled=True)
        return back.reshape(4, 2, 2, 2 * MOST, wide)

    act_a = expert(own_a, left_a, right_a, *far_a)
    left_b, right_b, act_a = barrier((left_b, right_b, act_a))
    back_a = give_back(act_a)
    back_b = give_back(expert(own_b, left_b, right_b, *far(left_b, right_b)))
    out = pl.pallas_call(
        combine_kernel,
        out_shape=jax.ShapeDtypeStruct((steps, n, 1024), BF),
        in_specs=[VM] * 3,
        out_specs=VM,
        compiler_params=pltpu.CompilerParams(vmem_limit_bytes=10 << 20),
        name="combine",
    )(meta, back_a, back_b)
    return out.reshape(steps, n, 2, 2, 256)


def solution(mesh):
    fine = Mesh(mesh.devices.reshape(2, 4, 2, 8, 2), ("dp", "y", "c", "z", "xl"))
    group, tensor = ("dp", "y", "c"), ("z", "xl")
    in_specs = (
        P(None, group, tensor),
        P(None, group, None),
        P(None, group, None),
        P(("y", "c"), tensor, None),
        P(("y", "c"), tensor, None),
    )
    out_specs = P(None, group, None, None, tensor)
    return jax.shard_map(body, mesh=fine, in_specs=in_specs, out_specs=out_specs, check_vma=False)
```

```python
import jax
import jax.numpy as jnp
from jax import lax
from jax.experimental import pallas as pl
from jax.experimental.pallas import tpu as pltpu
from jax.sharding import Mesh, PartitionSpec as P

MOST = 80
X = ("dp", "xl")
BF, F32 = jnp.bfloat16, jnp.float32
ANY = pl.BlockSpec(memory_space=pl.ANY)
VM = pl.BlockSpec(memory_space=pltpu.VMEM)
SM = pl.BlockSpec(memory_space=pltpu.SMEM)


def ring(x, axis, size, step):
    return lax.ppermute(x, axis, [(i, (i + step) % size) for i in range(size)])


def ranks(member):
    n = member.shape[1]
    before = lax.broadcasted_iota(jnp.int32, (n, n), 0) < lax.broadcasted_iota(jnp.int32, (n, n), 1)
    return jnp.dot(member.astype(BF), before.astype(BF), preferred_element_type=F32)


def slots(rank, member):
    row = lax.broadcasted_iota(jnp.int32, (MOST, rank.shape[1]), 0).astype(F32)
    return (row == rank) & (member > 0)


def dispatch_kernel(pos, meta, *refs):
    y, xl = pos[0], pos[2]
    feats, outs = refs[:8], refs[8:]
    ss, width, n = feats[0].shape
    lane = lax.broadcasted_iota(jnp.int32, (MOST, 128), 1)
    for s in range(ss):
        own = meta[2 * xl + s]
        rows = []
        members = []
        for d in range(4):
            e = lax.rem(y + d, 4).astype(F32)
            members.append(((own[0:1] == e) | (own[1:2] == e)).astype(F32))
        rank = ranks(jnp.concatenate(members, axis=0))
        for d in range(4):
            place = slots(rank[d : d + 1], members[d])
            rows.append(place.astype(BF))
            e = lax.rem(y + d, 4).astype(F32)
            weight = jnp.where(own[0:1] == e, own[2:3], own[3:4])
            whole = jnp.broadcast_to(jnp.sum(jnp.where(place, weight, 0.0), axis=1, keepdims=True), (MOST, 128))
            high = whole.astype(BF)
            rest = whole - high.astype(F32)
            mid = rest.astype(BF)
            low = (rest - mid.astype(F32)).astype(BF)
            terms = jnp.where(lane == 0, high.astype(F32), jnp.where(lane == 1, mid.astype(F32), jnp.where(lane == 2, low.astype(F32), 0.0)))
            outs[d][s * MOST : (s + 1) * MOST, 8 * width :] = terms.astype(BF)
        onehot = jnp.concatenate(rows, axis=0)
        for k in range(8):
            picked = lax.dot_general(onehot, feats[k][s], (((1,), (1,)), ((), ())), preferred_element_type=F32).astype(BF)
            for d in range(4):
                outs[d][s * MOST : (s + 1) * MOST, k * width : (k + 1) * width] = picked[d * MOST : (d + 1) * MOST]


def columns_kernel(pos, gate, up, out_a, out_b, held, sem):
    for flag, src in ((0, gate), (1, up)):

        @pl.when(pos[3] == flag)
        def _(src=src):
            copy = pltpu.make_async_copy(src.at[0], held, sem)
            copy.start()
            copy.wait()

    for r, out in enumerate((out_a, out_b)):
        for z in range(8):
            for t in range(2):
                first = z * 512 + t * 256 + r * 128
                out[z, :, t * 128 : (t + 1) * 128] = held[:, first : first + 128]


def expert_kernel(pos, *refs):
    xs, ws, (out, xbuf, wbuf, gates, xsem, wsem) = refs[:8], refs[8:13], refs[13:]
    y, c, xl, dp, z = (pos[i] for i in range(5))
    width = 16 * ws[0].shape[1]
    for here in range(4):

        @pl.when(dp * 2 + xl == here)
        def _(here=here):
            for slot in range(4):
                for src, low in {0: [(ws[0], 0)], 3: [(ws[1], 0)], 1: [(ws[2], 0)], 2: [(ws[3], 0), (ws[4], 4)]}[(slot - here) % 4]:
                    for k in range(src.shape[0]):
                        place = wbuf.at[slot // 2, lax.rem(low + k + 8 - z, 8), slot % 2]
                        pltpu.make_async_copy(src.at[k], place, wsem.at[slot, low + k]).start()

    def wait(half):
        for slot in (2 * half, 2 * half + 1):
            for k in range(8):
                pltpu.make_async_copy(ws[0].at[k], wbuf.at[half, k, slot % 2], wsem.at[slot, k]).wait()

    rows = [pltpu.make_async_copy(xs[g], xbuf.at[g], xsem.at[g]) for g in range(8)]
    for cp in rows:
        cp.start()
    wait(0)
    for g in range(8):
        rows[g].wait()
        gates[g] = jnp.dot(xbuf[g, :, :width], wbuf[0].reshape(width, 256), preferred_element_type=F32)
    wait(1)
    for g in range(8):
        d, cc = g % 4, g // 4
        rw = jnp.sum(xbuf[g, :, width:].astype(F32), axis=1, keepdims=True)
        gate = gates[g]
        up = jnp.dot(xbuf[g, :, :width], wbuf[1].reshape(width, 256), preferred_element_type=F32)
        act = (rw * (gate / (1.0 + jnp.exp(-gate)) * up)).astype(BF)
        for t in range(2):
            out[lax.rem(y + 4 - d, 4), c + cc - 2 * c * cc, t] = act[:, t * 128 : (t + 1) * 128]


def combine_kernel(meta, recv_a, recv_b, out):
    steps = meta.shape[0]
    for s in range(steps):
        own = meta[s]
        members = [((own[0:1] == e) | (own[1:2] == e)).astype(F32) for e in range(4)]
        rank = ranks(jnp.concatenate(members, axis=0))
        left, right = [], []
        for e in range(4):
            place = slots(rank[e : e + 1], members[e])
            left.append(jnp.concatenate([(place & (own[k : k + 1] == e)).astype(BF) for k in range(2)], axis=1))
            part = pl.ds((s % 2) * MOST, MOST)
            right.append(jnp.concatenate([r[e, h, s // 2, part] for h in range(2) for r in (recv_a, recv_b)], axis=1))
        picked = lax.dot_general(
            jnp.concatenate(left, axis=0), jnp.concatenate(right, axis=0), (((0,), (0,)), ((), ())), preferred_element_type=F32
        ).astype(BF)
        n = picked.shape[0] // 2
        out[s] = jnp.concatenate([picked[:n], picked[n:]], axis=1)


def body(tokens, expert_ids, route_weights, gate_train, up_train):
    barrier = lax.optimization_barrier
    dp, y, c, z, xl = (lax.axis_index(a) for a in ("dp", "y", "c", "z", "xl"))
    pos = jnp.stack([y, c, xl, dp, z]).astype(jnp.int32)
    steps, n, width = tokens.shape
    meta = jnp.concatenate([expert_ids.astype(F32), route_weights], axis=2).transpose(0, 2, 1)
    turned = tokens.transpose(0, 2, 1).reshape(2, steps // 2, width, n)
    mine = lax.dynamic_index_in_dim(turned, xl, 0, keepdims=False)
    theirs = lax.dynamic_index_in_dim(turned, 1 - xl, 0, keepdims=False)
    got = ring(theirs, "xl", 2, 1)
    pair = jnp.concatenate([jnp.where(xl == 0, mine, got), jnp.where(xl == 0, got, mine)], axis=1)
    rows, units = gate_train.shape[1:]
    wide = units // 32
    blocks = pl.pallas_call(
        columns_kernel,
        out_shape=[jax.ShapeDtypeStruct((8, rows, 2 * wide), BF)] * 2,
        in_specs=[SM, ANY, ANY],
        out_specs=[VM] * 2,
        scratch_shapes=[pltpu.VMEM((rows, units), BF), pltpu.SemaphoreType.DMA(())],
        compiler_params=pltpu.CompilerParams(vmem_limit_bytes=58 << 20),
        name="columns",
    )(pos, gate_train, up_train)

    def exchange(x):
        return lax.all_to_all(x, "z", split_axis=0, concat_axis=0, tiled=True)

    def sides(own):
        return ring(own, X, 4, 1), ring(own, X, 4, -1)

    def far(left, right):
        return ring(left[:4], X, 4, 1), ring(right[4:], X, 4, -1)

    below, above = [pair], [pair]
    for k in range(3):
        if k == 2:
            below[2], above[2], *blocks = barrier((below[2], above[2], *blocks))
        below.append(ring(below[-1], "z", 8, 1))
        above.append(ring(above[-1], "z", 8, -1))
    part_a, *last = barrier((blocks[0], ring(below[3][:1], "z", 8, 1), ring(above[3][1:], "z", 8, -1)))
    own_a = exchange(part_a)
    feats = [pair] + above[1:] + [jnp.concatenate(last, axis=0)] + below[:0:-1]
    sent = pl.pallas_call(
        dispatch_kernel,
        out_shape=[jax.ShapeDtypeStruct((2 * MOST, 16 * width + 128), BF)] * 4,
        in_specs=[SM] + [VM] * 9,
        out_specs=[VM] * 4,
        compiler_params=pltpu.CompilerParams(vmem_limit_bytes=24 << 20),
        name="dispatch",
    )(pos, meta, *feats)
    near = ring(sent[1], "y", 4, 1), ring(sent[3], "y", 4, 3)
    other = [ring(sent[0], "c", 2, 1)]
    part_b, own_a = barrier((blocks[1], own_a))
    own_b = exchange(part_b)
    left_a, right_a = sides(own_a)
    left_a, right_a, far_rows, other[0], *near = barrier((left_a, right_a, sent[2], other[0], *near))
    far_a = far(left_a, right_a)
    opposite = ring(far_rows, "y", 4, 2)
    own_b, opposite, *rest = barrier((own_b, opposite, *far_a, *near))
    far_a, near = rest[:2], rest[2:]
    left_b, right_b = sides(own_b)
    held = [sent[0], near[0], opposite, near[1]]
    left_b, right_b, *rest = barrier((left_b, right_b, *held[1:]))
    other += [ring(h, "c", 2, 1) for h in rest]

    def expert(*ws):
        return pl.pallas_call(
            expert_kernel,
            out_shape=jax.ShapeDtypeStruct((4, 2, 2, 2 * MOST, wide), BF),
            in_specs=[SM] + [ANY] * 13,
            out_specs=VM,
            scratch_shapes=[
                pltpu.VMEM((8, 2 * MOST, 16 * width + 128), BF),
                pltpu.VMEM((2, 8, 2, rows, 2 * wide), BF),
                pltpu.VMEM((8, 2 * MOST, 256), F32),
                pltpu.SemaphoreType.DMA((8,)),
                pltpu.SemaphoreType.DMA((4, 8)),
            ],
            compiler_params=pltpu.CompilerParams(vmem_limit_bytes=58 << 20),
            cost_estimate=pl.CostEstimate(
                flops=16 * MOST * 16 * width * 8 * wide, bytes_accessed=12 << 20, transcendentals=16 * MOST * 2 * wide
            ),
            name="expert",
        )(pos, *held, *other, *ws)

    def give_back(act):
        back = lax.all_to_all(act.reshape(16, 2 * MOST, wide), ("y", "c", "xl"), split_axis=0, concat_axis=0, tiled=True)
        return back.reshape(4, 2, 2, 2 * MOST, wide)

    act_a = expert(own_a, left_a, right_a, *far_a)
    back_a = give_back(act_a)
    back_b = give_back(expert(own_b, left_b, right_b, *far(left_b, right_b)))
    out = pl.pallas_call(
        combine_kernel,
        out_shape=jax.ShapeDtypeStruct((steps, n, 1024), BF),
        in_specs=[VM] * 3,
        out_specs=VM,
        compiler_params=pltpu.CompilerParams(vmem_limit_bytes=24 << 20),
        name="combine",
    )(meta, back_a, back_b)
    return out.reshape(steps, n, 2, 2, 256)


def solution(mesh):
    fine = Mesh(mesh.devices.reshape(2, 4, 2, 8, 2), ("dp", "y", "c", "z", "xl"))
    group, tensor = ("dp", "y", "c"), ("z", "xl")
    in_specs = (
        P(None, group, tensor),
        P(None, group, None),
        P(None, group, None),
        P(("y", "c"), tensor, None),
        P(("y", "c"), tensor, None),
    )
    out_specs = P(None, group, None, None, tensor)
    return jax.shard_map(body, mesh=fine, in_specs=in_specs, out_specs=out_specs, check_vma=False)
```

```python
import jax
import jax.numpy as jnp
from jax import lax
from jax.experimental import pallas as pl
from jax.experimental.pallas import tpu as pltpu
from jax.sharding import Mesh, PartitionSpec as P

MOST = 80
X = ("dp", "xl")
BF, F32 = jnp.bfloat16, jnp.float32
ANY = pl.BlockSpec(memory_space=pl.ANY)
VM = pl.BlockSpec(memory_space=pltpu.VMEM)
SM = pl.BlockSpec(memory_space=pltpu.SMEM)


def ring(x, axis, size, step):
    return lax.ppermute(x, axis, [(i, (i + step) % size) for i in range(size)])


def ranks(member):
    n = member.shape[1]
    before = lax.broadcasted_iota(jnp.int32, (n, n), 0) < lax.broadcasted_iota(jnp.int32, (n, n), 1)
    return jnp.dot(member.astype(BF), before.astype(BF), preferred_element_type=F32)


def slots(rank, member):
    row = lax.broadcasted_iota(jnp.int32, (MOST, rank.shape[1]), 0).astype(F32)
    return (row == rank) & (member > 0)


def dispatch_kernel(pos, meta, *refs):
    y, xl = pos[0], pos[2]
    feats, outs = refs[:8], refs[8:]
    ss, width, n = feats[0].shape
    lane = lax.broadcasted_iota(jnp.int32, (MOST, 128), 1)
    for s in range(ss):
        own = meta[2 * xl + s]
        rows = []
        members = []
        for d in range(4):
            e = lax.rem(y + d, 4).astype(F32)
            members.append(((own[0:1] == e) | (own[1:2] == e)).astype(F32))
        rank = ranks(jnp.concatenate(members, axis=0))
        for d in range(4):
            place = slots(rank[d : d + 1], members[d])
            rows.append(place.astype(BF))
            e = lax.rem(y + d, 4).astype(F32)
            weight = jnp.where(own[0:1] == e, own[2:3], own[3:4])
            whole = jnp.broadcast_to(jnp.sum(jnp.where(place, weight, 0.0), axis=1, keepdims=True), (MOST, 128))
            high = whole.astype(BF)
            rest = whole - high.astype(F32)
            mid = rest.astype(BF)
            low = (rest - mid.astype(F32)).astype(BF)
            terms = jnp.where(lane == 0, high.astype(F32), jnp.where(lane == 1, mid.astype(F32), jnp.where(lane == 2, low.astype(F32), 0.0)))
            outs[d][s * MOST : (s + 1) * MOST, 8 * width :] = terms.astype(BF)
        onehot = jnp.concatenate(rows, axis=0)
        for k in range(8):
            picked = lax.dot_general(onehot, feats[k][s], (((1,), (1,)), ((), ())), preferred_element_type=F32).astype(BF)
            for d in range(4):
                outs[d][s * MOST : (s + 1) * MOST, k * width : (k + 1) * width] = picked[d * MOST : (d + 1) * MOST]


def columns_kernel(pos, gate, up, out_a, out_b, held, sem):
    for flag, src in ((0, gate), (1, up)):

        @pl.when(pos[3] == flag)
        def _(src=src):
            copy = pltpu.make_async_copy(src.at[0], held, sem)
            copy.start()
            copy.wait()

    for r, out in enumerate((out_a, out_b)):
        for z in range(8):
            for t in range(2):
                first = z * 512 + t * 256 + r * 128
                out[z, :, t * 128 : (t + 1) * 128] = held[:, first : first + 128]


def expert_kernel(pos, *refs):
    xs, ws, (out, xbuf, wbuf, xsem, wsem) = refs[:8], refs[8:13], refs[13:]
    y, c, xl, dp, z = (pos[i] for i in range(5))
    width = 16 * ws[0].shape[1]
    copies = []
    for i, (src, off, low) in enumerate(((ws[0], 0, 0), (ws[1], 3, 0), (ws[2], 1, 0), (ws[3], 2, 0), (ws[4], 2, 4))):
        j = lax.rem(dp * 2 + xl + off, 4)
        for k in range(src.shape[0]):
            place = wbuf.at[lax.div(j, 2), lax.rem(low + k + 8 - z, 8), lax.rem(j, 2)]
            copies.append(pltpu.make_async_copy(src.at[k], place, wsem.at[i, k]))
    rows = [pltpu.make_async_copy(xs[g], xbuf.at[g], xsem.at[g]) for g in range(8)]
    for cp in copies:
        cp.start()
    rows[0].start()
    for cp in copies:
        cp.wait()
    rows[1].start()
    for g in range(8):
        d, cc = g % 4, g // 4
        if g < 6:
            rows[g + 2].start()
        rows[g].wait()
        rw = jnp.sum(xbuf[g, :, width:].astype(F32), axis=1, keepdims=True)
        gate = jnp.dot(xbuf[g, :, :width], wbuf[0].reshape(width, 256), preferred_element_type=F32)
        up = jnp.dot(xbuf[g, :, :width], wbuf[1].reshape(width, 256), preferred_element_type=F32)
        act = (rw * (gate / (1.0 + jnp.exp(-gate)) * up)).astype(BF)
        for t in range(2):
            out[lax.rem(y + 4 - d, 4), c + cc - 2 * c * cc, t] = act[:, t * 128 : (t + 1) * 128]


def combine_kernel(meta, recv_a, recv_b, out):
    steps = meta.shape[0]
    for s in range(steps):
        own = meta[s]
        members = [((own[0:1] == e) | (own[1:2] == e)).astype(F32) for e in range(4)]
        rank = ranks(jnp.concatenate(members, axis=0))
        left, right = [], []
        for e in range(4):
            place = slots(rank[e : e + 1], members[e])
            left.append(jnp.concatenate([(place & (own[k : k + 1] == e)).astype(BF) for k in range(2)], axis=1))
            part = pl.ds((s % 2) * MOST, MOST)
            right.append(jnp.concatenate([r[e, h, s // 2, part] for h in range(2) for r in (recv_a, recv_b)], axis=1))
        picked = lax.dot_general(
            jnp.concatenate(left, axis=0), jnp.concatenate(right, axis=0), (((0,), (0,)), ((), ())), preferred_element_type=F32
        ).astype(BF)
        n = picked.shape[0] // 2
        out[s] = jnp.concatenate([picked[:n], picked[n:]], axis=1)


def body(tokens, expert_ids, route_weights, gate_train, up_train):
    barrier = lax.optimization_barrier
    dp, y, c, z, xl = (lax.axis_index(a) for a in ("dp", "y", "c", "z", "xl"))
    pos = jnp.stack([y, c, xl, dp, z]).astype(jnp.int32)
    steps, n, width = tokens.shape
    meta = jnp.concatenate([expert_ids.astype(F32), route_weights], axis=2).transpose(0, 2, 1)
    turned = tokens.transpose(0, 2, 1).reshape(2, steps // 2, width, n)
    mine = lax.dynamic_index_in_dim(turned, xl, 0, keepdims=False)
    theirs = lax.dynamic_index_in_dim(turned, 1 - xl, 0, keepdims=False)
    got = ring(theirs, "xl", 2, 1)
    pair = jnp.concatenate([jnp.where(xl == 0, mine, got), jnp.where(xl == 0, got, mine)], axis=1)
    rows, units = gate_train.shape[1:]
    wide = units // 32
    blocks = pl.pallas_call(
        columns_kernel,
        out_shape=[jax.ShapeDtypeStruct((8, rows, 2 * wide), BF)] * 2,
        in_specs=[SM, ANY, ANY],
        out_specs=[VM] * 2,
        scratch_shapes=[pltpu.VMEM((rows, units), BF), pltpu.SemaphoreType.DMA(())],
        compiler_params=pltpu.CompilerParams(vmem_limit_bytes=58 << 20),
        name="columns",
    )(pos, gate_train, up_train)

    def exchange(x):
        return lax.all_to_all(x, "z", split_axis=0, concat_axis=0, tiled=True)

    def sides(own):
        return ring(own, X, 4, 1), ring(own, X, 4, -1)

    def far(left, right):
        return ring(left[:4], X, 4, 1), ring(right[4:], X, 4, -1)

    below = [pair, ring(pair, "z", 8, 1), ring(pair, "z", 8, 2)]
    above = [pair, ring(pair, "z", 8, -1), ring(pair, "z", 8, -2)]
    below[1], above[1], below[2], above[2], *blocks = barrier((below[1], above[1], below[2], above[2], *blocks))
    part_a, *last = barrier(
        (
            blocks[0],
            ring(above[2], "z", 8, -1),
            ring(below[2][:1], "z", 8, 2),
            ring(above[2][1:], "z", 8, -2),
            ring(below[2], "z", 8, 1),
        )
    )
    own_a = exchange(part_a)
    feats = [*above, last[0], jnp.concatenate(last[1:3], axis=0), last[3], *below[:0:-1]]
    sent = pl.pallas_call(
        dispatch_kernel,
        out_shape=[jax.ShapeDtypeStruct((2 * MOST, 16 * width + 128), BF)] * 4,
        in_specs=[SM] + [VM] * 9,
        out_specs=[VM] * 4,
        compiler_params=pltpu.CompilerParams(vmem_limit_bytes=24 << 20),
        name="dispatch",
    )(pos, meta, *feats)
    near = ring(sent[1], "y", 4, 1), ring(sent[3], "y", 4, 3)
    other = [ring(sent[0], "c", 2, 1)]
    part_b, own_a = barrier((blocks[1], own_a))
    own_b = exchange(part_b)
    left_a, right_a = sides(own_a)
    far_rows, other[0], *near = barrier((sent[2], other[0], *near))
    opposite = ring(far_rows, "y", 4, 2)
    left_a, right_a, *near = barrier((left_a, right_a, *near))
    far_a = far(left_a, right_a)
    other += [ring(h, "c", 2, 1) for h in near]
    own_b, opposite, *rest = barrier((own_b, opposite, *far_a, *other))
    far_a, other = rest[:2], rest[2:]
    left_b, right_b = sides(own_b)
    held = [sent[0], near[0], opposite, near[1]]
    other = [other[0], other[1], ring(opposite, "c", 2, 1), other[2]]

    def expert(*ws):
        return pl.pallas_call(
            expert_kernel,
            out_shape=jax.ShapeDtypeStruct((4, 2, 2, 2 * MOST, wide), BF),
            in_specs=[SM] + [ANY] * 13,
            out_specs=VM,
            scratch_shapes=[
                pltpu.VMEM((8, 2 * MOST, 16 * width + 128), BF),
                pltpu.VMEM((2, 8, 2, rows, 2 * wide), BF),
                pltpu.SemaphoreType.DMA((8,)),
                pltpu.SemaphoreType.DMA((5, 8)),
            ],
            compiler_params=pltpu.CompilerParams(vmem_limit_bytes=58 << 20),
            cost_estimate=pl.CostEstimate(
                flops=16 * MOST * 16 * width * 8 * wide, bytes_accessed=12 << 20, transcendentals=16 * MOST * 2 * wide
            ),
            name="expert",
        )(pos, *held, *other, *ws)

    def give_back(act):
        back = lax.all_to_all(act.reshape(16, 2 * MOST, wide), ("y", "c", "xl"), split_axis=0, concat_axis=0, tiled=True)
        return back.reshape(4, 2, 2, 2 * MOST, wide)

    act_a = expert(own_a, left_a, right_a, *far_a)
    left_b, right_b, act_a = barrier((left_b, right_b, act_a))
    back_a = give_back(act_a)
    back_b = give_back(expert(own_b, left_b, right_b, *far(left_b, right_b)))
    out = pl.pallas_call(
        combine_kernel,
        out_shape=jax.ShapeDtypeStruct((steps, n, 1024), BF),
        in_specs=[VM] * 3,
        out_specs=VM,
        compiler_params=pltpu.CompilerParams(vmem_limit_bytes=24 << 20),
        name="combine",
    )(meta, back_a, back_b)
    return out.reshape(steps, n, 2, 2, 256)


def solution(mesh):
    fine = Mesh(mesh.devices.reshape(2, 4, 2, 8, 2), ("dp", "y", "c", "z", "xl"))
    group, tensor = ("dp", "y", "c"), ("z", "xl")
    in_specs = (
        P(None, group, tensor),
        P(None, group, None),
        P(None, group, None),
        P(("y", "c"), tensor, None),
        P(("y", "c"), tensor, None),
    )
    out_specs = P(None, group, None, None, tensor)
    return jax.shard_map(body, mesh=fine, in_specs=in_specs, out_specs=out_specs, check_vma=False)
```

```python
import functools

import jax
import jax.numpy as jnp
from jax import lax
from jax.experimental import pallas as pl
from jax.experimental.pallas import tpu as pltpu
from jax.sharding import Mesh, PartitionSpec as P

MOST = 80
X = ("dp", "xl")
BF, F32 = jnp.bfloat16, jnp.float32
ANY = pl.BlockSpec(memory_space=pl.ANY)
VM = pl.BlockSpec(memory_space=pltpu.VMEM)
SM = pl.BlockSpec(memory_space=pltpu.SMEM)


def ring(x, axis, size, step):
    return lax.ppermute(x, axis, [(i, (i + step) % size) for i in range(size)])


def ranks(member):
    n = member.shape[1]
    before = lax.broadcasted_iota(jnp.int32, (n, n), 0) < lax.broadcasted_iota(jnp.int32, (n, n), 1)
    return jnp.dot(member.astype(BF), before.astype(BF), preferred_element_type=F32)


def slots(rank, member):
    row = lax.broadcasted_iota(jnp.int32, (MOST, rank.shape[1]), 0).astype(F32)
    return (row == rank) & (member > 0)


def dispatch_kernel(pos, meta, *refs):
    y, xl = pos[0], pos[2]
    feats, outs = refs[:8], refs[8:]
    ss, width, n = feats[0].shape
    lane = lax.broadcasted_iota(jnp.int32, (MOST, 128), 1)
    for s in range(ss):
        own = meta[2 * xl + s]
        rows = []
        members = []
        for d in range(4):
            e = lax.rem(y + d, 4).astype(F32)
            members.append(((own[0:1] == e) | (own[1:2] == e)).astype(F32))
        rank = ranks(jnp.concatenate(members, axis=0))
        for d in range(4):
            place = slots(rank[d : d + 1], members[d])
            rows.append(place.astype(BF))
            e = lax.rem(y + d, 4).astype(F32)
            weight = jnp.where(own[0:1] == e, own[2:3], own[3:4])
            whole = jnp.broadcast_to(jnp.sum(jnp.where(place, weight, 0.0), axis=1, keepdims=True), (MOST, 128))
            high = whole.astype(BF)
            rest = whole - high.astype(F32)
            mid = rest.astype(BF)
            low = (rest - mid.astype(F32)).astype(BF)
            terms = jnp.where(lane == 0, high.astype(F32), jnp.where(lane == 1, mid.astype(F32), jnp.where(lane == 2, low.astype(F32), 0.0)))
            outs[d][s * MOST : (s + 1) * MOST, 8 * width :] = terms.astype(BF)
        onehot = jnp.concatenate(rows, axis=0)
        for k in range(8):
            picked = lax.dot_general(onehot, feats[k][s], (((1,), (1,)), ((), ())), preferred_element_type=F32).astype(BF)
            for d in range(4):
                outs[d][s * MOST : (s + 1) * MOST, k * width : (k + 1) * width] = picked[d * MOST : (d + 1) * MOST]


def columns_kernel(pos, gate, up, out_a, out_b, held, sem):
    for flag, src in ((0, gate), (1, up)):

        @pl.when(pos[3] == flag)
        def _(src=src):
            copy = pltpu.make_async_copy(src.at[0], held, sem)
            copy.start()
            copy.wait()

    for r, out in enumerate((out_a, out_b)):
        for z in range(8):
            for t in range(2):
                first = z * 512 + t * 256 + r * 128
                out[z, :, t * 128 : (t + 1) * 128] = held[:, first : first + 128]


def expert_kernel(first, last, *refs):
    pos, refs = refs[0], refs[1:]
    count = last - first
    xs, ws, refs = refs[:count], refs[count : count + 5], refs[count + 5 :]
    if first:
        kept, refs = refs[0], refs[1:]
    out, xbuf, wbuf, xsem, wsem = refs
    y, c, xl, dp, z = (pos[i] for i in range(5))
    width = 16 * ws[0].shape[1]
    copies = []
    for i, (src, off, low) in enumerate(((ws[0], 0, 0), (ws[1], 3, 0), (ws[2], 1, 0), (ws[3], 2, 0), (ws[4], 2, 4))):
        j = lax.rem(dp * 2 + xl + off, 4)
        for k in range(src.shape[0]):
            place = wbuf.at[lax.div(j, 2), lax.rem(low + k + 8 - z, 8), lax.rem(j, 2)]
            copies.append(pltpu.make_async_copy(src.at[k], place, wsem.at[i, k]))
    rows = [pltpu.make_async_copy(xs[g], xbuf.at[g], xsem.at[g]) for g in range(count)]
    for cp in copies:
        cp.start()
    rows[0].start()
    if first:
        for e in range(4):
            out[e, c] = kept[e, c]
    for cp in copies:
        cp.wait()
    rows[1].start()
    for g in range(count):
        d, cc = (first + g) % 4, (first + g) // 4
        if g < count - 2:
            rows[g + 2].start()
        rows[g].wait()
        rw = jnp.sum(xbuf[g, :, width:].astype(F32), axis=1, keepdims=True)
        gate = jnp.dot(xbuf[g, :, :width], wbuf[0].reshape(width, 256), preferred_element_type=F32)
        up = jnp.dot(xbuf[g, :, :width], wbuf[1].reshape(width, 256), preferred_element_type=F32)
        act = (rw * (gate / (1.0 + jnp.exp(-gate)) * up)).astype(BF)
        for t in range(2):
            out[lax.rem(y + 4 - d, 4), c + cc - 2 * c * cc, t] = act[:, t * 128 : (t + 1) * 128]


def combine_kernel(meta, recv_a, recv_b, out):
    steps = meta.shape[0]
    for s in range(steps):
        own = meta[s]
        members = [((own[0:1] == e) | (own[1:2] == e)).astype(F32) for e in range(4)]
        rank = ranks(jnp.concatenate(members, axis=0))
        left, right = [], []
        for e in range(4):
            place = slots(rank[e : e + 1], members[e])
            left.append(jnp.concatenate([(place & (own[k : k + 1] == e)).astype(BF) for k in range(2)], axis=1))
            part = pl.ds((s % 2) * MOST, MOST)
            right.append(jnp.concatenate([r[e, h, s // 2, part] for h in range(2) for r in (recv_a, recv_b)], axis=1))
        picked = lax.dot_general(
            jnp.concatenate(left, axis=0), jnp.concatenate(right, axis=0), (((0,), (0,)), ((), ())), preferred_element_type=F32
        ).astype(BF)
        n = picked.shape[0] // 2
        out[s] = jnp.concatenate([picked[:n], picked[n:]], axis=1)


def body(tokens, expert_ids, route_weights, gate_train, up_train):
    barrier = lax.optimization_barrier
    dp, y, c, z, xl = (lax.axis_index(a) for a in ("dp", "y", "c", "z", "xl"))
    pos = jnp.stack([y, c, xl, dp, z]).astype(jnp.int32)
    steps, n, width = tokens.shape
    meta = jnp.concatenate([expert_ids.astype(F32), route_weights], axis=2).transpose(0, 2, 1)
    turned = tokens.transpose(0, 2, 1).reshape(2, steps // 2, width, n)
    mine = lax.dynamic_index_in_dim(turned, xl, 0, keepdims=False)
    theirs = lax.dynamic_index_in_dim(turned, 1 - xl, 0, keepdims=False)
    got = ring(theirs, "xl", 2, 1)
    pair = jnp.concatenate([jnp.where(xl == 0, mine, got), jnp.where(xl == 0, got, mine)], axis=1)
    rows, units = gate_train.shape[1:]
    wide = units // 32
    blocks = pl.pallas_call(
        columns_kernel,
        out_shape=[jax.ShapeDtypeStruct((8, rows, 2 * wide), BF)] * 2,
        in_specs=[SM, ANY, ANY],
        out_specs=[VM] * 2,
        scratch_shapes=[pltpu.VMEM((rows, units), BF), pltpu.SemaphoreType.DMA(())],
        compiler_params=pltpu.CompilerParams(vmem_limit_bytes=58 << 20),
        name="columns",
    )(pos, gate_train, up_train)

    def exchange(x):
        return lax.all_to_all(x, "z", split_axis=0, concat_axis=0, tiled=True)

    def sides(own):
        return ring(own, X, 4, 1), ring(own, X, 4, -1)

    def far(left, right):
        return ring(left[:4], X, 4, 1), ring(right[4:], X, 4, -1)

    below, above = [pair], [pair]
    for k in range(3):
        if k == 2:
            below[2], above[2], *blocks = barrier((below[2], above[2], *blocks))
        below.append(ring(below[-1], "z", 8, 1))
        above.append(ring(above[-1], "z", 8, -1))
    part_a, *last = barrier((blocks[0], ring(below[3][:1], "z", 8, 1), ring(above[3][1:], "z", 8, -1)))
    own_a = exchange(part_a)
    feats = [pair] + above[1:] + [jnp.concatenate(last, axis=0)] + below[:0:-1]
    sent = pl.pallas_call(
        dispatch_kernel,
        out_shape=[jax.ShapeDtypeStruct((2 * MOST, 16 * width + 128), BF)] * 4,
        in_specs=[SM] + [VM] * 9,
        out_specs=[VM] * 4,
        compiler_params=pltpu.CompilerParams(vmem_limit_bytes=24 << 20),
        name="dispatch",
    )(pos, meta, *feats)
    near = ring(sent[1], "y", 4, 1), ring(sent[3], "y", 4, 3)
    other = [ring(sent[0], "c", 2, 1)]
    part_b, own_a = barrier((blocks[1], own_a))
    own_b = exchange(part_b)
    left_a, right_a = sides(own_a)
    far_rows, other[0], *near = barrier((sent[2], other[0], *near))
    opposite = ring(far_rows, "y", 4, 2)
    left_a, right_a, *near = barrier((left_a, right_a, *near))
    far_a = far(left_a, right_a)
    own_b, opposite, *rest = barrier((own_b, opposite, *near, *far_a))
    near, ws_a = rest[:2], [own_a, left_a, right_a, *rest[2:]]
    left_b, right_b = sides(own_b)
    held = [sent[0], near[0], opposite, near[1]]

    def expert(first, last, xs, ws, kept=()):
        return pl.pallas_call(
            functools.partial(expert_kernel, first, last),
            out_shape=jax.ShapeDtypeStruct((4, 2, 2, 2 * MOST, wide), BF),
            in_specs=[SM] + [ANY] * (len(xs) + 5) + [VM] * len(kept),
            out_specs=VM,
            scratch_shapes=[
                pltpu.VMEM((len(xs), 2 * MOST, 16 * width + 128), BF),
                pltpu.VMEM((2, 8, 2, rows, 2 * wide), BF),
                pltpu.SemaphoreType.DMA((8,)),
                pltpu.SemaphoreType.DMA((5, 8)),
            ],
            compiler_params=pltpu.CompilerParams(vmem_limit_bytes=58 << 20),
            cost_estimate=pl.CostEstimate(
                flops=2 * len(xs) * MOST * 16 * width * 8 * wide, bytes_accessed=12 << 20, transcendentals=4 * len(xs) * MOST * wide
            ),
            name="expert",
        )(pos, *xs, *ws, *kept)

    act_a = expert(0, 4, held, ws_a)
    act_a, left_b, right_b, *rest = barrier((act_a, left_b, right_b, *held[1:]))
    other += [ring(h, "c", 2, 1) for h in rest]
    act_a = expert(4, 8, other, ws_a, (act_a,))
    def give_back(act):
        back = lax.all_to_all(act.reshape(16, 2 * MOST, wide), ("y", "c", "xl"), split_axis=0, concat_axis=0, tiled=True)
        return back.reshape(4, 2, 2, 2 * MOST, wide)

    back_a = give_back(act_a)
    back_b = give_back(expert(0, 8, held + other, [own_b, left_b, right_b, *far(left_b, right_b)]))
    out = pl.pallas_call(
        combine_kernel,
        out_shape=jax.ShapeDtypeStruct((steps, n, 1024), BF),
        in_specs=[VM] * 3,
        out_specs=VM,
        compiler_params=pltpu.CompilerParams(vmem_limit_bytes=24 << 20),
        name="combine",
    )(meta, back_a, back_b)
    return out.reshape(steps, n, 2, 2, 256)


def solution(mesh):
    fine = Mesh(mesh.devices.reshape(2, 4, 2, 8, 2), ("dp", "y", "c", "z", "xl"))
    group, tensor = ("dp", "y", "c"), ("z", "xl")
    in_specs = (
        P(None, group, tensor),
        P(None, group, None),
        P(None, group, None),
        P(("y", "c"), tensor, None),
        P(("y", "c"), tensor, None),
    )
    out_specs = P(None, group, None, None, tensor)
    return jax.shard_map(body, mesh=fine, in_specs=in_specs, out_specs=out_specs, check_vma=False)
```

```python
import jax
import jax.numpy as jnp
from jax import lax
from jax.experimental import pallas as pl
from jax.experimental.pallas import tpu as pltpu
from jax.sharding import Mesh, PartitionSpec as P

MOST = 80
X = ("dp", "xl")
BF, F32 = jnp.bfloat16, jnp.float32
ANY = pl.BlockSpec(memory_space=pl.ANY)
VM = pl.BlockSpec(memory_space=pltpu.VMEM)
SM = pl.BlockSpec(memory_space=pltpu.SMEM)


def in_hbm(x):
    return pltpu.with_memory_space_constraint(x, pltpu.HBM)


def ring(x, axis, size, step):
    return lax.ppermute(x, axis, [(i, (i + step) % size) for i in range(size)])


def ranks(member):
    n = member.shape[1]
    before = lax.broadcasted_iota(jnp.int32, (n, n), 0) < lax.broadcasted_iota(jnp.int32, (n, n), 1)
    return jnp.dot(member.astype(BF), before.astype(BF), preferred_element_type=F32)


def slots(rank, member):
    row = lax.broadcasted_iota(jnp.int32, (MOST, rank.shape[1]), 0).astype(F32)
    return (row == rank) & (member > 0)


def dispatch_kernel(pos, meta, *refs):
    y, xl = pos[0], pos[2]
    feats, outs = refs[:8], refs[8:]
    ss, width, n = feats[0].shape
    lane = lax.broadcasted_iota(jnp.int32, (MOST, 128), 1)
    for s in range(ss):
        own = meta[2 * xl + s]
        rows = []
        members = []
        for d in range(4):
            e = lax.rem(y + d, 4).astype(F32)
            members.append(((own[0:1] == e) | (own[1:2] == e)).astype(F32))
        rank = ranks(jnp.concatenate(members, axis=0))
        for d in range(4):
            place = slots(rank[d : d + 1], members[d])
            rows.append(place.astype(BF))
            e = lax.rem(y + d, 4).astype(F32)
            weight = jnp.where(own[0:1] == e, own[2:3], own[3:4])
            whole = jnp.broadcast_to(jnp.sum(jnp.where(place, weight, 0.0), axis=1, keepdims=True), (MOST, 128))
            high = whole.astype(BF)
            rest = whole - high.astype(F32)
            mid = rest.astype(BF)
            low = (rest - mid.astype(F32)).astype(BF)
            terms = jnp.where(lane == 0, high.astype(F32), jnp.where(lane == 1, mid.astype(F32), jnp.where(lane == 2, low.astype(F32), 0.0)))
            outs[d][s * MOST : (s + 1) * MOST, 8 * width :] = terms.astype(BF)
        onehot = jnp.concatenate(rows, axis=0)
        for k in range(8):
            picked = lax.dot_general(onehot, feats[k][s], (((1,), (1,)), ((), ())), preferred_element_type=F32).astype(BF)
            for d in range(4):
                outs[d][s * MOST : (s + 1) * MOST, k * width : (k + 1) * width] = picked[d * MOST : (d + 1) * MOST]


def columns_kernel(pos, gate, up, out_a, out_b, held, sem):
    for flag, src in ((0, gate), (1, up)):

        @pl.when(pos[3] == flag)
        def _(src=src):
            copy = pltpu.make_async_copy(src.at[0], held, sem)
            copy.start()
            copy.wait()

    for r, out in enumerate((out_a, out_b)):
        for z in range(8):
            for t in range(2):
                first = z * 512 + t * 256 + r * 128
                out[z, :, t * 128 : (t + 1) * 128] = held[:, first : first + 128]


def expert_kernel(pos, *refs):
    xs, ws, (out, xbuf, wbuf, xsem) = refs[:8], refs[8:13], refs[13:]
    y, c, xl, dp, z = (pos[i] for i in range(5))
    width = 16 * ws[0].shape[1]
    rows = [pltpu.make_async_copy(xs[g], xbuf.at[g], xsem.at[g]) for g in range(8)]
    for cp in rows:
        cp.start()
    for src, off, low in ((ws[0], 0, 0), (ws[1], 3, 0), (ws[2], 1, 0), (ws[3], 2, 0), (ws[4], 2, 4)):
        j = lax.rem(dp * 2 + xl + off, 4)
        for k in range(src.shape[0]):
            wbuf[lax.div(j, 2), lax.rem(low + k + 8 - z, 8), lax.rem(j, 2)] = src[k]
    for g in range(8):
        d, cc = g % 4, g // 4
        rows[g].wait()
        rw = jnp.sum(xbuf[g, :, width:].astype(F32), axis=1, keepdims=True)
        gate = jnp.dot(xbuf[g, :, :width], wbuf[0].reshape(width, 256), preferred_element_type=F32)
        up = jnp.dot(xbuf[g, :, :width], wbuf[1].reshape(width, 256), preferred_element_type=F32)
        act = (rw * (gate / (1.0 + jnp.exp(-gate)) * up)).astype(BF)
        for t in range(2):
            out[lax.rem(y + 4 - d, 4), c + cc - 2 * c * cc, t] = act[:, t * 128 : (t + 1) * 128]


def combine_kernel(meta, recv_a, recv_b, out):
    steps = meta.shape[0]
    for s in range(steps):
        own = meta[s]
        members = [((own[0:1] == e) | (own[1:2] == e)).astype(F32) for e in range(4)]
        rank = ranks(jnp.concatenate(members, axis=0))
        left, right = [], []
        for e in range(4):
            place = slots(rank[e : e + 1], members[e])
            left.append(jnp.concatenate([(place & (own[k : k + 1] == e)).astype(BF) for k in range(2)], axis=1))
            part = pl.ds((s % 2) * MOST, MOST)
            right.append(jnp.concatenate([r[e, h, s // 2, part] for h in range(2) for r in (recv_a, recv_b)], axis=1))
        picked = lax.dot_general(
            jnp.concatenate(left, axis=0), jnp.concatenate(right, axis=0), (((0,), (0,)), ((), ())), preferred_element_type=F32
        ).astype(BF)
        n = picked.shape[0] // 2
        out[s] = jnp.concatenate([picked[:n], picked[n:]], axis=1)


def body(tokens, expert_ids, route_weights, gate_train, up_train):
    barrier = lax.optimization_barrier
    dp, y, c, z, xl = (lax.axis_index(a) for a in ("dp", "y", "c", "z", "xl"))
    pos = jnp.stack([y, c, xl, dp, z]).astype(jnp.int32)
    steps, n, width = tokens.shape
    meta = jnp.concatenate([expert_ids.astype(F32), route_weights], axis=2).transpose(0, 2, 1)
    turned = tokens.transpose(0, 2, 1).reshape(2, steps // 2, width, n)
    mine = lax.dynamic_index_in_dim(turned, xl, 0, keepdims=False)
    theirs = lax.dynamic_index_in_dim(turned, 1 - xl, 0, keepdims=False)
    got = ring(theirs, "xl", 2, 1)
    pair = jnp.concatenate([jnp.where(xl == 0, mine, got), jnp.where(xl == 0, got, mine)], axis=1)
    rows, units = gate_train.shape[1:]
    wide = units // 32
    blocks = pl.pallas_call(
        columns_kernel,
        out_shape=[pltpu.VMEM((8, rows, 2 * wide), BF)] * 2,
        in_specs=[SM, ANY, ANY],
        out_specs=[VM] * 2,
        scratch_shapes=[pltpu.VMEM((rows, units), BF), pltpu.SemaphoreType.DMA(())],
        compiler_params=pltpu.CompilerParams(vmem_limit_bytes=8 << 20),
        name="columns",
    )(pos, in_hbm(gate_train), in_hbm(up_train))

    def exchange(x):
        return lax.all_to_all(x, "z", split_axis=0, concat_axis=0, tiled=True)

    def sides(own):
        return ring(own, X, 4, 1), ring(own, X, 4, -1)

    def far(left, right):
        return ring(left[:4], X, 4, 1), ring(right[4:], X, 4, -1)

    below, above = [pair], [pair]
    for k in range(3):
        if k == 2:
            below[2], above[2], *blocks = barrier((below[2], above[2], *blocks))
        below.append(ring(below[-1], "z", 8, 1))
        above.append(ring(above[-1], "z", 8, -1))
    part_a, *last = barrier((blocks[0], ring(below[3][:1], "z", 8, 1), ring(above[3][1:], "z", 8, -1)))
    own_a = exchange(part_a)
    feats = [pair] + above[1:] + [jnp.concatenate(last, axis=0)] + below[:0:-1]
    sent = pl.pallas_call(
        dispatch_kernel,
        out_shape=[pltpu.VMEM((2 * MOST, 16 * width + 128), BF)] * 4,
        in_specs=[SM] + [VM] * 9,
        out_specs=[VM] * 4,
        compiler_params=pltpu.CompilerParams(vmem_limit_bytes=10 << 20),
        name="dispatch",
    )(pos, meta, *feats)
    near = ring(sent[1], "y", 4, 1), ring(sent[3], "y", 4, 3)
    other = [ring(sent[0], "c", 2, 1)]
    part_b, own_a = barrier((blocks[1], own_a))
    own_b = exchange(part_b)
    left_a, right_a = sides(own_a)
    far_rows, other[0], *near = barrier((sent[2], other[0], *near))
    opposite = ring(far_rows, "y", 4, 2)
    left_a, right_a, *near = barrier((left_a, right_a, *near))
    far_a = far(left_a, right_a)
    other += [ring(h, "c", 2, 1) for h in near]
    own_b, opposite, *rest = barrier((own_b, opposite, *far_a, *other))
    far_a, other = rest[:2], rest[2:]
    left_b, right_b = sides(own_b)
    held = [sent[0], near[0], opposite, near[1]]
    other = [other[0], other[1], ring(opposite, "c", 2, 1), other[2]]

    def expert(*ws):
        return pl.pallas_call(
            expert_kernel,
            out_shape=pltpu.VMEM((4, 2, 2, 2 * MOST, wide), BF),
            in_specs=[SM] + [ANY] * 8 + [VM] * 5,
            out_specs=VM,
            scratch_shapes=[
                pltpu.VMEM((8, 2 * MOST, 16 * width + 128), BF),
                pltpu.VMEM((2, 8, 2, rows, 2 * wide), BF),
                pltpu.SemaphoreType.DMA((8,)),
            ],
            compiler_params=pltpu.CompilerParams(vmem_limit_bytes=18 << 20),
            cost_estimate=pl.CostEstimate(
                flops=16 * MOST * 16 * width * 8 * wide, bytes_accessed=12 << 20, transcendentals=16 * MOST * 2 * wide
            ),
            name="expert",
        )(pos, *map(in_hbm, (*held, *other)), *ws)

    def give_back(act):
        back = lax.all_to_all(act.reshape(16, 2 * MOST, wide), ("y", "c", "xl"), split_axis=0, concat_axis=0, tiled=True)
        return back.reshape(4, 2, 2, 2 * MOST, wide)

    act_a = expert(own_a, left_a, right_a, *far_a)
    left_b, right_b, act_a = barrier((left_b, right_b, act_a))
    back_a = give_back(act_a)
    back_b = give_back(expert(own_b, left_b, right_b, *far(left_b, right_b)))
    out = pl.pallas_call(
        combine_kernel,
        out_shape=jax.ShapeDtypeStruct((steps, n, 1024), BF),
        in_specs=[VM] * 3,
        out_specs=VM,
        compiler_params=pltpu.CompilerParams(vmem_limit_bytes=10 << 20),
        name="combine",
    )(meta, back_a, back_b)
    return out.reshape(steps, n, 2, 2, 256)


def solution(mesh):
    fine = Mesh(mesh.devices.reshape(2, 4, 2, 8, 2), ("dp", "y", "c", "z", "xl"))
    group, tensor = ("dp", "y", "c"), ("z", "xl")
    in_specs = (
        P(None, group, tensor),
        P(None, group, None),
        P(None, group, None),
        P(("y", "c"), tensor, None),
        P(("y", "c"), tensor, None),
    )
    out_specs = P(None, group, None, None, tensor)
    return jax.shard_map(body, mesh=fine, in_specs=in_specs, out_specs=out_specs, check_vma=False)
```

```python
import jax
import jax.numpy as jnp
from jax import lax
from jax.experimental import pallas as pl
from jax.experimental.pallas import tpu as pltpu
from jax.sharding import Mesh, PartitionSpec as P

MOST = 80
X = ("dp", "xl")
BF, F32 = jnp.bfloat16, jnp.float32
ANY = pl.BlockSpec(memory_space=pl.ANY)
VM = pl.BlockSpec(memory_space=pltpu.VMEM)
SM = pl.BlockSpec(memory_space=pltpu.SMEM)


def ring(x, axis, size, step):
    return lax.ppermute(x, axis, [(i, (i + step) % size) for i in range(size)])


def ranks(member):
    n = member.shape[1]
    before = lax.broadcasted_iota(jnp.int32, (n, n), 0) < lax.broadcasted_iota(jnp.int32, (n, n), 1)
    return jnp.dot(member.astype(BF), before.astype(BF), preferred_element_type=F32)


def slots(rank, member):
    row = lax.broadcasted_iota(jnp.int32, (MOST, rank.shape[1]), 0).astype(F32)
    return (row == rank) & (member > 0)


def dispatch_kernel(pos, meta, *refs):
    y, xl = pos[0], pos[2]
    feats, outs = refs[:8], refs[8:]
    ss, width, n = feats[0].shape
    lane = lax.broadcasted_iota(jnp.int32, (MOST, 128), 1)
    for s in range(ss):
        own = meta[2 * xl + s]
        rows = []
        members = []
        for d in range(4):
            e = lax.rem(y + d, 4).astype(F32)
            members.append(((own[0:1] == e) | (own[1:2] == e)).astype(F32))
        rank = ranks(jnp.concatenate(members, axis=0))
        for d in range(4):
            place = slots(rank[d : d + 1], members[d])
            rows.append(place.astype(BF))
            e = lax.rem(y + d, 4).astype(F32)
            weight = jnp.where(own[0:1] == e, own[2:3], own[3:4])
            whole = jnp.broadcast_to(jnp.sum(jnp.where(place, weight, 0.0), axis=1, keepdims=True), (MOST, 128))
            high = whole.astype(BF)
            rest = whole - high.astype(F32)
            mid = rest.astype(BF)
            low = (rest - mid.astype(F32)).astype(BF)
            terms = jnp.where(lane == 0, high.astype(F32), jnp.where(lane == 1, mid.astype(F32), jnp.where(lane == 2, low.astype(F32), 0.0)))
            outs[d][s * MOST : (s + 1) * MOST, 8 * width :] = terms.astype(BF)
        onehot = jnp.concatenate(rows, axis=0)
        for k in range(8):
            picked = lax.dot_general(onehot, feats[k][s], (((1,), (1,)), ((), ())), preferred_element_type=F32).astype(BF)
            for d in range(4):
                outs[d][s * MOST : (s + 1) * MOST, k * width : (k + 1) * width] = picked[d * MOST : (d + 1) * MOST]


def columns_kernel(pos, gate, up, out_a, out_b, held, sem):
    for flag, src in ((0, gate), (1, up)):

        @pl.when(pos[3] == flag)
        def _(src=src):
            copy = pltpu.make_async_copy(src.at[0], held, sem)
            copy.start()
            copy.wait()

    for r, out in enumerate((out_a, out_b)):
        for z in range(8):
            for t in range(2):
                first = z * 512 + t * 256 + r * 128
                out[z, :, t * 128 : (t + 1) * 128] = held[:, first : first + 128]


def expert_kernel(pos, *refs):
    xs, ws, (out, xbuf, wbuf, xsem, wsem) = refs[:8], refs[8:13], refs[13:]
    y, c, xl, dp, z = (pos[i] for i in range(5))
    width = 16 * ws[0].shape[1]
    copies = []
    for i, (src, off, low) in enumerate(((ws[0], 0, 0), (ws[1], 3, 0), (ws[2], 1, 0), (ws[3], 2, 0), (ws[4], 2, 4))):
        j = lax.rem(dp * 2 + xl + off, 4)
        for k in range(src.shape[0]):
            place = wbuf.at[lax.div(j, 2), lax.rem(low + k + 8 - z, 8), lax.rem(j, 2)]
            copies.append(pltpu.make_async_copy(src.at[k], place, wsem.at[i, k]))
    rows = [pltpu.make_async_copy(xs[g], xbuf.at[g], xsem.at[g]) for g in range(8)]
    for cp in copies:
        cp.start()
    rows[0].start()
    for cp in copies:
        cp.wait()
    rows[1].start()
    for g in range(8):
        d, cc = g % 4, g // 4
        if g < 6:
            rows[g + 2].start()
        rows[g].wait()
        rw = jnp.sum(xbuf[g, :, width:].astype(F32), axis=1, keepdims=True)
        gate = jnp.dot(xbuf[g, :, :width], wbuf[0].reshape(width, 256), preferred_element_type=F32)
        up = jnp.dot(xbuf[g, :, :width], wbuf[1].reshape(width, 256), preferred_element_type=F32)
        act = (rw * (gate / (1.0 + jnp.exp(-gate)) * up)).astype(BF)
        for t in range(2):
            out[lax.rem(y + 4 - d, 4), c + cc - 2 * c * cc, t] = act[:, t * 128 : (t + 1) * 128]


def combine_kernel(meta, recv_a, recv_b, out):
    steps = meta.shape[0]
    for s in range(steps):
        own = meta[s]
        members = [((own[0:1] == e) | (own[1:2] == e)).astype(F32) for e in range(4)]
        rank = ranks(jnp.concatenate(members, axis=0))
        left, right = [], []
        for e in range(4):
            place = slots(rank[e : e + 1], members[e])
            left.append(jnp.concatenate([(place & (own[k : k + 1] == e)).astype(BF) for k in range(2)], axis=1))
            part = pl.ds((s % 2) * MOST, MOST)
            right.append(jnp.concatenate([r[e, h, s // 2, part] for h in range(2) for r in (recv_a, recv_b)], axis=1))
        picked = lax.dot_general(
            jnp.concatenate(left, axis=0), jnp.concatenate(right, axis=0), (((0,), (0,)), ((), ())), preferred_element_type=F32
        ).astype(BF)
        n = picked.shape[0] // 2
        out[s] = jnp.concatenate([picked[:n], picked[n:]], axis=1)


def body(tokens, expert_ids, route_weights, gate_train, up_train):
    barrier = lax.optimization_barrier
    dp, y, c, z, xl = (lax.axis_index(a) for a in ("dp", "y", "c", "z", "xl"))
    pos = jnp.stack([y, c, xl, dp, z]).astype(jnp.int32)
    steps, n, width = tokens.shape
    meta = jnp.concatenate([expert_ids.astype(F32), route_weights], axis=2).transpose(0, 2, 1)
    turned = tokens.transpose(0, 2, 1).reshape(2, steps // 2, width, n)
    mine = lax.dynamic_index_in_dim(turned, xl, 0, keepdims=False)
    theirs = lax.dynamic_index_in_dim(turned, 1 - xl, 0, keepdims=False)
    got = ring(theirs, "xl", 2, 1)
    pair = jnp.concatenate([jnp.where(xl == 0, mine, got), jnp.where(xl == 0, got, mine)], axis=1)
    rows, units = gate_train.shape[1:]
    wide = units // 32
    blocks = pl.pallas_call(
        columns_kernel,
        out_shape=[jax.ShapeDtypeStruct((8, rows, 2 * wide), BF)] * 2,
        in_specs=[SM, ANY, ANY],
        out_specs=[VM] * 2,
        scratch_shapes=[pltpu.VMEM((rows, units), BF), pltpu.SemaphoreType.DMA(())],
        compiler_params=pltpu.CompilerParams(vmem_limit_bytes=58 << 20),
        name="columns",
    )(pos, gate_train, up_train)

    def exchange(x):
        return lax.all_to_all(x, "z", split_axis=0, concat_axis=0, tiled=True)

    def sides(own):
        return ring(own, X, 4, 1), ring(own, X, 4, -1)

    def far(left, right):
        return ring(left[:4], X, 4, 1), ring(right[4:], X, 4, -1)

    below, above = [pair], [pair]
    for k in range(3):
        if k == 2:
            below[2], above[2], *blocks = barrier((below[2], above[2], *blocks))
        below.append(ring(below[-1], "z", 8, 1))
        above.append(ring(above[-1], "z", 8, -1))
    part_a, *last = barrier((blocks[0], ring(below[3][:1], "z", 8, 1), ring(above[3][1:], "z", 8, -1)))
    own_a = exchange(part_a)
    feats = [pair] + above[1:] + [jnp.concatenate(last, axis=0)] + below[:0:-1]
    sent = pl.pallas_call(
        dispatch_kernel,
        out_shape=[jax.ShapeDtypeStruct((2 * MOST, 16 * width + 128), BF)] * 4,
        in_specs=[SM] + [VM] * 9,
        out_specs=[VM] * 4,
        compiler_params=pltpu.CompilerParams(vmem_limit_bytes=24 << 20),
        name="dispatch",
    )(pos, meta, *feats)
    near = ring(sent[1], "y", 4, 1), ring(sent[3], "y", 4, 3)
    other = [ring(sent[0], "c", 2, 1)]
    part_b, own_a = barrier((blocks[1], own_a))
    own_b = exchange(part_b)
    left_a, right_a = sides(own_a)
    far_rows, other[0], *near = barrier((sent[2], other[0], *near))
    opposite = ring(far_rows, "y", 4, 2)
    far_a = far(left_a, right_a)
    other += [ring(h, "c", 2, 1) for h in near]
    own_b, opposite, *rest = barrier((own_b, opposite, *far_a, *other))
    far_a, other = rest[:2], rest[2:]
    left_b, right_b = sides(own_b)
    held = [sent[0], near[0], opposite, near[1]]
    other = [other[0], other[1], ring(opposite, "c", 2, 1), other[2]]

    def expert(*ws):
        return pl.pallas_call(
            expert_kernel,
            out_shape=jax.ShapeDtypeStruct((4, 2, 2, 2 * MOST, wide), BF),
            in_specs=[SM] + [ANY] * 13,
            out_specs=VM,
            scratch_shapes=[
                pltpu.VMEM((8, 2 * MOST, 16 * width + 128), BF),
                pltpu.VMEM((2, 8, 2, rows, 2 * wide), BF),
                pltpu.SemaphoreType.DMA((8,)),
                pltpu.SemaphoreType.DMA((5, 8)),
            ],
            compiler_params=pltpu.CompilerParams(vmem_limit_bytes=58 << 20),
            cost_estimate=pl.CostEstimate(
                flops=16 * MOST * 16 * width * 8 * wide, bytes_accessed=12 << 20, transcendentals=16 * MOST * 2 * wide
            ),
            name="expert",
        )(pos, *held, *other, *ws)

    def give_back(act):
        back = lax.all_to_all(act.reshape(16, 2 * MOST, wide), ("y", "c", "xl"), split_axis=0, concat_axis=0, tiled=True)
        return back.reshape(4, 2, 2, 2 * MOST, wide)

    act_a = expert(own_a, left_a, right_a, *far_a)
    left_b, right_b, act_a = barrier((left_b, right_b, act_a))
    back_a = give_back(act_a)
    back_b = give_back(expert(own_b, left_b, right_b, *far(left_b, right_b)))
    out = pl.pallas_call(
        combine_kernel,
        out_shape=jax.ShapeDtypeStruct((steps, n, 1024), BF),
        in_specs=[VM] * 3,
        out_specs=VM,
        compiler_params=pltpu.CompilerParams(vmem_limit_bytes=24 << 20),
        name="combine",
    )(meta, back_a, back_b)
    return out.reshape(steps, n, 2, 2, 256)


def solution(mesh):
    fine = Mesh(mesh.devices.reshape(2, 4, 2, 8, 2), ("dp", "y", "c", "z", "xl"))
    group, tensor = ("dp", "y", "c"), ("z", "xl")
    in_specs = (
        P(None, group, tensor),
        P(None, group, None),
        P(None, group, None),
        P(("y", "c"), tensor, None),
        P(("y", "c"), tensor, None),
    )
    out_specs = P(None, group, None, None, tensor)
    return jax.shard_map(body, mesh=fine, in_specs=in_specs, out_specs=out_specs, check_vma=False)
```
